128 devices in a mesh: enc: 4 (over x), seq: 16 (over z, y), tp: 2 (over core).
Axes of the slice: x: 4, y: 4, z: 4, core: 2. Of those that a mesh axis runs over, the one named last changes fastest.
Arguments:
- audio_rows: bfloat16 [8192, 1280], P(('enc', 'seq')), may hold values from -6 to 6
- vision_rows: bfloat16 [4096, 5120], P(('enc', 'seq')), may hold values from -6 to 6
- audio_weight: bfloat16 [1280, 3584], P('seq', 'tp'), may hold values from -0.15625 to 0.15625
- vision_weight: bfloat16 [1280, 4, 3584], P('seq', None, 'tp'), may hold values from -0.078125 to 0.078125
- text_rows: bfloat16 [16384, 3584], P(('enc', 'seq'), 'tp'), may hold values from -6 to 6
- row_target: int32 [64, 192], replicated, may hold values from 0 to 16383, as said below
- segment_ids: int32 [64, 256], P(('enc', 'seq')), may hold values from 0 to 3, never falling along the last dimension, each value on 1 to 128 neighbouring positions
- norm_gain: float32 [3584], replicated, may hold values from 0.1 to 1.9
- qkv_weight: bfloat16 [3584, 2304], P(None, 'tp'), may hold values from -1 to 1
- attn_grad: bfloat16 [16384, 1792], P(('enc', 'seq'), 'tp'), may hold values from -6 to 6
Outputs:
- audio_grad: bfloat16 [8192, 3584], P(('enc', 'seq'), 'tp')
- vision_grad: bfloat16 [4096, 3584], P(('enc', 'seq'), 'tp')
The draws below stay inside these ranges and needn't reach their ends.
Inputs may be any that keep to these rules, and one draw needn't show every extreme that they name: `row_target`: no two entries are equal. Every sample (positions s * 256 to (s + 1) * 256 - 1) receives exactly 192 encoder rows. The rows of one sending device name the positions of one sample between 2 and 4 times; every sending device sends exactly 4 rows to some sample, and every sample receives exactly 4 rows from some sending device.
All inputs are finite; a program needn't handle non-finite values.
Results may differ from the reference program's by a relative error of at most 0.018.
Values may be sent and summed in bfloat16 or wider, within the bound.
No kernel may reach another device: no remote copies, remote signals or barrier semaphores. Data moves between devices by JAX's collectives and lax.ppermute only.
A program may use at most 128 MiB of HBM per device.

```python
import math
import jax
import jax.numpy as jnp
import numpy as np
from jax import lax

D = 3584
HEADS = 14
KV_HEADS = 2
HEAD_DIM = 128
AUDIO_WIDTH = 1280
MERGE = 4
TOK_DEV = 256
SEGS = 4
GROUP_WIDTH = 1152
VISION_WIDTH = 5120
AUDIO_DEV = 128
VISION_DEV = 64
ENC_ROWS = 192
SAMPLES = 64
TOKENS = 16384
AUDIO_ROWS = 8192
VISION_ROWS = 4096
N_ENC = 4
N_SEQ = 16


def draw_text_rows(key, part):
    key = jax.random.fold_in(key, 23)
    noise_key = jax.random.fold_in(key, 0)
    noise_rows = jnp.clip(jax.random.normal(noise_key, (TOKENS, D), jnp.float32), -6.0, 6.0)
    text_draw = noise_rows
    return jnp.clip(text_draw, -6.0, 6.0).astype(jnp.bfloat16)


def draw_qkv_weight(key, part):
    key = jax.random.fold_in(key, 37)
    random_key = jax.random.fold_in(key, 0)
    group_heads = HEADS // KV_HEADS
    random_part = jax.random.normal(random_key, (D, KV_HEADS, group_heads + 2, HEAD_DIM), jnp.float32)
    random_part = jnp.clip(random_part, -5.0, 5.0) * D ** (-0.5)
    return random_part.reshape(D, KV_HEADS * GROUP_WIDTH).astype(jnp.bfloat16)


def draw_row_target(key, part):
    key = jax.random.fold_in(key, 11)
    key_spread, key_perm, key_rows, key_slots = jax.random.split(key, 4)
    senders = N_ENC * N_SEQ
    mean_rows = ENC_ROWS // senders
    spread = mean_rows // 2
    halves = jax.random.randint(key_spread, (senders // 2,), -spread, spread + 1)
    halves = halves.at[0].set(spread)
    offsets = jnp.stack([halves, -halves], axis=1).reshape(senders)
    shuffle = jax.random.permutation(key_perm, senders)
    diagonal = (shuffle[None, :] - jnp.arange(senders)[:, None]) % senders
    counts = mean_rows + offsets[diagonal]

    def sender_rows(row_key, row_counts):
        listed = jnp.repeat(jnp.arange(senders), row_counts, total_repeat_length=ENC_ROWS)
        return jax.random.permutation(row_key, listed)
    dest = jax.vmap(sender_rows)(jax.random.split(key_rows, senders), counts)
    flat_dest = dest.reshape(senders * ENC_ROWS)
    one_hot = (flat_dest[:, None] == jnp.arange(senders)[None, :]).astype(jnp.int32)
    rank = jnp.sum((jnp.cumsum(one_hot, axis=0) - 1) * one_hot, axis=1)

    def sample_slots(slot_key):
        return jax.random.permutation(slot_key, TOK_DEV)[:ENC_ROWS]
    slots = jax.vmap(sample_slots)(jax.random.split(key_slots, senders))
    position = slots[flat_dest, rank]
    return (flat_dest * TOK_DEV + position).reshape(senders, ENC_ROWS).astype(jnp.int32)


def level_of(rng, extent, shards, smallest, high):
    def one(dim, shards_of):
        heights = jax.random.uniform(jax.random.fold_in(jax.random.fold_in(rng, 6), dim), (shards_of,), jnp.float32, smallest / len(shards), high / len(shards))
        return jnp.repeat(jnp.exp(heights), extent[dim] // shards_of).reshape((-1,) + (1,) * (len(extent) - dim - 1))

    gain = one(*shards[0])
    for cut in shards[1:]:
        gain = gain * one(*cut)
    return gain


def profile(count, total, limit, lean):
    weights = [(1 << 20) // math.isqrt(standing ** lean) + 1 for standing in range(2, count + 1)]
    surplus, given = total - limit - (count - 1), [1] * (count - 1)
    while surplus > 0:
        candidates = [i for i in range(count - 1) if given[i] < limit]
        whole, budget = sum([weights[i] for i in candidates]), surplus
        for i in candidates:
            addition = min(limit - given[i], max(1, budget * weights[i] // whole), surplus)
            given[i] = given[i] + addition
            surplus = surplus - addition
    return np.array([limit] + given)


def ragged_sizes(own_key, amount, total, most, skew):
    if amount == 2:
        one = jax.random.randint(own_key, (), max(1, total - most), min(most, total - 1) + 1)
        return jnp.stack([one, total - one])
    tallies = jnp.asarray(profile(amount, total, most, skew), jnp.int32)
    pairs = (amount - 1) // 2
    source_of, sink = tallies[1:1 + 2 * pairs:2], tallies[2:2 + 2 * pairs:2]
    margin = jnp.minimum(source_of - 1, most - sink)
    moved = jax.random.randint(jax.random.fold_in(own_key, 1), (pairs,), 0, 1 << 20) % (margin + 1)
    tallies = tallies.at[1:1 + 2 * pairs:2].set(source_of - moved).at[2:2 + 2 * pairs:2].set(sink + moved)
    return tallies[jax.random.permutation(jax.random.fold_in(own_key, 2), amount)]


def bell_draw(rng, dims, width, reach, cuts=(), held_as=jnp.bfloat16):
    gain = level_of(rng, dims, cuts, -0.22, 0.18) if cuts else 1.0
    result = jax.random.normal(rng, dims, jnp.float32) * width * gain
    return jnp.minimum(jnp.maximum(result, -reach), reach).astype(held_as)


def setup_inputs(seed: int = 0) -> dict:
    keys = jax.random.split(jax.random.key(seed), 11)
    return {
        "audio_rows": bell_draw(keys[0], (AUDIO_ROWS, AUDIO_WIDTH), 1.0, 6.0, ((0, 64),)),
        "vision_rows": bell_draw(keys[1], (VISION_ROWS, VISION_WIDTH), 1.0, 6.0, ((0, 64),)),
        "audio_weight": bell_draw(keys[2], (AUDIO_WIDTH, D), AUDIO_WIDTH ** -0.5, 0.15625, ((0, 16), (1, 2))),
        "vision_weight": bell_draw(keys[3], (AUDIO_WIDTH, MERGE, D), VISION_WIDTH ** -0.5, 0.078125, ((0, 16), (2, 2))),
        "text_rows": draw_text_rows(jax.random.fold_in(keys[10], 71), 0),
        "row_target": draw_row_target(jax.random.fold_in(keys[10], 71), 0),
        "segment_ids": jax.vmap(lambda own: jnp.searchsorted(jnp.cumsum(ragged_sizes(own, SEGS, TOK_DEV, TOK_DEV // 2, 2)), jnp.arange(TOK_DEV), side="right"))(jax.random.split(keys[6], SAMPLES)).reshape((SAMPLES, TOK_DEV)).astype(jnp.int32),
        "norm_gain": jnp.clip(1.0 + 0.18 * jax.random.normal(keys[7], (D,), jnp.float32), 0.1, 1.9),
        "qkv_weight": draw_qkv_weight(jax.random.fold_in(keys[10], 71), 0),
        "attn_grad": bell_draw(keys[9], (TOKENS, HEADS * HEAD_DIM), 1.0, 6.0, ((0, 64), (1, 2))),
    }


epsilon = 1e-06

def group_grads(query_rows, key_rows, value_rows, upstream, allowed, score_scale):
    query_wide = query_rows.astype(jnp.float32)
    key_wide = key_rows.astype(jnp.float32)
    value_wide = value_rows.astype(jnp.float32)
    upstream_wide = upstream.astype(jnp.float32)
    scores = jnp.einsum('qhd,kd->hqk', query_wide, key_wide, precision=lax.Precision.HIGHEST) * score_scale
    scores = jnp.where(allowed[None], scores, -1e+30)
    row_max = lax.optimization_barrier(jnp.max(scores, axis=2, keepdims=True))
    weights = jnp.exp(scores - row_max)
    weights = weights / lax.optimization_barrier(jnp.sum(weights, axis=2, keepdims=True))
    probs_low = lax.optimization_barrier(weights.astype(jnp.bfloat16)).astype(jnp.float32)
    weight_grad = jnp.einsum('qhd,kd->hqk', upstream_wide, value_wide, precision=lax.Precision.HIGHEST)
    row_delta = lax.optimization_barrier(jnp.sum(weight_grad * weights, axis=2, keepdims=True))
    score_grad = weights * (weight_grad - row_delta) * score_scale
    score_low = lax.optimization_barrier(score_grad.astype(jnp.bfloat16)).astype(jnp.float32)
    grad_query = jnp.einsum('hqk,kd->qhd', score_low, key_wide, precision=lax.Precision.HIGHEST)
    grad_key = jnp.einsum('hqk,qhd->kd', score_low, query_wide, precision=lax.Precision.HIGHEST)
    grad_value = jnp.einsum('hqk,qhd->kd', probs_low, upstream_wide, precision=lax.Precision.HIGHEST)
    return (grad_query, grad_key, grad_value)

def head_grads(scaled, upstream, segments, heads_per_group, head_size):
    length = scaled.shape[0]
    groups = scaled.shape[1] // ((heads_per_group + 2) * head_size)
    blocks = scaled.reshape(length, groups, heads_per_group + 2, head_size)
    query_rows = jnp.moveaxis(blocks[:, :, :heads_per_group], 1, 0)
    key_rows = jnp.moveaxis(blocks[:, :, heads_per_group], 1, 0)
    value_rows = jnp.moveaxis(blocks[:, :, heads_per_group + 1], 1, 0)
    upstream_rows = jnp.moveaxis(upstream.reshape(length, groups, heads_per_group, head_size), 1, 0)
    positions = jnp.arange(length)
    allowed = (segments[:, None] == segments[None, :]) & (positions[None, :] <= positions[:, None])
    score_scale = head_size ** (-0.5)

    def per_group(group_items):
        grad_query, grad_key, grad_value = group_grads(group_items[0], group_items[1], group_items[2], group_items[3], allowed, score_scale)
        return jnp.concatenate([grad_query, grad_key[:, None], grad_value[:, None]], axis=1)
    stacked = lax.map(per_group, (query_rows, key_rows, value_rows, upstream_rows))
    return jnp.moveaxis(stacked, 0, 1).reshape(length, groups * (heads_per_group + 2) * head_size)

def sample_grad(sample_rows, segments, upstream, norm_gain, qkv_weight):
    model_width = sample_rows.shape[1]
    inv_rms = lax.rsqrt(lax.optimization_barrier(jnp.mean(sample_rows.astype(jnp.float32) * sample_rows.astype(jnp.float32), axis=1, keepdims=True)) + epsilon)
    normed = (sample_rows.astype(jnp.float32) * norm_gain).astype(jnp.bfloat16)
    unscaled = jnp.dot(normed, qkv_weight, preferred_element_type=jnp.float32)
    scaled = (unscaled * inv_rms).astype(jnp.bfloat16)
    grads = head_grads(scaled, upstream, segments, HEADS // KV_HEADS, HEAD_DIM)
    scaled_grad = (grads * inv_rms).astype(jnp.bfloat16)
    back_proj = lax.dot_general(scaled_grad, qkv_weight, (((1,), (1,)), ((), ())), preferred_element_type=jnp.float32)
    row_stat = lax.optimization_barrier(jnp.sum(grads * unscaled, axis=1, keepdims=True))
    row_grads = norm_gain * back_proj - sample_rows.astype(jnp.float32) * (inv_rms ** 3 / model_width) * row_stat
    return row_grads.astype(jnp.bfloat16)

def reference(audio_rows, vision_rows, audio_weight, vision_weight, text_rows, row_target, segment_ids, norm_gain, qkv_weight, attn_grad):
    audio_proj = jnp.dot(audio_rows, audio_weight, preferred_element_type=jnp.float32).astype(jnp.bfloat16)
    vision_matrix = vision_weight.reshape(AUDIO_WIDTH * MERGE, D)
    vision_proj = jnp.dot(vision_rows, vision_matrix, preferred_element_type=jnp.float32).astype(jnp.bfloat16)
    encoded = jnp.concatenate([audio_proj.reshape(SAMPLES, AUDIO_DEV, D), vision_proj.reshape(SAMPLES, VISION_DEV, D)], axis=1)
    encoded = encoded.reshape(SAMPLES * ENC_ROWS, D)
    targets = row_target.reshape(SAMPLES * ENC_ROWS).astype(jnp.int32)
    inputs = text_rows.at[targets].set(encoded).reshape(SAMPLES, TOK_DEV, D)
    upstream = attn_grad.reshape(SAMPLES, TOK_DEV, HEADS * HEAD_DIM)

    def per_sample(sample_items):
        return sample_grad(sample_items[0], sample_items[1], sample_items[2], norm_gain, qkv_weight)
    row_grads = lax.map(per_sample, (inputs, segment_ids, upstream)).reshape(TOKENS, D)
    enc_grads = row_grads[targets].reshape(SAMPLES, ENC_ROWS, D)
    audio_grad = enc_grads[:, :AUDIO_DEV].reshape(AUDIO_ROWS, D)
    vision_grad = enc_grads[:, AUDIO_DEV:].reshape(VISION_ROWS, D)
    return (audio_grad, vision_grad)
```

```python
import jax
import jax.numpy as jnp
from jax import lax
from jax.sharding import PartitionSpec as P

HEADS = 14
KV_HEADS = 2
HEAD_DIM = 128

epsilon = 1e-06


def group_grads(query_rows, key_rows, value_rows, upstream, allowed, score_scale):
    scores = (
        jnp.einsum("qhd,kd->hqk", query_rows, key_rows, preferred_element_type=jnp.float32)
        * score_scale
    )
    scores = jnp.where(allowed[None], scores, -1e30)
    row_max = jnp.max(scores, axis=2, keepdims=True)
    weights = jnp.exp(scores - row_max)
    weights = weights / jnp.sum(weights, axis=2, keepdims=True)
    probs_low = weights.astype(jnp.bfloat16)
    weight_grad = jnp.einsum(
        "qhd,kd->hqk", upstream, value_rows, preferred_element_type=jnp.float32
    )
    row_delta = jnp.sum(weight_grad * weights, axis=2, keepdims=True)
    score_grad = (weights * (weight_grad - row_delta) * score_scale).astype(jnp.bfloat16)
    grad_query = jnp.einsum("hqk,kd->qhd", score_grad, key_rows, preferred_element_type=jnp.float32)
    grad_key = jnp.einsum("hqk,qhd->kd", score_grad, query_rows, preferred_element_type=jnp.float32)
    grad_value = jnp.einsum("hqk,qhd->kd", probs_low, upstream, preferred_element_type=jnp.float32)
    return (grad_query, grad_key, grad_value)


def head_grads(scaled, upstream, segments, heads_per_group, head_size):
    length = scaled.shape[0]
    blocks = scaled.reshape(length, heads_per_group + 2, head_size)
    positions = jnp.arange(length)
    allowed = (segments[:, None] == segments[None, :]) & (positions[None, :] <= positions[:, None])
    grad_query, grad_key, grad_value = group_grads(
        blocks[:, :heads_per_group],
        blocks[:, heads_per_group],
        blocks[:, heads_per_group + 1],
        upstream.reshape(length, heads_per_group, head_size),
        allowed,
        head_size ** (-0.5),
    )
    stacked = jnp.concatenate([grad_query, grad_key[:, None], grad_value[:, None]], axis=1)
    return stacked.reshape(length, (heads_per_group + 2) * head_size)


def swap(x):
    return lax.ppermute(x, "tp", [(0, 1), (1, 0)])


def ranks(dest):
    count = dest.shape[1]
    same = dest[:, :, None] == dest[:, None, :]
    earlier = jnp.arange(count)[None, :] < jnp.arange(count)[:, None]
    return jnp.sum((same & earlier[None]).astype(jnp.int32), axis=2)


def local(
    audio_rows,
    vision_rows,
    audio_weight,
    vision_weight,
    text_rows,
    row_target,
    segment_ids,
    norm_gain,
    qkv_weight,
    attn_grad,
):
    bf16, f32 = jnp.bfloat16, jnp.float32
    t = lax.axis_index("tp")
    e = lax.axis_index("enc")
    j = lax.axis_index("seq")
    n_enc = 4
    n_seq = 16
    self_index = e * n_seq + j
    senders, enc_rows = row_target.shape
    length, slab = text_rows.shape
    audio_count, audio_width = audio_rows.shape
    vision_count = vision_rows.shape[0]
    merge = vision_weight.shape[1]
    k_rows = audio_weight.shape[0]
    cap = 4
    wide = slab // 128 // n_enc * 128
    tail = slab // n_enc - wide

    def columns(w):
        w = w.reshape(-1, slab)
        main = lax.dynamic_slice_in_dim(w, e * wide, wide, 1)
        last = lax.dynamic_slice_in_dim(w, n_enc * wide + e * tail, tail, 1)
        return jnp.concatenate([main, last], axis=1)

    shard = jnp.concatenate([columns(audio_weight), columns(vision_weight)], axis=0)
    gathered = lax.all_gather(shard, "seq", axis=0, tiled=False)
    w_audio = gathered[:, :k_rows].reshape(audio_width, wide + tail)
    w_vision = gathered[:, k_rows:].reshape(audio_width * merge, wide + tail)

    ah, vh = audio_count // 2, vision_count // 2
    audio_half = lax.dynamic_slice_in_dim(audio_rows, t * ah, ah, 0)
    vision_half = lax.dynamic_slice_in_dim(vision_rows, t * vh, vh, 0)
    packed = jnp.concatenate(
        [audio_half] + [vision_half[:, i * audio_width : (i + 1) * audio_width] for i in range(merge)],
        axis=0,
    )
    own = [packed] + [
        lax.ppermute(packed, "enc", [(i, (i + k) % n_enc) for i in range(n_enc)])
        for k in range(1, n_enc)
    ]
    other = [swap(b) for b in own]
    blocks = jnp.stack(own + other)
    x_audio = blocks[:, :ah].reshape(2 * n_enc * ah, audio_width)
    x_vision = jnp.concatenate(
        [
            blocks[:, ah + i * vh : ah + (i + 1) * vh].reshape(2 * n_enc * vh, audio_width)
            for i in range(merge)
        ],
        axis=1,
    )
    audio_proj = jnp.dot(x_audio, w_audio, preferred_element_type=f32).astype(bf16)
    vision_proj = jnp.dot(x_vision, w_vision, preferred_element_type=f32).astype(bf16)
    encoded = jnp.concatenate([audio_proj, vision_proj], axis=0)

    order = (e - jnp.arange(n_enc)) % n_enc
    line = row_target.reshape(n_enc, n_seq, enc_rows)[:, j]
    line_dest = line // length
    line_slot = line_dest * (n_enc * cap) + jnp.arange(n_enc)[:, None] * cap + ranks(line_dest)
    line_slot = line_slot[order]
    a_slot = line_slot[:, :audio_count].reshape(n_enc, 2, ah)
    v_slot = line_slot[:, audio_count:].reshape(n_enc, 2, vh)
    halves = jnp.stack([t, 1 - t])
    a_slot = jnp.moveaxis(a_slot, 1, 0)[halves].reshape(-1)
    v_slot = jnp.moveaxis(v_slot, 1, 0)[halves].reshape(-1)
    row_slot = jnp.concatenate([a_slot, v_slot])
    selector = (jnp.arange(senders * n_enc * cap)[:, None] == row_slot[None, :]).astype(bf16)
    outgoing = jnp.dot(selector, encoded, preferred_element_type=f32).astype(bf16)
    outgoing = outgoing.reshape(senders, n_enc * cap, wide + tail)

    dest = row_target // length
    mine = (dest == self_index).astype(jnp.int32)
    rank_all = jnp.cumsum(mine, axis=1) - 1
    hot = (rank_all[:, :, None] == jnp.arange(cap)[None, None, :]) & (mine[:, :, None] == 1)
    incoming = jnp.sum(jnp.where(hot, (row_target % length)[:, :, None] + 1, 0), axis=1) - 1
    by_line = incoming.reshape(n_enc, n_seq, cap).transpose(1, 0, 2).reshape(1, senders * cap)
    placement = (jnp.arange(length)[:, None] == by_line).astype(bf16)
    filled = jnp.max(placement, axis=1) > 0

    arrived = lax.all_to_all(outgoing, ("enc", "seq"), split_axis=0, concat_axis=0, tiled=True)
    arrived = arrived.reshape(n_enc, senders * cap, wide + tail)
    placed = jnp.einsum("ps,esc->epc", placement, arrived, preferred_element_type=f32).astype(bf16)
    placed = jnp.concatenate(
        [placed[i, :, :wide] for i in range(n_enc)] + [placed[i, :, wide:] for i in range(n_enc)],
        axis=1,
    )
    row_slab = jnp.where(filled[:, None], placed, text_rows)

    other_slab = swap(row_slab)
    full_rows = jnp.concatenate(
        [jnp.where(t == 0, row_slab, other_slab), jnp.where(t == 0, other_slab, row_slab)], axis=1
    )
    model_width = full_rows.shape[1]
    inv_rms = lax.rsqrt(
        jnp.mean(full_rows.astype(f32) * full_rows.astype(f32), axis=1, keepdims=True) + epsilon
    )
    normed = (full_rows.astype(f32) * norm_gain).astype(bf16)
    unscaled = jnp.dot(normed, qkv_weight, preferred_element_type=f32)
    scaled = (unscaled * inv_rms).astype(bf16)
    grads = head_grads(scaled, attn_grad, segment_ids[0], HEADS // KV_HEADS, HEAD_DIM)
    scaled_grad = (grads * inv_rms).astype(bf16)
    row_part = jnp.sum(grads * unscaled, axis=1, keepdims=True)
    partial_proj = lax.dot_general(
        scaled_grad, qkv_weight, (((1,), (1,)), ((), ())), preferred_element_type=f32
    )
    low, high = partial_proj[:, :slab], partial_proj[:, slab:]
    keep = jnp.where(t == 0, low, high)
    give = jnp.where(t == 0, high, low).astype(bf16)
    back = keep + swap(give).astype(f32)
    stat = row_part + swap(row_part)
    gain_slab = lax.dynamic_slice_in_dim(norm_gain, t * slab, slab, 0)
    row_grads = gain_slab * back - row_slab.astype(f32) * (inv_rms**3 / model_width) * stat
    row_grads = row_grads.astype(bf16)

    half = slab // 2
    flat = jnp.arange(senders * 2 * cap)
    slot_pos = incoming.reshape(-1)
    pos8 = jnp.broadcast_to(incoming[:, None, :], (senders, 2, cap)).reshape(-1, 1)
    part8 = (flat // cap % 2)[:, None]
    hits = pos8 == jnp.arange(length)[None, :]
    out8 = jnp.dot(
        (hits & (part8 == 0)).astype(bf16), row_grads[:, :half], preferred_element_type=f32
    ) + jnp.dot((hits & (part8 == 1)).astype(bf16), row_grads[:, half:], preferred_element_type=f32)
    out8 = out8.astype(bf16).reshape(senders, 2 * cap, half)
    returned = lax.all_to_all(out8, ("enc", "seq"), split_axis=0, concat_axis=0, tiled=True)
    returned = returned.reshape(senders * 2 * cap, half)
    own_target = lax.dynamic_index_in_dim(row_target, self_index, 0, keepdims=True)
    own_dest = own_target // length
    own_cell = (own_dest * (2 * cap) + ranks(own_dest)).reshape(-1, 1)
    result = jnp.concatenate(
        [
            jnp.dot(
                (own_cell + h * cap == flat[None, :]).astype(bf16),
                returned,
                preferred_element_type=f32,
            ).astype(bf16)
            for h in range(2)
        ],
        axis=1,
    )
    return (result[:audio_count], result[audio_count:])


def solution(mesh):
    in_specs = (
        P(("enc", "seq"), None),
        P(("enc", "seq"), None),
        P("seq", "tp"),
        P("seq", None, "tp"),
        P(("enc", "seq"), "tp"),
        P(),
        P(("enc", "seq"), None),
        P(),
        P(None, "tp"),
        P(("enc", "seq"), "tp"),
    )
    out_specs = (P(("enc", "seq"), "tp"), P(("enc", "seq"), "tp"))
    return jax.shard_map(local, mesh=mesh, in_specs=in_specs, out_specs=out_specs, check_vma=False)
```

```python
import jax
import jax.numpy as jnp
from jax import lax
from jax.experimental import pallas as pl
from jax.experimental.pallas import tpu as pltpu
from jax.sharding import PartitionSpec as P

HEAD_DIM = 128

epsilon = 1e-06


NT = (((1,), (1,)), ((), ()))
NN = (((1,), (0,)), ((), ()))
TAIL = 128


def dot(x, y, dims=NN):
    return lax.dot_general(x, y, dims, preferred_element_type=jnp.float32)


def attend_kernel(
    half_ref,
    own_ref,
    other_ref,
    gain_ref,
    weight_ref,
    upstream_ref,
    seg_row_ref,
    seg_col_ref,
    give_ref,
    keep_ref,
    inv_ref,
    stat_ref,
    normed_ref,
    unscaled_ref,
    scaled_ref,
    sgrad_ref,
    bias_ref,
):
    bf16, f32 = jnp.bfloat16, jnp.float32
    rows, slab = own_ref.shape
    group = weight_ref.shape[1]
    heads = group // HEAD_DIM - 2
    t = half_ref[0]
    own_at = pl.multiple_of(t * slab, HEAD_DIM)
    other_at = pl.multiple_of((1 - t) * slab, HEAD_DIM)
    score_scale = HEAD_DIM ** (-0.5)

    squares = jnp.zeros((rows, HEAD_DIM), f32)
    for part, ref in ((t, own_ref), (1 - t, other_ref)):
        gain = gain_ref[pl.ds(part, 1), :]
        for c in range(0, slab, HEAD_DIM):
            x = ref[:, c : c + HEAD_DIM].astype(f32)
            squares = squares + x * x
            at = pl.multiple_of(part * slab + c, HEAD_DIM)
            normed_ref[:, pl.ds(at, HEAD_DIM)] = (x * gain[:, c : c + HEAD_DIM]).astype(bf16)
    inv = lax.rsqrt(jnp.sum(squares, axis=1, keepdims=True) / (2 * slab) + epsilon)
    inv_ref[...] = inv

    width = 384

    @pl.loop(0, group // width)
    def _(n):
        cols = pl.ds(pl.multiple_of(n * width, width), width)
        value = dot(normed_ref[...], weight_ref[:, cols])
        unscaled_ref[:, cols] = value
        scaled_ref[:, cols] = (value * inv).astype(bf16)

    place_u = lax.broadcasted_iota(jnp.int32, (rows, rows), 0)
    place_t = lax.broadcasted_iota(jnp.int32, (rows, rows), 1)
    allowed = (seg_col_ref[...] == seg_row_ref[...]) & (place_u <= place_t)
    bias_ref[...] = jnp.where(allowed, 0.0, -1e30)

    key = scaled_ref[:, heads * HEAD_DIM : (heads + 1) * HEAD_DIM]
    val = scaled_ref[:, (heads + 1) * HEAD_DIM :]
    grad_key = jnp.zeros((rows, HEAD_DIM), f32)
    grad_val = jnp.zeros((rows, HEAD_DIM), f32)
    stat = jnp.zeros((rows, HEAD_DIM), f32)
    for h in range(heads):
        cols = slice(h * HEAD_DIM, (h + 1) * HEAD_DIM)
        query = scaled_ref[:, cols]
        up = upstream_ref[:, cols]
        scores = dot(key, query, NT) * score_scale + bias_ref[...]
        scores = jnp.exp(scores - jnp.max(scores, axis=0, keepdims=True))
        probs = scores * (1.0 / jnp.sum(scores, axis=0, keepdims=True))
        dprobs = dot(val, up, NT)
        delta = jnp.sum(probs * dprobs, axis=0, keepdims=True)
        sgrad = (probs * (dprobs - delta) * score_scale).astype(bf16)
        grad_val = grad_val + dot(probs.astype(bf16), up)
        grad_key = grad_key + dot(sgrad, query)
        grad_query = dot(sgrad.T, key)
        stat = stat + grad_query * unscaled_ref[:, cols]
        sgrad_ref[:, cols] = (grad_query * inv).astype(bf16)
    cols = slice(heads * HEAD_DIM, (heads + 1) * HEAD_DIM)
    stat = stat + grad_key * unscaled_ref[:, cols]
    sgrad_ref[:, cols] = (grad_key * inv).astype(bf16)
    cols = slice((heads + 1) * HEAD_DIM, (heads + 2) * HEAD_DIM)
    stat = stat + grad_val * unscaled_ref[:, cols]
    sgrad_ref[:, cols] = (grad_val * inv).astype(bf16)
    total = jnp.sum(stat, axis=1, keepdims=True)
    stat_ref[...] = total
    lane = lax.broadcasted_iota(jnp.int32, (rows, TAIL), 1)
    high = total.astype(bf16)
    low = (total - high.astype(f32)).astype(bf16)
    give_ref[:, slab:] = jnp.where(lane == 0, high.astype(f32), low.astype(f32)).astype(bf16)

    step = 256

    @pl.loop(0, slab // step)
    def _(n):
        at = pl.multiple_of(n * step, step)
        rows_at = pl.ds(pl.multiple_of(other_at + at, HEAD_DIM), step)
        give_ref[:, pl.ds(at, step)] = dot(sgrad_ref[...], weight_ref[rows_at, :], NT).astype(bf16)

    @pl.loop(0, slab // step)
    def _(n):
        at = pl.multiple_of(n * step, step)
        rows_at = pl.ds(pl.multiple_of(own_at + at, HEAD_DIM), step)
        keep_ref[:, pl.ds(at, step)] = dot(sgrad_ref[...], weight_ref[rows_at, :], NT)


def attend(half, own, other, norm_gain, qkv_weight, upstream, segments):
    rows, slab = own.shape
    group = qkv_weight.shape[1]
    f32, bf16 = jnp.float32, jnp.bfloat16
    vmem = pl.BlockSpec(memory_space=pltpu.VMEM)
    return pl.pallas_call(
        attend_kernel,
        out_shape=(
            jax.ShapeDtypeStruct((rows, slab + TAIL), bf16),
            jax.ShapeDtypeStruct((rows, slab), f32),
            jax.ShapeDtypeStruct((rows, 1), f32),
            jax.ShapeDtypeStruct((rows, 1), f32),
        ),
        in_specs=[pl.BlockSpec(memory_space=pltpu.SMEM)] + [vmem] * 7,
        out_specs=(vmem,) * 4,
        scratch_shapes=[
            pltpu.VMEM((rows, 2 * slab), bf16),
            pltpu.VMEM((rows, group), f32),
            pltpu.VMEM((rows, group), bf16),
            pltpu.VMEM((rows, group), bf16),
            pltpu.VMEM((rows, rows), f32),
        ],
        compiler_params=pltpu.CompilerParams(vmem_limit_bytes=40 * 1024 * 1024),
        cost_estimate=pl.CostEstimate(flops=5_000_000_000, bytes_accessed=14_000_000, transcendentals=500_000),
    )(
        half.reshape(1),
        own,
        other,
        norm_gain.reshape(2, slab),
        qkv_weight,
        upstream,
        segments.reshape(1, rows),
        segments.reshape(rows, 1),
    )


def swap(x):
    return lax.ppermute(x, "tp", [(0, 1), (1, 0)])


def ranks(dest):
    count = dest.shape[1]
    same = dest[:, :, None] == dest[:, None, :]
    earlier = jnp.arange(count)[None, :] < jnp.arange(count)[:, None]
    return jnp.sum((same & earlier[None]).astype(jnp.int32), axis=2)


def local(
    audio_rows,
    vision_rows,
    audio_weight,
    vision_weight,
    text_rows,
    row_target,
    segment_ids,
    norm_gain,
    qkv_weight,
    attn_grad,
):
    bf16, f32 = jnp.bfloat16, jnp.float32
    t = lax.axis_index("tp")
    e = lax.axis_index("enc")
    j = lax.axis_index("seq")
    n_enc = 4
    n_seq = 16
    self_index = e * n_seq + j
    senders, enc_rows = row_target.shape
    length, slab = text_rows.shape
    audio_count, audio_width = audio_rows.shape
    vision_count = vision_rows.shape[0]
    merge = vision_weight.shape[1]
    k_rows = audio_weight.shape[0]
    cap = 4
    wide = slab // 128 // n_enc * 128
    tail = slab // n_enc - wide

    def columns(w):
        w = w.reshape(-1, slab)
        main = lax.dynamic_slice_in_dim(w, e * wide, wide, 1)
        last = lax.dynamic_slice_in_dim(w, n_enc * wide + e * tail, tail, 1)
        return jnp.concatenate([main, last], axis=1)

    shard = jnp.concatenate([columns(audio_weight), columns(vision_weight)], axis=0)
    gathered = lax.all_gather(shard, "seq", axis=0, tiled=False)
    w_audio = gathered[:, :k_rows].reshape(audio_width, wide + tail)
    w_vision = gathered[:, k_rows:].reshape(audio_width * merge, wide + tail)

    ah, vh = audio_count // 2, vision_count // 2
    audio_half = lax.dynamic_slice_in_dim(audio_rows, t * ah, ah, 0)
    vision_half = lax.dynamic_slice_in_dim(vision_rows, t * vh, vh, 0)
    packed = jnp.concatenate(
        [audio_half] + [vision_half[:, i * audio_width : (i + 1) * audio_width] for i in range(merge)],
        axis=0,
    )
    own = [packed] + [
        lax.ppermute(packed, "enc", [(i, (i + k) % n_enc) for i in range(n_enc)])
        for k in range(1, n_enc)
    ]
    other = [swap(b) for b in own]
    blocks = jnp.stack(own + other)
    x_audio = blocks[:, :ah].reshape(2 * n_enc * ah, audio_width)
    x_vision = jnp.concatenate(
        [
            blocks[:, ah + i * vh : ah + (i + 1) * vh].reshape(2 * n_enc * vh, audio_width)
            for i in range(merge)
        ],
        axis=1,
    )
    audio_proj = jnp.dot(x_audio, w_audio, preferred_element_type=f32).astype(bf16)
    vision_proj = jnp.dot(x_vision, w_vision, preferred_element_type=f32).astype(bf16)
    encoded = jnp.concatenate([audio_proj, vision_proj], axis=0)

    order = (e - jnp.arange(n_enc)) % n_enc
    line = row_target.reshape(n_enc, n_seq, enc_rows)[:, j]
    line_dest = line // length
    line_slot = line_dest * (n_enc * cap) + jnp.arange(n_enc)[:, None] * cap + ranks(line_dest)
    line_slot = line_slot[order]
    a_slot = line_slot[:, :audio_count].reshape(n_enc, 2, ah)
    v_slot = line_slot[:, audio_count:].reshape(n_enc, 2, vh)
    halves = jnp.stack([t, 1 - t])
    a_slot = jnp.moveaxis(a_slot, 1, 0)[halves].reshape(-1)
    v_slot = jnp.moveaxis(v_slot, 1, 0)[halves].reshape(-1)
    row_slot = jnp.concatenate([a_slot, v_slot])
    selector = (jnp.arange(senders * n_enc * cap)[:, None] == row_slot[None, :]).astype(bf16)
    outgoing = jnp.dot(selector, encoded, preferred_element_type=f32).astype(bf16)
    outgoing = outgoing.reshape(senders, n_enc * cap, wide + tail)

    dest = row_target // length
    mine = (dest == self_index).astype(jnp.int32)
    rank_all = jnp.cumsum(mine, axis=1) - 1
    hot = (rank_all[:, :, None] == jnp.arange(cap)[None, None, :]) & (mine[:, :, None] == 1)
    incoming = jnp.sum(jnp.where(hot, (row_target % length)[:, :, None] + 1, 0), axis=1) - 1
    by_line = incoming.reshape(n_enc, n_seq, cap).transpose(1, 0, 2).reshape(1, senders * cap)
    placement = (jnp.arange(length)[:, None] == by_line).astype(bf16)
    filled = jnp.max(placement, axis=1) > 0

    arrived = lax.all_to_all(outgoing, ("enc", "seq"), split_axis=0, concat_axis=0, tiled=True)
    arrived = arrived.reshape(n_enc, senders * cap, wide + tail)
    placed = jnp.einsum("ps,esc->epc", placement, arrived, preferred_element_type=f32).astype(bf16)
    placed = jnp.concatenate(
        [placed[i, :, :wide] for i in range(n_enc)] + [placed[i, :, wide:] for i in range(n_enc)],
        axis=1,
    )
    row_slab = jnp.where(filled[:, None], placed, text_rows)

    other_slab = swap(row_slab)
    give, keep, inv_rms, row_part = attend(
        t, row_slab, other_slab, norm_gain, qkv_weight, attn_grad, segment_ids[0]
    )
    model_width = 2 * slab
    taken = swap(give)
    back = keep + taken[:, :slab].astype(f32)
    stat = row_part + taken[:, slab : slab + 1].astype(f32) + taken[:, slab + 1 : slab + 2].astype(f32)
    gain_slab = lax.dynamic_slice_in_dim(norm_gain, t * slab, slab, 0)
    row_grads = gain_slab * back - row_slab.astype(f32) * (inv_rms**3 / model_width) * stat
    row_grads = row_grads.astype(bf16)

    half = slab // 2
    flat = jnp.arange(senders * 2 * cap)
    slot_pos = incoming.reshape(-1)
    pos8 = jnp.broadcast_to(incoming[:, None, :], (senders, 2, cap)).reshape(-1, 1)
    part8 = (flat // cap % 2)[:, None]
    hits = pos8 == jnp.arange(length)[None, :]
    out8 = jnp.dot(
        (hits & (part8 == 0)).astype(bf16), row_grads[:, :half], preferred_element_type=f32
    ) + jnp.dot((hits & (part8 == 1)).astype(bf16), row_grads[:, half:], preferred_element_type=f32)
    out8 = out8.astype(bf16).reshape(senders, 2 * cap, half)
    returned = lax.all_to_all(out8, ("enc", "seq"), split_axis=0, concat_axis=0, tiled=True)
    returned = returned.reshape(senders * 2 * cap, half)
    own_target = lax.dynamic_index_in_dim(row_target, self_index, 0, keepdims=True)
    own_dest = own_target // length
    own_cell = (own_dest * (2 * cap) + ranks(own_dest)).reshape(-1, 1)
    result = jnp.concatenate(
        [
            jnp.dot(
                (own_cell + h * cap == flat[None, :]).astype(bf16),
                returned,
                preferred_element_type=f32,
            ).astype(bf16)
            for h in range(2)
        ],
        axis=1,
    )
    return (result[:audio_count], result[audio_count:])


def solution(mesh):
    in_specs = (
        P(("enc", "seq"), None),
        P(("enc", "seq"), None),
        P("seq", "tp"),
        P("seq", None, "tp"),
        P(("enc", "seq"), "tp"),
        P(),
        P(("enc", "seq"), None),
        P(),
        P(None, "tp"),
        P(("enc", "seq"), "tp"),
    )
    out_specs = (P(("enc", "seq"), "tp"), P(("enc", "seq"), "tp"))
    return jax.shard_map(local, mesh=mesh, in_specs=in_specs, out_specs=out_specs, check_vma=False)
```

```python
import jax
import jax.numpy as jnp
from jax import lax
from jax.experimental import pallas as pl
from jax.experimental.pallas import tpu as pltpu
from jax.sharding import PartitionSpec as P

HEAD_DIM = 128

epsilon = 1e-06


NT = (((1,), (1,)), ((), ()))
NN = (((1,), (0,)), ((), ()))
TAIL = 128


def dot(x, y, dims=NN):
    return lax.dot_general(x, y, dims, preferred_element_type=jnp.float32)


def attend_kernel(
    half_ref,
    own_ref,
    other_ref,
    gain_ref,
    weight_ref,
    upstream_ref,
    seg_row_ref,
    seg_col_ref,
    give_ref,
    keep_ref,
    inv_ref,
    stat_ref,
    normed_ref,
    unscaled_ref,
    scaled_ref,
    sgrad_ref,
    bias_ref,
    held_ref,
    sems,
):
    bf16, f32 = jnp.bfloat16, jnp.float32
    rows, slab = own_ref.shape
    group = weight_ref.shape[1]
    heads = group // HEAD_DIM - 2
    width = held_ref.shape[2]
    pieces = group // width
    copies = [
        pltpu.make_async_copy(
            weight_ref.at[:, n * width : (n + 1) * width], held_ref.at[n], sems.at[n]
        )
        for n in range(pieces)
    ]
    for copy in copies:
        copy.start()
    t = half_ref[0]
    own_at = pl.multiple_of(t * slab, HEAD_DIM)
    other_at = pl.multiple_of((1 - t) * slab, HEAD_DIM)
    score_scale = HEAD_DIM ** (-0.5)

    squares = jnp.zeros((rows, HEAD_DIM), f32)
    for part, ref in ((t, own_ref), (1 - t, other_ref)):
        gain = gain_ref[pl.ds(part, 1), :]
        for c in range(0, slab, HEAD_DIM):
            x = ref[:, c : c + HEAD_DIM].astype(f32)
            squares = squares + x * x
            at = pl.multiple_of(part * slab + c, HEAD_DIM)
            normed_ref[:, pl.ds(at, HEAD_DIM)] = (x * gain[:, c : c + HEAD_DIM]).astype(bf16)
    inv = lax.rsqrt(jnp.sum(squares, axis=1, keepdims=True) / (2 * slab) + epsilon)
    inv_ref[...] = inv

    for n in range(pieces):
        copies[n].wait()
        value = dot(normed_ref[...], held_ref[n])
        unscaled_ref[:, n * width : (n + 1) * width] = value
        scaled_ref[:, n * width : (n + 1) * width] = (value * inv).astype(bf16)

    place_u = lax.broadcasted_iota(jnp.int32, (rows, rows), 0)
    place_t = lax.broadcasted_iota(jnp.int32, (rows, rows), 1)
    allowed = (seg_col_ref[...] == seg_row_ref[...]) & (place_u <= place_t)
    bias_ref[...] = jnp.where(allowed, 0.0, -1e30)

    key = scaled_ref[:, heads * HEAD_DIM : (heads + 1) * HEAD_DIM]
    val = scaled_ref[:, (heads + 1) * HEAD_DIM :]
    grad_key = jnp.zeros((rows, HEAD_DIM), f32)
    grad_val = jnp.zeros((rows, HEAD_DIM), f32)
    stat = jnp.zeros((rows, HEAD_DIM), f32)
    for h in range(heads):
        cols = slice(h * HEAD_DIM, (h + 1) * HEAD_DIM)
        query = scaled_ref[:, cols]
        up = upstream_ref[:, cols]
        scores = dot(key, query, NT) * score_scale + bias_ref[...]
        scores = jnp.exp(scores - jnp.max(scores, axis=0, keepdims=True))
        probs = scores * (1.0 / jnp.sum(scores, axis=0, keepdims=True))
        dprobs = dot(val, up, NT)
        delta = jnp.sum(probs * dprobs, axis=0, keepdims=True)
        sgrad = (probs * (dprobs - delta) * score_scale).astype(bf16)
        grad_val = grad_val + dot(probs.astype(bf16), up)
        grad_key = grad_key + dot(sgrad, query)
        grad_query = dot(sgrad.T, key)
        stat = stat + grad_query * unscaled_ref[:, cols]
        sgrad_ref[:, cols] = (grad_query * inv).astype(bf16)
    cols = slice(heads * HEAD_DIM, (heads + 1) * HEAD_DIM)
    stat = stat + grad_key * unscaled_ref[:, cols]
    sgrad_ref[:, cols] = (grad_key * inv).astype(bf16)
    cols = slice((heads + 1) * HEAD_DIM, (heads + 2) * HEAD_DIM)
    stat = stat + grad_val * unscaled_ref[:, cols]
    sgrad_ref[:, cols] = (grad_val * inv).astype(bf16)
    total = jnp.sum(stat, axis=1, keepdims=True)
    stat_ref[...] = total
    lane = lax.broadcasted_iota(jnp.int32, (rows, TAIL), 1)
    high = total.astype(bf16)
    low = (total - high.astype(f32)).astype(bf16)
    give_ref[:, slab:] = jnp.where(lane == 0, high.astype(f32), low.astype(f32)).astype(bf16)

    step = 256

    def rows_of(rows_at):
        return jnp.concatenate([held_ref[n, rows_at, :] for n in range(pieces)], axis=1)

    @pl.loop(0, slab // step)
    def _(n):
        at = pl.multiple_of(n * step, step)
        rows_at = pl.ds(pl.multiple_of(other_at + at, HEAD_DIM), step)
        give_ref[:, pl.ds(at, step)] = dot(sgrad_ref[...], rows_of(rows_at), NT).astype(bf16)

    @pl.loop(0, slab // step)
    def _(n):
        at = pl.multiple_of(n * step, step)
        rows_at = pl.ds(pl.multiple_of(own_at + at, HEAD_DIM), step)
        keep_ref[:, pl.ds(at, step)] = dot(sgrad_ref[...], rows_of(rows_at), NT)


def attend(half, own, other, norm_gain, qkv_weight, upstream, segments):
    rows, slab = own.shape
    group = qkv_weight.shape[1]
    f32, bf16 = jnp.float32, jnp.bfloat16
    vmem = pl.BlockSpec(memory_space=pltpu.VMEM)
    return pl.pallas_call(
        attend_kernel,
        out_shape=(
            jax.ShapeDtypeStruct((rows, slab + TAIL), bf16),
            jax.ShapeDtypeStruct((rows, slab), f32),
            jax.ShapeDtypeStruct((rows, 1), f32),
            jax.ShapeDtypeStruct((rows, 1), f32),
        ),
        in_specs=[pl.BlockSpec(memory_space=pltpu.SMEM), vmem, vmem, vmem]
        + [pl.BlockSpec(memory_space=pl.ANY), vmem, vmem, vmem],
        out_specs=(vmem,) * 4,
        scratch_shapes=[
            pltpu.VMEM((rows, 2 * slab), bf16),
            pltpu.VMEM((rows, group), f32),
            pltpu.VMEM((rows, group), bf16),
            pltpu.VMEM((rows, group), bf16),
            pltpu.VMEM((rows, rows), f32),
            pltpu.VMEM((group // 384, 2 * slab, 384), bf16),
            pltpu.SemaphoreType.DMA((group // 384,)),
        ],
        compiler_params=pltpu.CompilerParams(vmem_limit_bytes=28 * 1024 * 1024),
        cost_estimate=pl.CostEstimate(flops=5_000_000_000, bytes_accessed=14_000_000, transcendentals=500_000),
    )(
        half.reshape(1),
        own,
        other,
        norm_gain.reshape(2, slab),
        qkv_weight,
        upstream,
        segments.reshape(1, rows),
        segments.reshape(rows, 1),
    )


def roll_half(x):
    return pltpu.roll(x.astype(jnp.float32), 64, 1).astype(x.dtype)


A_ROWS, A_TAIL = 192, 96
B_ROWS, B_TAIL = 208, 112
A_PIECE = 3 * A_ROWS + A_TAIL
B_PIECE = 3 * B_ROWS + B_TAIL


def pack_kernel(e_ref, am_ref, at_ref, vm_ref, vt_ref, a_ref, b_ref):
    k = am_ref.shape[0]
    cut = A_ROWS - k
    for n in range(3):
        cols = slice(n * 128, (n + 1) * 128)
        a_ref[n * A_ROWS : n * A_ROWS + k, :] = am_ref[:, cols]
        a_ref[n * A_ROWS + k : (n + 1) * A_ROWS, :] = vm_ref[:cut, cols]
        b_ref[n * B_ROWS : (n + 1) * B_ROWS, :] = vm_ref[cut:, cols]
    odd = e_ref[0] % 2 == 1
    tail = jnp.concatenate([at_ref[...], vt_ref[...]], axis=0).astype(jnp.float32)
    moved = pltpu.roll(tail, 64, 1)
    first = jnp.where(odd, moved, tail)
    second = jnp.where(odd, tail, moved)
    lane = lax.broadcasted_iota(jnp.int32, (B_TAIL, 128), 1)
    a_ref[3 * A_ROWS :, :] = jnp.where(
        lane[:A_TAIL] < 64, first[:A_TAIL], second[A_TAIL:A_ROWS]
    ).astype(a_ref.dtype)
    high = jnp.concatenate(
        [second[A_ROWS + B_TAIL :], jnp.zeros((2 * B_TAIL - B_ROWS, 128), jnp.float32)], axis=0
    )
    b_ref[3 * B_ROWS :, :] = jnp.where(
        lane < 64, first[A_ROWS : A_ROWS + B_TAIL], high
    ).astype(b_ref.dtype)


def pack_weights(e, audio_main, audio_tail, vision_main, vision_tail):
    vmem = pl.BlockSpec(memory_space=pltpu.VMEM)
    return pl.pallas_call(
        pack_kernel,
        out_shape=(
            jax.ShapeDtypeStruct((A_PIECE, 128), jnp.bfloat16),
            jax.ShapeDtypeStruct((B_PIECE, 128), jnp.bfloat16),
        ),
        in_specs=[pl.BlockSpec(memory_space=pltpu.SMEM)] + [vmem] * 4,
        out_specs=(vmem,) * 2,
        compiler_params=pltpu.CompilerParams(vmem_limit_bytes=8 * 1024 * 1024),
        cost_estimate=pl.CostEstimate(flops=0, bytes_accessed=800_000, transcendentals=0),
    )(e.reshape(1), audio_main, audio_tail, vision_main, vision_tail)


def encode_kernel(
    a_at_ref,
    b_at_ref,
    ga0,
    ga1,
    ga2,
    ga3,
    gb0,
    gb1,
    gb2,
    gb3,
    own_ref,
    other_ref,
    cell_ref,
    out_ref,
    w_ref,
    ta_ref,
    tb_ref,
    x_ref,
    enc_ref,
    sems,
):
    bf16, f32 = jnp.bfloat16, jnp.float32
    audio_width = x_ref.shape[3]
    audio_k = audio_width // 16
    vision_k = 4 * audio_k
    cut = A_ROWS - audio_k
    pltpu.make_async_copy(own_ref, x_ref.at[0], sems.at[0]).start()
    pltpu.make_async_copy(other_ref, x_ref.at[1], sems.at[1]).start()
    for m, (ga, gb) in enumerate(((ga0, gb0), (ga1, gb1), (ga2, gb2), (ga3, gb3))):

        @pl.loop(0, 4)
        def _(n):
            p = m * 4 + n
            a_at = a_at_ref[p]
            b_at = b_at_ref[p]
            base_a = pl.multiple_of(n * A_PIECE, 16)
            base_b = pl.multiple_of(n * B_PIECE, 16)
            audio_at = pl.multiple_of(a_at * audio_k, 16)
            low_at = pl.multiple_of(audio_width + a_at * vision_k, 16)
            high_at = pl.multiple_of(audio_width + b_at * vision_k + cut, 16)
            for c in range(3):
                pltpu.make_async_copy(
                    ga.at[pl.ds(base_a + c * A_ROWS, audio_k), :],
                    w_ref.at[c, pl.ds(audio_at, audio_k), :],
                    sems.at[2],
                ).start()
                pltpu.make_async_copy(
                    ga.at[pl.ds(base_a + c * A_ROWS + audio_k, cut), :],
                    w_ref.at[c, pl.ds(low_at, cut), :],
                    sems.at[2],
                ).start()
                pltpu.make_async_copy(
                    gb.at[pl.ds(base_b + c * B_ROWS, B_ROWS), :],
                    w_ref.at[c, pl.ds(high_at, B_ROWS), :],
                    sems.at[2],
                ).start()
            pltpu.make_async_copy(
                ga.at[pl.ds(base_a + 3 * A_ROWS, A_TAIL), :], ta_ref.at[p], sems.at[3]
            ).start()
            pltpu.make_async_copy(
                gb.at[pl.ds(base_b + 3 * B_ROWS, B_TAIL), :], tb_ref.at[p], sems.at[4]
            ).start()

    count = cell_ref.shape[1]
    cells = out_ref.shape[0]
    line = lax.broadcasted_iota(jnp.int32, (cells, count), 0)
    first = jnp.where(line == cell_ref[0:1, :], 1.0, 0.0).astype(bf16)
    second = jnp.where(line == cell_ref[1:2, :], 1.0, 0.0).astype(bf16)

    pltpu.make_async_copy(ta_ref, ta_ref, sems.at[3]).wait()
    pltpu.make_async_copy(tb_ref, tb_ref, sems.at[4]).wait()

    @pl.loop(0, 16)
    def _(p):
        a_at = a_at_ref[p]
        b_at = b_at_ref[p]
        audio_at = pl.multiple_of(a_at * audio_k, 16)
        low_at = pl.multiple_of(audio_width + a_at * vision_k, 16)
        high_at = pl.multiple_of(audio_width + b_at * vision_k + cut, 16)
        ta = ta_ref[p]
        w_ref[3, pl.ds(audio_at, audio_k), :] = ta[:audio_k]
        w_ref[3, pl.ds(low_at, A_TAIL - audio_k), :] = ta[audio_k:]
        w_ref[3, pl.ds(low_at + (A_TAIL - audio_k), A_TAIL), :] = roll_half(ta)
        tb = tb_ref[p]
        w_ref[3, pl.ds(high_at, B_TAIL), :] = tb
        w_ref[3, pl.ds(high_at + B_TAIL, B_ROWS - B_TAIL), :] = roll_half(tb)[: B_ROWS - B_TAIL]

    pltpu.make_async_copy(own_ref, x_ref.at[0], sems.at[0]).wait()
    pltpu.make_async_copy(other_ref, x_ref.at[1], sems.at[1]).wait()
    pltpu.make_async_copy(w_ref.at[0:3], w_ref.at[0:3], sems.at[2]).wait()

    halves, n_enc = x_ref.shape[:2]
    audio = 64
    vision = 32
    n_audio = halves * n_enc * audio
    for c in (0, 2):
        cols = slice(c * 128, (c + 2) * 128)

        def weights(at, size):
            return jnp.concatenate([w_ref[c, at : at + size, :], w_ref[c + 1, at : at + size, :]], axis=1)

        rows = x_ref[:, :, :audio, :].reshape(n_audio, audio_width)
        enc_ref[:n_audio, cols] = dot(rows, weights(0, audio_width)).astype(bf16)
        total = jnp.zeros((halves * n_enc * vision, 256), f32)
        for i in range(4):
            rows = x_ref[:, :, audio + i * vision : audio + (i + 1) * vision, :]
            rows = rows.reshape(halves * n_enc * vision, audio_width)
            total = total + dot(rows, weights((i + 1) * audio_width, audio_width))
        enc_ref[n_audio:, cols] = total.astype(bf16)

    main = enc_ref[:, :384]
    out_ref[:, :384] = dot(first, main).astype(bf16)
    out_ref[:, 384:768] = dot(second, main).astype(bf16)
    last = enc_ref[:, 384:].astype(f32)
    lane = lax.broadcasted_iota(jnp.int32, last.shape, 1)
    last = jnp.where(lane < 64, last, 0.0)
    moved = pltpu.roll(last, 64, 1)
    out_ref[:, 768:] = (dot(first, last.astype(bf16)) + dot(second, moved.astype(bf16))).astype(bf16)


def encode(a_at, b_at, pieces_a, pieces_b, own, other, cells, n_cells):
    bf16 = jnp.bfloat16
    n_enc, rows, width = own.shape
    smem = pl.BlockSpec(memory_space=pltpu.SMEM)
    vmem = pl.BlockSpec(memory_space=pltpu.VMEM)
    anywhere = pl.BlockSpec(memory_space=pl.ANY)
    return pl.pallas_call(
        encode_kernel,
        out_shape=jax.ShapeDtypeStruct((n_cells, 896), bf16),
        in_specs=[smem, smem] + [anywhere] * 10 + [vmem],
        out_specs=vmem,
        scratch_shapes=[
            pltpu.VMEM((4, 5 * width, 128), bf16),
            pltpu.VMEM((16, A_TAIL, 128), bf16),
            pltpu.VMEM((16, B_TAIL, 128), bf16),
            pltpu.VMEM((2, n_enc, rows, width), bf16),
            pltpu.VMEM((cells.shape[1], 512), bf16),
            pltpu.SemaphoreType.DMA((5,)),
        ],
        compiler_params=pltpu.CompilerParams(vmem_limit_bytes=28 * 1024 * 1024),
        cost_estimate=pl.CostEstimate(
            flops=3_000_000_000, bytes_accessed=11_000_000, transcendentals=0
        ),
    )(a_at, b_at, *pieces_a, *pieces_b, own, other, cells)


def place_kernel(e_row_ref, arrived_ref, text_ref, filled_ref, out_ref):
    bf16, f32 = jnp.bfloat16, jnp.float32
    rows = out_ref.shape[0]
    each = arrived_ref.shape[0] // 4
    line = lax.broadcasted_iota(jnp.int32, (rows, each), 0)
    first = jnp.where(line == e_row_ref[0:1, :], 1.0, 0.0).astype(bf16)
    second = jnp.where(line == e_row_ref[1:2, :], 1.0, 0.0).astype(bf16)
    both = jnp.concatenate([first, second], axis=1)
    taken = filled_ref[...] > 0.5
    lane = lax.broadcasted_iota(jnp.int32, (rows, 128), 1)
    low = []
    high = []
    for e in range(4):
        at = slice(e * each, (e + 1) * each)
        main = jnp.concatenate([arrived_ref[at, :384], arrived_ref[at, 384:768]], axis=0)
        cols = slice(e * 384, (e + 1) * 384)
        text = text_ref[:, cols].astype(f32)
        out_ref[:, cols] = jnp.where(taken, dot(both, main), text).astype(bf16)
        last = arrived_ref[at, 768:]
        low.append(dot(first, last))
        high.append(dot(second, last))
    for q in range(2):
        left = low[2 * q] + pltpu.roll(high[2 * q], 64, 1)
        right = pltpu.roll(low[2 * q + 1], 64, 1) + high[2 * q + 1]
        cols = slice(1536 + q * 128, 1536 + (q + 1) * 128)
        text = text_ref[:, cols].astype(f32)
        out_ref[:, cols] = jnp.where(taken, jnp.where(lane < 64, left, right), text).astype(bf16)


def place(spots, arrived, text, filled):
    vmem = pl.BlockSpec(memory_space=pltpu.VMEM)
    return pl.pallas_call(
        place_kernel,
        out_shape=jax.ShapeDtypeStruct(text.shape, text.dtype),
        in_specs=[vmem] * 4,
        out_specs=vmem,
        compiler_params=pltpu.CompilerParams(vmem_limit_bytes=12 * 1024 * 1024),
        cost_estimate=pl.CostEstimate(flops=300_000_000, bytes_accessed=3_000_000, transcendentals=0),
    )(spots, arrived, text, filled)


def swap(x):
    return lax.ppermute(x, "tp", [(0, 1), (1, 0)])


def shift_y(x, k):
    return lax.ppermute(x, "seq", [(i, i // 4 * 4 + (i % 4 + k) % 4) for i in range(16)])


def shift_z(x, k):
    return lax.ppermute(x, "seq", [(i, (i // 4 + k) % 4 * 4 + i % 4) for i in range(16)])


def ranks(dest):
    count = dest.shape[1]
    same = dest[:, :, None] == dest[:, None, :]
    earlier = jnp.arange(count)[None, :] < jnp.arange(count)[:, None]
    return jnp.sum((same & earlier[None]).astype(jnp.int32), axis=2)


def local(
    audio_rows,
    vision_rows,
    audio_weight,
    vision_weight,
    text_rows,
    row_target,
    segment_ids,
    norm_gain,
    qkv_weight,
    attn_grad,
):
    bf16, f32 = jnp.bfloat16, jnp.float32
    t = lax.axis_index("tp")
    e = lax.axis_index("enc")
    j = lax.axis_index("seq")
    n_enc = 4
    n_seq = 16
    self_index = e * n_seq + j
    senders, enc_rows = row_target.shape
    length, slab = text_rows.shape
    audio_count, audio_width = audio_rows.shape
    vision_count = vision_rows.shape[0]
    merge = vision_weight.shape[1]
    cap = 4
    wide = slab // 128 // n_enc * 128

    def columns(w):
        axis = w.ndim - 1
        main = lax.dynamic_slice_in_dim(w, e * wide, wide, axis)
        last = lax.dynamic_slice_in_dim(w, n_enc * wide + (e // 2) * 128, 128, axis)
        return main.reshape(-1, wide), last.reshape(-1, 128)

    piece_a, piece_b = pack_weights(e, *columns(audio_weight), *columns(vision_weight))
    hops = (1, 3, 2)
    along_y = [piece_a] + [shift_y(piece_a, k) for k in hops]
    along_z = [piece_b] + [shift_z(piece_b, k) for k in hops]
    along_y, along_z = lax.optimization_barrier((along_y, along_z))
    stack_a = jnp.concatenate(along_y, axis=0)
    stack_b = jnp.concatenate(along_z, axis=0)
    stack_a, stack_b = lax.optimization_barrier((stack_a, stack_b))
    pieces_a = [stack_a] + [shift_z(stack_a, k) for k in hops]
    pieces_b = [stack_b] + [shift_y(stack_b, k) for k in hops]
    z, y = j // 4, j % 4
    back = jnp.array((0,) + hops, jnp.int32)
    a_at = (((z - back) % 4)[:, None] * 4 + ((y - back) % 4)[None, :]).reshape(-1)
    b_at = (((y - back) % 4)[:, None] + ((z - back) % 4)[None, :] * 4).reshape(-1)

    ah, vh = audio_count // 2, vision_count // 2
    audio_half = lax.dynamic_slice_in_dim(audio_rows, t * ah, ah, 0)
    vision_half = lax.dynamic_slice_in_dim(vision_rows, t * vh, vh, 0)
    packed = jnp.concatenate(
        [audio_half] + [vision_half[:, i * audio_width : (i + 1) * audio_width] for i in range(merge)],
        axis=0,
    )
    own = lax.all_gather(packed, "enc", axis=0, tiled=False)
    other = swap(own)

    line = row_target.reshape(n_enc, n_seq, enc_rows)[:, j]
    line_dest = line // length
    line_slot = line_dest * (n_enc * cap) + jnp.arange(n_enc)[:, None] * cap + ranks(line_dest)
    a_slot = line_slot[:, :audio_count].reshape(n_enc, 2, ah)
    v_slot = line_slot[:, audio_count:].reshape(n_enc, 2, vh)
    halves = jnp.stack([t, 1 - t])
    a_slot = jnp.moveaxis(a_slot, 1, 0)[halves].reshape(-1)
    v_slot = jnp.moveaxis(v_slot, 1, 0)[halves].reshape(-1)
    row_slot = jnp.concatenate([a_slot, v_slot])
    cell = row_slot // 16 * 8 + row_slot % 8
    part = row_slot // 8 % 2
    cells = jnp.stack([jnp.where(part == 0, cell, -1), jnp.where(part == 1, cell, -1)])

    dest = row_target // length
    mine = (dest == self_index).astype(jnp.int32)
    rank_all = jnp.cumsum(mine, axis=1) - 1
    hot = (rank_all[:, :, None] == jnp.arange(cap)[None, None, :]) & (mine[:, :, None] == 1)
    incoming = jnp.sum(jnp.where(hot, (row_target % length)[:, :, None] + 1, 0), axis=1) - 1
    by_line = incoming.reshape(2, 2, n_seq, cap).transpose(0, 2, 1, 3).reshape(2, -1)
    filled = jnp.max(
        (jnp.arange(length)[:, None] == incoming.reshape(1, -1)).astype(jnp.float32), axis=1, keepdims=True
    )
    outgoing = encode(a_at, b_at, pieces_a, pieces_b, own, other, cells, senders * 8)
    arrived = lax.all_to_all(
        outgoing.reshape(senders, 8, slab // 2), ("enc", "seq"), split_axis=0, concat_axis=0, tiled=True
    )
    row_slab = place(by_line, arrived.reshape(senders * 8, slab // 2), text_rows, filled)

    other_slab = swap(row_slab)
    give, keep, inv_rms, row_part = attend(
        t, row_slab, other_slab, norm_gain, qkv_weight, attn_grad, segment_ids[0]
    )
    model_width = 2 * slab
    taken = swap(give)
    back = keep + taken[:, :slab].astype(f32)
    stat = row_part + taken[:, slab : slab + 1].astype(f32) + taken[:, slab + 1 : slab + 2].astype(f32)
    gain_slab = lax.dynamic_slice_in_dim(norm_gain, t * slab, slab, 0)
    row_grads = gain_slab * back - row_slab.astype(f32) * (inv_rms**3 / model_width) * stat
    row_grads = row_grads.astype(bf16)

    half = slab // 2
    flat = jnp.arange(senders * 2 * cap)
    pos8 = jnp.broadcast_to(incoming[:, None, :], (senders, 2, cap)).reshape(-1, 1)
    part8 = (flat // cap % 2)[:, None]
    hits = pos8 == jnp.arange(length)[None, :]
    out8 = jnp.dot(
        (hits & (part8 == 0)).astype(bf16), row_grads[:, :half], preferred_element_type=f32
    ) + jnp.dot((hits & (part8 == 1)).astype(bf16), row_grads[:, half:], preferred_element_type=f32)
    out8 = out8.astype(bf16).reshape(senders, 2 * cap, half)
    returned = lax.all_to_all(out8, ("enc", "seq"), split_axis=0, concat_axis=0, tiled=True)
    returned = returned.reshape(senders * 2 * cap, half)
    own_target = lax.dynamic_index_in_dim(row_target, self_index, 0, keepdims=True)
    own_dest = own_target // length
    own_cell = (own_dest * (2 * cap) + ranks(own_dest)).reshape(-1, 1)
    result = jnp.concatenate(
        [
            jnp.dot(
                (own_cell + h * cap == flat[None, :]).astype(bf16),
                returned,
                preferred_element_type=f32,
            ).astype(bf16)
            for h in range(2)
        ],
        axis=1,
    )
    return (result[:audio_count], result[audio_count:])


def solution(mesh):
    in_specs = (
        P(("enc", "seq"), None),
        P(("enc", "seq"), None),
        P("seq", "tp"),
        P("seq", None, "tp"),
        P(("enc", "seq"), "tp"),
        P(),
        P(("enc", "seq"), None),
        P(),
        P(None, "tp"),
        P(("enc", "seq"), "tp"),
    )
    out_specs = (P(("enc", "seq"), "tp"), P(("enc", "seq"), "tp"))
    return jax.shard_map(local, mesh=mesh, in_specs=in_specs, out_specs=out_specs, check_vma=False)
```

```python
import jax
import jax.numpy as jnp
from jax import lax
from jax.experimental import pallas as pl
from jax.experimental.pallas import tpu as pltpu
from jax.sharding import PartitionSpec as P

HEAD_DIM = 128

epsilon = 1e-06


NT = (((1,), (1,)), ((), ()))
NN = (((1,), (0,)), ((), ()))
TAIL = 128
BIG = 56 * 1024 * 1024


def dot(x, y, dims=NN):
    return lax.dot_general(x, y, dims, preferred_element_type=jnp.float32)


def attend_kernel(
    half_ref,
    own_hbm,
    other_hbm,
    gain_ref,
    weight_ref,
    upstream_hbm,
    seg_row_ref,
    seg_col_ref,
    give_ref,
    keep_ref,
    inv_ref,
    stat_ref,
    normed_ref,
    unscaled_ref,
    scaled_ref,
    sgrad_ref,
    bias_ref,
    held_ref,
    own_ref,
    other_ref,
    upstream_ref,
    sems,
):
    bf16, f32 = jnp.bfloat16, jnp.float32
    rows, slab = own_hbm.shape
    group = weight_ref.shape[1]
    heads = group // HEAD_DIM - 2
    width = held_ref.shape[2]
    pieces = group // width
    copies = [
        pltpu.make_async_copy(
            weight_ref.at[:, n * width : (n + 1) * width], held_ref.at[n], sems.at[n]
        )
        for n in range(pieces)
    ]
    small = [
        pltpu.make_async_copy(own_hbm, own_ref, sems.at[pieces]),
        pltpu.make_async_copy(other_hbm, other_ref, sems.at[pieces + 1]),
        pltpu.make_async_copy(upstream_hbm, upstream_ref, sems.at[pieces + 2]),
    ]
    for copy in small[:2] + copies + small[2:]:
        copy.start()
    small[0].wait()
    small[1].wait()
    t = half_ref[0]
    own_at = pl.multiple_of(t * slab, HEAD_DIM)
    other_at = pl.multiple_of((1 - t) * slab, HEAD_DIM)
    score_scale = HEAD_DIM ** (-0.5)

    squares = jnp.zeros((rows, HEAD_DIM), f32)
    for part, ref in ((t, own_ref), (1 - t, other_ref)):
        gain = gain_ref[pl.ds(part, 1), :]
        for c in range(0, slab, HEAD_DIM):
            x = ref[:, c : c + HEAD_DIM].astype(f32)
            squares = squares + x * x
            at = pl.multiple_of(part * slab + c, HEAD_DIM)
            normed_ref[:, pl.ds(at, HEAD_DIM)] = (x * gain[:, c : c + HEAD_DIM]).astype(bf16)
    inv = lax.rsqrt(jnp.sum(squares, axis=1, keepdims=True) / (2 * slab) + epsilon)
    inv_ref[...] = inv

    for n in range(pieces):
        copies[n].wait()
        value = dot(normed_ref[...], held_ref[n])
        unscaled_ref[:, n * width : (n + 1) * width] = value
        scaled_ref[:, n * width : (n + 1) * width] = (value * inv).astype(bf16)

    place_u = lax.broadcasted_iota(jnp.int32, (rows, rows), 0)
    place_t = lax.broadcasted_iota(jnp.int32, (rows, rows), 1)
    allowed = (seg_col_ref[...] == seg_row_ref[...]) & (place_u <= place_t)
    bias_ref[...] = jnp.where(allowed, 0.0, -1e30)

    small[2].wait()
    key = scaled_ref[:, heads * HEAD_DIM : (heads + 1) * HEAD_DIM]
    val = scaled_ref[:, (heads + 1) * HEAD_DIM :]
    grad_key = jnp.zeros((rows, HEAD_DIM), f32)
    grad_val = jnp.zeros((rows, HEAD_DIM), f32)
    stat = jnp.zeros((rows, HEAD_DIM), f32)
    for h in range(heads):
        cols = slice(h * HEAD_DIM, (h + 1) * HEAD_DIM)
        query = scaled_ref[:, cols]
        up = upstream_ref[:, cols]
        scores = dot(key, query, NT) * score_scale + bias_ref[...]
        scores = jnp.exp(scores - jnp.max(scores, axis=0, keepdims=True))
        probs = scores * (1.0 / jnp.sum(scores, axis=0, keepdims=True))
        dprobs = dot(val, up, NT)
        delta = jnp.sum(probs * dprobs, axis=0, keepdims=True)
        sgrad = (probs * (dprobs - delta) * score_scale).astype(bf16)
        grad_val = grad_val + dot(probs.astype(bf16), up)
        grad_key = grad_key + dot(sgrad, query)
        grad_query = dot(sgrad.T, key)
        stat = stat + grad_query * unscaled_ref[:, cols]
        sgrad_ref[:, cols] = (grad_query * inv).astype(bf16)
    cols = slice(heads * HEAD_DIM, (heads + 1) * HEAD_DIM)
    stat = stat + grad_key * unscaled_ref[:, cols]
    sgrad_ref[:, cols] = (grad_key * inv).astype(bf16)
    cols = slice((heads + 1) * HEAD_DIM, (heads + 2) * HEAD_DIM)
    stat = stat + grad_val * unscaled_ref[:, cols]
    sgrad_ref[:, cols] = (grad_val * inv).astype(bf16)
    total = jnp.sum(stat, axis=1, keepdims=True)
    stat_ref[...] = total
    lane = lax.broadcasted_iota(jnp.int32, (rows, TAIL), 1)
    high = total.astype(bf16)
    low = (total - high.astype(f32)).astype(bf16)
    give_ref[:, slab:] = jnp.where(lane == 0, high.astype(f32), low.astype(f32)).astype(bf16)

    step = 256

    def rows_of(rows_at):
        return jnp.concatenate([held_ref[n, rows_at, :] for n in range(pieces)], axis=1)

    @pl.loop(0, slab // step)
    def _(n):
        at = pl.multiple_of(n * step, step)
        rows_at = pl.ds(pl.multiple_of(other_at + at, HEAD_DIM), step)
        give_ref[:, pl.ds(at, step)] = dot(sgrad_ref[...], rows_of(rows_at), NT).astype(bf16)

    @pl.loop(0, slab // step)
    def _(n):
        at = pl.multiple_of(n * step, step)
        rows_at = pl.ds(pl.multiple_of(own_at + at, HEAD_DIM), step)
        keep_ref[:, pl.ds(at, step)] = dot(sgrad_ref[...], rows_of(rows_at), NT)


def attend(half, own, other, norm_gain, qkv_weight, upstream, segments):
    rows, slab = own.shape
    group = qkv_weight.shape[1]
    f32, bf16 = jnp.float32, jnp.bfloat16
    vmem = pl.BlockSpec(memory_space=pltpu.VMEM)
    anywhere = pl.BlockSpec(memory_space=pl.ANY)
    return pl.pallas_call(
        attend_kernel,
        out_shape=(
            jax.ShapeDtypeStruct((rows, slab + TAIL), bf16),
            jax.ShapeDtypeStruct((rows, slab), f32),
            jax.ShapeDtypeStruct((rows, 1), f32),
            jax.ShapeDtypeStruct((rows, 1), f32),
        ),
        in_specs=[pl.BlockSpec(memory_space=pltpu.SMEM), anywhere, anywhere, vmem]
        + [anywhere, anywhere, vmem, vmem],
        out_specs=(vmem,) * 4,
        scratch_shapes=[
            pltpu.VMEM((rows, 2 * slab), bf16),
            pltpu.VMEM((rows, group), f32),
            pltpu.VMEM((rows, group), bf16),
            pltpu.VMEM((rows, group), bf16),
            pltpu.VMEM((rows, rows), f32),
            pltpu.VMEM((group // 384, 2 * slab, 384), bf16),
            pltpu.VMEM((rows, slab), bf16),
            pltpu.VMEM((rows, slab), bf16),
            pltpu.VMEM(upstream.shape, bf16),
            pltpu.SemaphoreType.DMA((group // 384 + 3,)),
        ],
        compiler_params=pltpu.CompilerParams(vmem_limit_bytes=BIG),
        cost_estimate=pl.CostEstimate(flops=5_000_000_000, bytes_accessed=14_000_000, transcendentals=500_000),
    )(
        half.reshape(1),
        own,
        other,
        norm_gain.reshape(2, slab),
        qkv_weight,
        upstream,
        segments.reshape(1, rows),
        segments.reshape(rows, 1),
    )


def roll_half(x):
    return pltpu.roll(x.astype(jnp.float32), 64, 1).astype(x.dtype)


A_ROWS, A_TAIL = 192, 96
B_ROWS, B_TAIL = 208, 112
A_PIECE = 3 * A_ROWS + A_TAIL
B_PIECE = 3 * B_ROWS + B_TAIL


def pack_kernel(
    place_ref, am_ref, at_ref, vm_ref, vt_ref, audio_ref, vision_ref, a_ref, b_ref, rows_ref, sems
):
    t = place_ref[1]
    width = rows_ref.shape[1]
    ah, vh = audio_ref.shape[0] // 2, vision_ref.shape[0] // 2
    copies = [
        pltpu.make_async_copy(
            audio_ref.at[pl.ds(pl.multiple_of(t * ah, 16), ah), :], rows_ref.at[:ah], sems.at[0]
        )
    ] + [
        pltpu.make_async_copy(
            vision_ref.at[pl.ds(pl.multiple_of(t * vh, 16), vh), i * width : (i + 1) * width],
            rows_ref.at[ah + i * vh : ah + (i + 1) * vh],
            sems.at[1 + i],
        )
        for i in range(4)
    ]
    for copy in copies:
        copy.start()
    k = am_ref.shape[0]
    cut = A_ROWS - k
    for n in range(3):
        cols = slice(n * 128, (n + 1) * 128)
        a_ref[n * A_ROWS : n * A_ROWS + k, :] = am_ref[:, cols]
        a_ref[n * A_ROWS + k : (n + 1) * A_ROWS, :] = vm_ref[:cut, cols]
        b_ref[n * B_ROWS : (n + 1) * B_ROWS, :] = vm_ref[cut:, cols]
    odd = place_ref[0] % 2 == 1
    tail = jnp.concatenate([at_ref[...], vt_ref[...]], axis=0).astype(jnp.float32)
    moved = pltpu.roll(tail, 64, 1)
    first = jnp.where(odd, moved, tail)
    second = jnp.where(odd, tail, moved)
    lane = lax.broadcasted_iota(jnp.int32, (B_TAIL, 128), 1)
    a_ref[3 * A_ROWS :, :] = jnp.where(
        lane[:A_TAIL] < 64, first[:A_TAIL], second[A_TAIL:A_ROWS]
    ).astype(a_ref.dtype)
    high = jnp.concatenate(
        [second[A_ROWS + B_TAIL :], jnp.zeros((2 * B_TAIL - B_ROWS, 128), jnp.float32)], axis=0
    )
    b_ref[3 * B_ROWS :, :] = jnp.where(
        lane < 64, first[A_ROWS : A_ROWS + B_TAIL], high
    ).astype(b_ref.dtype)
    for copy in copies:
        copy.wait()


def pack(where, audio_main, audio_tail, vision_main, vision_tail, audio_rows, vision_rows):
    vmem = pl.BlockSpec(memory_space=pltpu.VMEM)
    anywhere = pl.BlockSpec(memory_space=pl.ANY)
    return pl.pallas_call(
        pack_kernel,
        out_shape=(
            jax.ShapeDtypeStruct((A_PIECE, 128), jnp.bfloat16),
            jax.ShapeDtypeStruct((B_PIECE, 128), jnp.bfloat16),
            jax.ShapeDtypeStruct(
                (audio_rows.shape[0] // 2 + 2 * vision_rows.shape[0], audio_rows.shape[1]), jnp.bfloat16
            ),
        ),
        in_specs=[pl.BlockSpec(memory_space=pltpu.SMEM)] + [vmem] * 4 + [anywhere] * 2,
        out_specs=(vmem, vmem, anywhere),
        scratch_shapes=[pltpu.SemaphoreType.DMA((5,))],
        compiler_params=pltpu.CompilerParams(vmem_limit_bytes=8 * 1024 * 1024),
        cost_estimate=pl.CostEstimate(flops=0, bytes_accessed=800_000, transcendentals=0),
    )(where, audio_main, audio_tail, vision_main, vision_tail, audio_rows, vision_rows)


def encode_kernel(
    a_at_ref,
    b_at_ref,
    ga0,
    ga1,
    ga2,
    ga3,
    ga4,
    gb0,
    gb1,
    gb2,
    gb3,
    gb4,
    own_ref,
    other_ref,
    cell_ref,
    out_ref,
    w_ref,
    ta_ref,
    tb_ref,
    x_ref,
    enc_ref,
    sems,
):
    bf16, f32 = jnp.bfloat16, jnp.float32
    audio_width = x_ref.shape[3]
    audio_k = audio_width // 16
    vision_k = 4 * audio_k
    cut = A_ROWS - audio_k
    pltpu.make_async_copy(own_ref, x_ref.at[0], sems.at[0]).start()
    pltpu.make_async_copy(other_ref, x_ref.at[1], sems.at[1]).start()
    sources = ((ga0, gb0, 0, 4), (ga1, gb1, 4, 4), (ga2, gb2, 8, 4), (ga3, gb3, 12, 2), (ga4, gb4, 14, 2))
    for ga, gb, start, count in sources:

        @pl.loop(0, count)
        def _(n):
            p = start + n
            a_at = a_at_ref[p]
            b_at = b_at_ref[p]
            base_a = pl.multiple_of(n * A_PIECE, 16)
            base_b = pl.multiple_of(n * B_PIECE, 16)
            audio_at = pl.multiple_of(a_at * audio_k, 16)
            low_at = pl.multiple_of(audio_width + a_at * vision_k, 16)
            high_at = pl.multiple_of(audio_width + b_at * vision_k + cut, 16)
            for c in range(3):
                pltpu.make_async_copy(
                    ga.at[pl.ds(base_a + c * A_ROWS, audio_k), :],
                    w_ref.at[c, pl.ds(audio_at, audio_k), :],
                    sems.at[2 + c],
                ).start()
                pltpu.make_async_copy(
                    ga.at[pl.ds(base_a + c * A_ROWS + audio_k, cut), :],
                    w_ref.at[c, pl.ds(low_at, cut), :],
                    sems.at[2 + c],
                ).start()
                pltpu.make_async_copy(
                    gb.at[pl.ds(base_b + c * B_ROWS, B_ROWS), :],
                    w_ref.at[c, pl.ds(high_at, B_ROWS), :],
                    sems.at[2 + c],
                ).start()
            pltpu.make_async_copy(
                ga.at[pl.ds(base_a + 3 * A_ROWS, A_TAIL), :], ta_ref.at[p], sems.at[5]
            ).start()
            pltpu.make_async_copy(
                gb.at[pl.ds(base_b + 3 * B_ROWS, B_TAIL), :], tb_ref.at[p], sems.at[6]
            ).start()

    count = cell_ref.shape[1]
    cells = out_ref.shape[0]
    line = lax.broadcasted_iota(jnp.int32, (cells, count), 0)
    first = jnp.where(line == cell_ref[0:1, :], 1.0, 0.0).astype(bf16)
    second = jnp.where(line == cell_ref[1:2, :], 1.0, 0.0).astype(bf16)

    halves, n_enc = x_ref.shape[:2]
    audio = 64
    vision = 32
    n_audio = halves * n_enc * audio
    n_vision = halves * n_enc * vision

    def project(c):
        cols = slice(c * 128, (c + 2) * 128)

        def weights(at, size):
            return jnp.concatenate([w_ref[c, at : at + size, :], w_ref[c + 1, at : at + size, :]], axis=1)

        rows = x_ref[:, :, :audio, :].reshape(n_audio, audio_width)
        enc_ref[:n_audio, cols] = dot(rows, weights(0, audio_width)).astype(bf16)
        total = jnp.zeros((n_vision, 256), f32)
        for i in range(4):
            rows = x_ref[:, :, audio + i * vision : audio + (i + 1) * vision, :]
            rows = rows.reshape(n_vision, audio_width)
            total = total + dot(rows, weights((i + 1) * audio_width, audio_width))
        enc_ref[n_audio:, cols] = total.astype(bf16)

    pltpu.make_async_copy(own_ref, x_ref.at[0], sems.at[0]).wait()
    pltpu.make_async_copy(other_ref, x_ref.at[1], sems.at[1]).wait()
    pltpu.make_async_copy(w_ref.at[0], w_ref.at[0], sems.at[2]).wait()
    pltpu.make_async_copy(w_ref.at[1], w_ref.at[1], sems.at[3]).wait()
    project(0)

    pltpu.make_async_copy(ta_ref, ta_ref, sems.at[5]).wait()
    pltpu.make_async_copy(tb_ref, tb_ref, sems.at[6]).wait()

    @pl.loop(0, 16)
    def _(p):
        a_at = a_at_ref[p]
        b_at = b_at_ref[p]
        audio_at = pl.multiple_of(a_at * audio_k, 16)
        low_at = pl.multiple_of(audio_width + a_at * vision_k, 16)
        high_at = pl.multiple_of(audio_width + b_at * vision_k + cut, 16)
        ta = ta_ref[p]
        w_ref[3, pl.ds(audio_at, audio_k), :] = ta[:audio_k]
        w_ref[3, pl.ds(low_at, A_TAIL - audio_k), :] = ta[audio_k:]
        w_ref[3, pl.ds(low_at + (A_TAIL - audio_k), A_TAIL), :] = roll_half(ta)
        tb = tb_ref[p]
        w_ref[3, pl.ds(high_at, B_TAIL), :] = tb
        w_ref[3, pl.ds(high_at + B_TAIL, B_ROWS - B_TAIL), :] = roll_half(tb)[: B_ROWS - B_TAIL]

    pltpu.make_async_copy(w_ref.at[2], w_ref.at[2], sems.at[4]).wait()
    project(2)

    main = enc_ref[:, :384]
    out_ref[:, :384] = dot(first, main).astype(bf16)
    out_ref[:, 384:768] = dot(second, main).astype(bf16)
    last = enc_ref[:, 384:].astype(f32)
    lane = lax.broadcasted_iota(jnp.int32, last.shape, 1)
    last = jnp.where(lane < 64, last, 0.0)
    moved = pltpu.roll(last, 64, 1)
    out_ref[:, 768:] = (dot(first, last.astype(bf16)) + dot(second, moved.astype(bf16))).astype(bf16)


def encode(a_at, b_at, pieces_a, pieces_b, own, other, cells, n_cells):
    bf16 = jnp.bfloat16
    n_enc, rows, width = own.shape
    smem = pl.BlockSpec(memory_space=pltpu.SMEM)
    vmem = pl.BlockSpec(memory_space=pltpu.VMEM)
    anywhere = pl.BlockSpec(memory_space=pl.ANY)
    return pl.pallas_call(
        encode_kernel,
        out_shape=jax.ShapeDtypeStruct((n_cells, 896), bf16),
        in_specs=[smem, smem] + [anywhere] * 12 + [vmem],
        out_specs=vmem,
        scratch_shapes=[
            pltpu.VMEM((4, 5 * width, 128), bf16),
            pltpu.VMEM((16, A_TAIL, 128), bf16),
            pltpu.VMEM((16, B_TAIL, 128), bf16),
            pltpu.VMEM((2, n_enc, rows, width), bf16),
            pltpu.VMEM((cells.shape[1], 512), bf16),
            pltpu.SemaphoreType.DMA((7,)),
        ],
        compiler_params=pltpu.CompilerParams(vmem_limit_bytes=BIG),
        cost_estimate=pl.CostEstimate(
            flops=3_000_000_000, bytes_accessed=11_000_000, transcendentals=0
        ),
    )(a_at, b_at, *pieces_a, *pieces_b, own, other, cells)


def place_kernel(e_row_ref, arrived_ref, text_ref, filled_ref, out_ref):
    bf16, f32 = jnp.bfloat16, jnp.float32
    rows = out_ref.shape[0]
    each = arrived_ref.shape[0] // 4
    line = lax.broadcasted_iota(jnp.int32, (rows, each), 0)
    first = jnp.where(line == e_row_ref[0:1, :], 1.0, 0.0).astype(bf16)
    second = jnp.where(line == e_row_ref[1:2, :], 1.0, 0.0).astype(bf16)
    both = jnp.concatenate([first, second], axis=1)
    taken = filled_ref[...] > 0.5
    lane = lax.broadcasted_iota(jnp.int32, (rows, 128), 1)
    low = []
    high = []
    for e in range(4):
        at = slice(e * each, (e + 1) * each)
        main = jnp.concatenate([arrived_ref[at, :384], arrived_ref[at, 384:768]], axis=0)
        cols = slice(e * 384, (e + 1) * 384)
        text = text_ref[:, cols].astype(f32)
        out_ref[:, cols] = jnp.where(taken, dot(both, main), text).astype(bf16)
        last = arrived_ref[at, 768:]
        low.append(dot(first, last))
        high.append(dot(second, last))
    for q in range(2):
        left = low[2 * q] + pltpu.roll(high[2 * q], 64, 1)
        right = pltpu.roll(low[2 * q + 1], 64, 1) + high[2 * q + 1]
        cols = slice(1536 + q * 128, 1536 + (q + 1) * 128)
        text = text_ref[:, cols].astype(f32)
        out_ref[:, cols] = jnp.where(taken, jnp.where(lane < 64, left, right), text).astype(bf16)


def place(spots, arrived, text, filled):
    vmem = pl.BlockSpec(memory_space=pltpu.VMEM)
    return pl.pallas_call(
        place_kernel,
        out_shape=jax.ShapeDtypeStruct(text.shape, text.dtype),
        in_specs=[vmem] * 4,
        out_specs=vmem,
        compiler_params=pltpu.CompilerParams(vmem_limit_bytes=12 * 1024 * 1024),
        cost_estimate=pl.CostEstimate(flops=300_000_000, bytes_accessed=3_000_000, transcendentals=0),
    )(spots, arrived, text, filled)


def finish_kernel(
    half_ref, rows_ref, keep_ref, taken_ref, inv_ref, stat_ref, gain_ref, spot_ref, out_ref
):
    bf16, f32 = jnp.bfloat16, jnp.float32
    rows, slab = rows_ref.shape
    cells = out_ref.shape[0]
    half = slab // 2
    inv = inv_ref[...]
    sent = taken_ref[:, slab:].astype(f32)
    stat = stat_ref[...] + sent[:, 0:1] + sent[:, 1:2]
    factor = inv * inv * inv / (2 * slab) * stat
    gain = gain_ref[pl.ds(half_ref[0], 1), :]
    line = lax.broadcasted_iota(jnp.int32, (cells, rows), 1)
    first = jnp.where(line == spot_ref[:, 0:1], 1.0, 0.0).astype(bf16)
    second = jnp.where(line == spot_ref[:, 1:2], 1.0, 0.0).astype(bf16)

    def grads(cols):
        total = keep_ref[:, cols] + taken_ref[:, cols].astype(f32)
        return (gain[:, cols] * total - rows_ref[:, cols].astype(f32) * factor).astype(bf16)

    for c in range(0, half, 128):
        low = grads(slice(c, c + 128))
        high = grads(slice(half + c, half + c + 128))
        out_ref[:, c : c + 128] = (dot(first, low) + dot(second, high)).astype(bf16)


def finish(half, rows, keep, taken, inv, stat, norm_gain, spots):
    vmem = pl.BlockSpec(memory_space=pltpu.VMEM)
    cells = spots.shape[0]
    slab = rows.shape[1]
    return pl.pallas_call(
        finish_kernel,
        out_shape=jax.ShapeDtypeStruct((cells, slab // 2), jnp.bfloat16),
        in_specs=[pl.BlockSpec(memory_space=pltpu.SMEM)] + [vmem] * 7,
        out_specs=vmem,
        compiler_params=pltpu.CompilerParams(vmem_limit_bytes=16 * 1024 * 1024),
        cost_estimate=pl.CostEstimate(flops=500_000_000, bytes_accessed=4_000_000, transcendentals=0),
    )(half.reshape(1), rows, keep, taken, inv, stat, norm_gain.reshape(2, slab), spots)


def collect_kernel(cell_ref, returned_ref, audio_ref, vision_ref):
    bf16 = jnp.bfloat16
    count = cell_ref.shape[0]
    cells, half = returned_ref.shape
    audio = audio_ref.shape[0]
    line = lax.broadcasted_iota(jnp.int32, (count, cells), 1)
    for h in range(2):
        hot = jnp.where(line == cell_ref[...] + 4 * h, 1.0, 0.0).astype(bf16)
        value = dot(hot, returned_ref[...]).astype(bf16)
        cols = slice(h * half, (h + 1) * half)
        audio_ref[:, cols] = value[:audio]
        vision_ref[:, cols] = value[audio:]


def collect(cell, returned, audio):
    vmem = pl.BlockSpec(memory_space=pltpu.VMEM)
    count = cell.shape[0]
    width = 2 * returned.shape[1]
    return pl.pallas_call(
        collect_kernel,
        out_shape=(
            jax.ShapeDtypeStruct((audio, width), jnp.bfloat16),
            jax.ShapeDtypeStruct((count - audio, width), jnp.bfloat16),
        ),
        in_specs=[vmem] * 2,
        out_specs=(vmem,) * 2,
        compiler_params=pltpu.CompilerParams(vmem_limit_bytes=12 * 1024 * 1024),
        cost_estimate=pl.CostEstimate(flops=400_000_000, bytes_accessed=2_000_000, transcendentals=0),
    )(cell, returned)


def swap(x):
    return lax.ppermute(x, "tp", [(0, 1), (1, 0)])


def shift_y(x, k):
    return lax.ppermute(x, "seq", [(i, i // 4 * 4 + (i % 4 + k) % 4) for i in range(16)])


def shift_z(x, k):
    return lax.ppermute(x, "seq", [(i, (i // 4 + k) % 4 * 4 + i % 4) for i in range(16)])


def ranks(dest):
    count = dest.shape[1]
    same = dest[:, :, None] == dest[:, None, :]
    earlier = jnp.arange(count)[None, :] < jnp.arange(count)[:, None]
    return jnp.sum((same & earlier[None]).astype(jnp.int32), axis=2)


def local(
    audio_rows,
    vision_rows,
    audio_weight,
    vision_weight,
    text_rows,
    row_target,
    segment_ids,
    norm_gain,
    qkv_weight,
    attn_grad,
):
    bf16, f32 = jnp.bfloat16, jnp.float32
    t = lax.axis_index("tp")
    e = lax.axis_index("enc")
    j = lax.axis_index("seq")
    n_enc = 4
    n_seq = 16
    self_index = e * n_seq + j
    senders, enc_rows = row_target.shape
    length, slab = text_rows.shape
    audio_count, audio_width = audio_rows.shape
    vision_count = vision_rows.shape[0]
    merge = vision_weight.shape[1]
    cap = 4
    wide = slab // 128 // n_enc * 128

    def columns(w):
        axis = w.ndim - 1
        main = lax.dynamic_slice_in_dim(w, e * wide, wide, axis)
        last = lax.dynamic_slice_in_dim(w, n_enc * wide + (e // 2) * 128, 128, axis)
        return main.reshape(-1, wide), last.reshape(-1, 128)

    piece_a, piece_b, packed = pack(
        jnp.stack([e, t]),
        *columns(audio_weight),
        *columns(vision_weight),
        audio_rows,
        vision_rows,
    )
    hops = (1, 3, 2)
    along_y = [piece_a] + [shift_y(piece_a, k) for k in hops]
    along_z = [piece_b] + [shift_z(piece_b, k) for k in hops]
    along_y, along_z = lax.optimization_barrier((along_y, along_z))
    stack_a = jnp.concatenate(along_y, axis=0)
    stack_b = jnp.concatenate(along_z, axis=0)
    stack_a, stack_b = lax.optimization_barrier((stack_a, stack_b))
    near = [shift_z(stack_a, 1), shift_z(stack_a, 3), shift_y(stack_b, 1), shift_y(stack_b, 3)]
    own = lax.all_gather(packed, "enc", axis=0, tiled=False)
    near, own = lax.optimization_barrier((near, own))
    far_a = [shift_z(near[0][: 2 * A_PIECE], 1), shift_z(near[1][2 * A_PIECE :], 3)]
    far_b = [shift_y(near[2][: 2 * B_PIECE], 1), shift_y(near[3][2 * B_PIECE :], 3)]
    other = swap(own)
    pieces_a = [stack_a] + near[:2] + far_a
    pieces_b = [stack_b] + near[2:] + far_b
    z, y = j // 4, j % 4
    back = jnp.array((0,) + hops, jnp.int32)
    a_at = (((z - back) % 4)[:, None] * 4 + ((y - back) % 4)[None, :]).reshape(-1)
    b_at = (((y - back) % 4)[:, None] + ((z - back) % 4)[None, :] * 4).reshape(-1)

    ah, vh = audio_count // 2, vision_count // 2

    line = row_target.reshape(n_enc, n_seq, enc_rows)[:, j]
    line_dest = line // length
    line_slot = line_dest * (n_enc * cap) + jnp.arange(n_enc)[:, None] * cap + ranks(line_dest)
    a_slot = line_slot[:, :audio_count].reshape(n_enc, 2, ah)
    v_slot = line_slot[:, audio_count:].reshape(n_enc, 2, vh)
    halves = jnp.stack([t, 1 - t])
    a_slot = jnp.moveaxis(a_slot, 1, 0)[halves].reshape(-1)
    v_slot = jnp.moveaxis(v_slot, 1, 0)[halves].reshape(-1)
    row_slot = jnp.concatenate([a_slot, v_slot])
    cell = row_slot // 16 * 8 + row_slot % 8
    part = row_slot // 8 % 2
    cells = jnp.stack([jnp.where(part == 0, cell, -1), jnp.where(part == 1, cell, -1)])

    dest = row_target // length
    mine = (dest == self_index).astype(jnp.int32)
    rank_all = jnp.cumsum(mine, axis=1) - 1
    hot = (rank_all[:, :, None] == jnp.arange(cap)[None, None, :]) & (mine[:, :, None] == 1)
    incoming = jnp.sum(jnp.where(hot, (row_target % length)[:, :, None] + 1, 0), axis=1) - 1
    by_line = incoming.reshape(2, 2, n_seq, cap).transpose(0, 2, 1, 3).reshape(2, -1)
    filled = jnp.max(
        (jnp.arange(length)[:, None] == incoming.reshape(1, -1)).astype(jnp.float32), axis=1, keepdims=True
    )
    outgoing = encode(a_at, b_at, pieces_a, pieces_b, own, other, cells, senders * 8)
    arrived = lax.all_to_all(
        outgoing.reshape(senders, 8, slab // 2), ("enc", "seq"), split_axis=0, concat_axis=0, tiled=True
    )
    row_slab = place(by_line, arrived.reshape(senders * 8, slab // 2), text_rows, filled)

    other_slab = swap(row_slab)
    give, keep, inv_rms, row_part = attend(
        t, row_slab, other_slab, norm_gain, qkv_weight, attn_grad, segment_ids[0]
    )
    taken = swap(give)

    half = slab // 2
    nowhere = jnp.full_like(incoming, -1)
    spots = jnp.stack(
        [
            jnp.stack([incoming, nowhere], axis=1).reshape(-1),
            jnp.stack([nowhere, incoming], axis=1).reshape(-1),
        ],
        axis=1,
    )
    own_target = lax.dynamic_index_in_dim(row_target, self_index, 0, keepdims=True)
    own_dest = own_target // length
    own_cell = (own_dest * (2 * cap) + ranks(own_dest)).reshape(-1, 1)
    out8 = finish(t, row_slab, keep, taken, inv_rms, row_part, norm_gain, spots)
    returned = lax.all_to_all(
        out8.reshape(senders, 2 * cap, half), ("enc", "seq"), split_axis=0, concat_axis=0, tiled=True
    )
    return collect(own_cell, returned.reshape(senders * 2 * cap, half), audio_count)


def solution(mesh):
    in_specs = (
        P(("enc", "seq"), None),
        P(("enc", "seq"), None),
        P("seq", "tp"),
        P("seq", None, "tp"),
        P(("enc", "seq"), "tp"),
        P(),
        P(("enc", "seq"), None),
        P(),
        P(None, "tp"),
        P(("enc", "seq"), "tp"),
    )
    out_specs = (P(("enc", "seq"), "tp"), P(("enc", "seq"), "tp"))
    return jax.shard_map(local, mesh=mesh, in_specs=in_specs, out_specs=out_specs, check_vma=False)
```

```python
import jax
import jax.numpy as jnp
from jax import lax
from jax.experimental import pallas as pl
from jax.experimental.pallas import tpu as pltpu
from jax.sharding import PartitionSpec as P

HEAD_DIM = 128

epsilon = 1e-06


NT = (((1,), (1,)), ((), ()))
NN = (((1,), (0,)), ((), ()))
TAIL = 128
BIG = 60 * 1024 * 1024


def dot(x, y, dims=NN):
    return lax.dot_general(x, y, dims, preferred_element_type=jnp.float32)


def attend_kernel(
    half_ref,
    own_hbm,
    other_hbm,
    gain_ref,
    weight_ref,
    upstream_hbm,
    seg_row_ref,
    seg_col_ref,
    give_hbm,
    keep_hbm,
    inv_ref,
    stat_ref,
    normed_ref,
    unscaled_ref,
    scaled_ref,
    sgrad_ref,
    bias_ref,
    held_ref,
    own_ref,
    other_ref,
    upstream_ref,
    give_ref,
    keep_ref,
    sems,
):
    bf16, f32 = jnp.bfloat16, jnp.float32
    rows, slab = own_hbm.shape
    group = weight_ref.shape[1]
    heads = group // HEAD_DIM - 2
    chunks = [(at, min(512, group - at)) for at in range(0, group, 512)]
    pieces = len(chunks)
    copies = [
        pltpu.make_async_copy(
            weight_ref.at[:, at : at + size], held_ref.at[:, at : at + size], sems.at[n]
        )
        for n, (at, size) in enumerate(chunks)
    ]
    small = [
        pltpu.make_async_copy(own_hbm, own_ref, sems.at[pieces]),
        pltpu.make_async_copy(other_hbm, other_ref, sems.at[pieces + 1]),
        pltpu.make_async_copy(upstream_hbm, upstream_ref, sems.at[pieces + 2]),
    ]
    for copy in small[:2] + copies + small[2:]:
        copy.start()
    place_u = lax.broadcasted_iota(jnp.int32, (rows, rows), 0)
    place_t = lax.broadcasted_iota(jnp.int32, (rows, rows), 1)
    allowed = (seg_col_ref[...] == seg_row_ref[...]) & (place_u <= place_t)
    bias_ref[...] = jnp.where(allowed, 0.0, -1e30)

    small[0].wait()
    small[1].wait()
    t = half_ref[0]
    own_at = pl.multiple_of(t * slab, HEAD_DIM)
    other_at = pl.multiple_of((1 - t) * slab, HEAD_DIM)
    score_scale = HEAD_DIM ** (-0.5)

    squares = jnp.zeros((rows, HEAD_DIM), f32)
    for part, ref in ((t, own_ref), (1 - t, other_ref)):
        gain = gain_ref[pl.ds(part, 1), :]
        for c in range(0, slab, HEAD_DIM):
            x = ref[:, c : c + HEAD_DIM].astype(f32)
            squares = squares + x * x
            at = pl.multiple_of(part * slab + c, HEAD_DIM)
            normed_ref[:, pl.ds(at, HEAD_DIM)] = (x * gain[:, c : c + HEAD_DIM]).astype(bf16)
    inv = lax.rsqrt(jnp.sum(squares, axis=1, keepdims=True) / (2 * slab) + epsilon)
    inv_ref[...] = inv

    for n, (at, size) in enumerate(chunks):
        copies[n].wait()
        value = dot(normed_ref[...], held_ref[:, at : at + size])
        unscaled_ref[:, at : at + size] = value
        scaled_ref[:, at : at + size] = (value * inv).astype(bf16)

    small[2].wait()
    key = scaled_ref[:, heads * HEAD_DIM : (heads + 1) * HEAD_DIM]
    val = scaled_ref[:, (heads + 1) * HEAD_DIM :]
    grad_key = jnp.zeros((rows, HEAD_DIM), f32)
    grad_val = jnp.zeros((rows, HEAD_DIM), f32)
    stat = jnp.zeros((rows, HEAD_DIM), f32)
    for h in range(heads):
        cols = slice(h * HEAD_DIM, (h + 1) * HEAD_DIM)
        query = scaled_ref[:, cols]
        up = upstream_ref[:, cols]
        scores = dot(key, query, NT) * score_scale + bias_ref[...]
        scores = jnp.exp(scores - jnp.max(scores, axis=0, keepdims=True))
        probs = scores * (1.0 / jnp.sum(scores, axis=0, keepdims=True))
        dprobs = dot(val, up, NT)
        delta = jnp.sum(probs * dprobs, axis=0, keepdims=True)
        sgrad = (probs * (dprobs - delta) * score_scale).astype(bf16)
        grad_val = grad_val + dot(probs.astype(bf16), up)
        grad_key = grad_key + dot(sgrad, query)
        grad_query = dot(sgrad.T, key)
        stat = stat + grad_query * unscaled_ref[:, cols]
        sgrad_ref[:, cols] = (grad_query * inv).astype(bf16)
    cols = slice(heads * HEAD_DIM, (heads + 1) * HEAD_DIM)
    stat = stat + grad_key * unscaled_ref[:, cols]
    sgrad_ref[:, cols] = (grad_key * inv).astype(bf16)
    cols = slice((heads + 1) * HEAD_DIM, (heads + 2) * HEAD_DIM)
    stat = stat + grad_val * unscaled_ref[:, cols]
    sgrad_ref[:, cols] = (grad_val * inv).astype(bf16)
    total = jnp.sum(stat, axis=1, keepdims=True)
    stat_ref[...] = total
    lane = lax.broadcasted_iota(jnp.int32, (rows, TAIL), 1)
    high = total.astype(bf16)
    low = (total - high.astype(f32)).astype(bf16)
    give_ref[:, slab:] = jnp.where(lane == 0, high.astype(f32), low.astype(f32)).astype(bf16)

    keep_ref[...] = dot(sgrad_ref[...], held_ref[pl.ds(own_at, slab), :], NT).astype(bf16)
    keep_out = pltpu.make_async_copy(keep_ref, keep_hbm, sems.at[pieces + 3])
    keep_out.start()
    give_ref[:, :slab] = dot(sgrad_ref[...], held_ref[pl.ds(other_at, slab), :], NT).astype(bf16)
    give_out = pltpu.make_async_copy(give_ref, give_hbm, sems.at[pieces + 4])
    give_out.start()
    keep_out.wait()
    give_out.wait()


def attend(half, own, other, gain, qkv_weight, upstream, seg_row, seg_col):
    rows, slab = own.shape
    group = qkv_weight.shape[1]
    f32, bf16 = jnp.float32, jnp.bfloat16
    vmem = pl.BlockSpec(memory_space=pltpu.VMEM)
    anywhere = pl.BlockSpec(memory_space=pl.ANY)
    return pl.pallas_call(
        attend_kernel,
        out_shape=(
            jax.ShapeDtypeStruct((rows, slab + TAIL), bf16),
            jax.ShapeDtypeStruct((rows, slab), bf16),
            jax.ShapeDtypeStruct((rows, 1), f32),
            jax.ShapeDtypeStruct((rows, 1), f32),
        ),
        in_specs=[pl.BlockSpec(memory_space=pltpu.SMEM), anywhere, anywhere, vmem]
        + [anywhere, anywhere, vmem, vmem],
        out_specs=(anywhere, anywhere, vmem, vmem),
        scratch_shapes=[
            pltpu.VMEM((rows, 2 * slab), bf16),
            pltpu.VMEM((rows, group), f32),
            pltpu.VMEM((rows, group), bf16),
            pltpu.VMEM((rows, group), bf16),
            pltpu.VMEM((rows, rows), f32),
            pltpu.VMEM((2 * slab, group), bf16),
            pltpu.VMEM((rows, slab), bf16),
            pltpu.VMEM((rows, slab), bf16),
            pltpu.VMEM(upstream.shape, bf16),
            pltpu.VMEM((rows, slab + TAIL), bf16),
            pltpu.VMEM((rows, slab), bf16),
            pltpu.SemaphoreType.DMA((8,)),
        ],
        compiler_params=pltpu.CompilerParams(vmem_limit_bytes=BIG),
        cost_estimate=pl.CostEstimate(flops=5_000_000_000, bytes_accessed=14_000_000, transcendentals=500_000),
    )(
        half.reshape(1),
        own,
        other,
        gain,
        qkv_weight,
        upstream,
        seg_row,
        seg_col,
    )


def roll_half(x):
    return pltpu.roll(x.astype(jnp.float32), 64, 1).astype(x.dtype)


A_ROWS, A_TAIL = 192, 32
B_ROWS, B_TAIL = 208, 48
A_PIECE = A_ROWS + A_TAIL
B_PIECE = B_ROWS + B_TAIL


def pack_kernel(
    place_ref,
    audio_w_ref,
    vision_w_ref,
    audio_ref,
    vision_ref,
    a_ref,
    b_ref,
    rows_ref,
    am_ref,
    at_ref,
    vm_ref,
    vt_ref,
    sems,
    row_sems,
):
    e = place_ref[0]
    t = place_ref[1]
    main_at = pl.multiple_of(e * 384, 128)
    tail_at = pl.multiple_of(1536 + e // 2 * 128, 128)
    loads = [
        pltpu.make_async_copy(vision_w_ref.at[:, :, pl.ds(main_at, 384)], vm_ref, sems.at[0]),
        pltpu.make_async_copy(vision_w_ref.at[:, :, pl.ds(tail_at, 128)], vt_ref, sems.at[1]),
        pltpu.make_async_copy(audio_w_ref.at[:, pl.ds(main_at, 384)], am_ref, sems.at[2]),
        pltpu.make_async_copy(audio_w_ref.at[:, pl.ds(tail_at, 128)], at_ref, sems.at[3]),
    ]
    for copy in loads:
        copy.start()
    width = rows_ref.shape[1]
    ah, vh = audio_ref.shape[0] // 2, vision_ref.shape[0] // 2
    copies = [
        pltpu.make_async_copy(
            audio_ref.at[pl.ds(pl.multiple_of(t * ah, 16), ah), :], rows_ref.at[:ah], row_sems.at[0]
        )
    ] + [
        pltpu.make_async_copy(
            vision_ref.at[pl.ds(pl.multiple_of(t * vh, 16), vh), i * width : (i + 1) * width],
            rows_ref.at[ah + i * vh : ah + (i + 1) * vh],
            row_sems.at[1 + i],
        )
        for i in range(4)
    ]
    for copy in copies:
        copy.start()
    for copy in loads:
        copy.wait()
    k = am_ref.shape[0]
    cut = A_ROWS - k
    vision_main = vm_ref[...].reshape(4 * k, 384)
    a_ref[:k, :] = am_ref[...]
    a_ref[k:A_ROWS, :] = vision_main[:cut]
    b_ref[:B_ROWS, :] = vision_main[cut:]
    odd = e % 2 == 1
    vision_tail = vt_ref[...].reshape(4 * k, 128)
    tail = jnp.concatenate([at_ref[...], vision_tail], axis=0).astype(jnp.float32)
    moved = pltpu.roll(tail, 64, 1)
    first = jnp.where(odd, moved, tail)
    second = jnp.where(odd, tail, moved)
    lane = lax.broadcasted_iota(jnp.int32, (B_TAIL, 128), 1)
    for q in range(3):
        cols = slice(q * 128, (q + 1) * 128)
        low = first[q * A_TAIL : (q + 1) * A_TAIL]
        high = second[96 + q * A_TAIL : 96 + (q + 1) * A_TAIL]
        a_ref[A_ROWS:, cols] = jnp.where(lane[:A_TAIL] < 64, low, high).astype(a_ref.dtype)
    base = A_ROWS
    for q in range(2):
        cols = slice(q * 128, (q + 1) * 128)
        low = first[base + q * B_TAIL : base + (q + 1) * B_TAIL]
        high = second[base + 112 + q * B_TAIL : base + 112 + (q + 1) * B_TAIL]
        b_ref[B_ROWS:, cols] = jnp.where(lane < 64, low, high).astype(b_ref.dtype)
    b_ref[B_ROWS : B_ROWS + 16, 256:] = first[base + 96 : base + 112].astype(b_ref.dtype)
    b_ref[B_ROWS + 16 :, 256:] = jnp.zeros((B_TAIL - 16, 128), b_ref.dtype)
    for copy in copies:
        copy.wait()


def pack(where, audio_weight, vision_weight, audio_rows, vision_rows):
    bf16 = jnp.bfloat16
    vmem = pl.BlockSpec(memory_space=pltpu.VMEM)
    anywhere = pl.BlockSpec(memory_space=pl.ANY)
    k = audio_weight.shape[0]
    return pl.pallas_call(
        pack_kernel,
        out_shape=(
            jax.ShapeDtypeStruct((A_PIECE, 384), bf16),
            jax.ShapeDtypeStruct((B_PIECE, 384), bf16),
            jax.ShapeDtypeStruct(
                (audio_rows.shape[0] // 2 + 2 * vision_rows.shape[0], audio_rows.shape[1]), bf16
            ),
        ),
        in_specs=[pl.BlockSpec(memory_space=pltpu.SMEM)] + [anywhere] * 4,
        out_specs=(vmem, vmem, anywhere),
        scratch_shapes=[
            pltpu.VMEM((k, 384), bf16),
            pltpu.VMEM((k, 128), bf16),
            pltpu.VMEM((k, 4, 384), bf16),
            pltpu.VMEM((k, 4, 128), bf16),
            pltpu.SemaphoreType.DMA((4,)),
            pltpu.SemaphoreType.DMA((5,)),
        ],
        compiler_params=pltpu.CompilerParams(vmem_limit_bytes=BIG),
        cost_estimate=pl.CostEstimate(flops=0, bytes_accessed=1_800_000, transcendentals=0),
    )(where, audio_weight, vision_weight, audio_rows, vision_rows)


def encode_kernel(
    a_at_ref,
    b_at_ref,
    ga0,
    ga1,
    ga2,
    ga3,
    gb0,
    gb1,
    gb2,
    gb3,
    own_ref,
    other_ref,
    cell_ref,
    out_ref,
    w_ref,
    wt_ref,
    ta_ref,
    tb_ref,
    x_ref,
    enc_ref,
    sems,
):
    bf16, f32 = jnp.bfloat16, jnp.float32
    audio_width = x_ref.shape[3]
    audio_k = audio_width // 16
    vision_k = 4 * audio_k
    cut = A_ROWS - audio_k
    sources = ((ga0, gb0), (ga1, gb1), (ga2, gb2), (ga3, gb3))

    def spots(p):
        audio_at = pl.multiple_of(a_at_ref[p] * audio_k, 16)
        low_at = pl.multiple_of(audio_width + a_at_ref[p] * vision_k, 16)
        high_at = pl.multiple_of(audio_width + b_at_ref[p] * vision_k + cut, 16)
        return audio_at, low_at, high_at

    def bases(n):
        return pl.multiple_of(n * A_PIECE, 16), pl.multiple_of(n * B_PIECE, 16)

    for m, (ga, gb) in enumerate(sources):

        @pl.loop(0, 4)
        def _(n):
            p = m * 4 + n
            base_a, base_b = bases(n)
            pltpu.make_async_copy(
                ga.at[pl.ds(base_a + A_ROWS, A_TAIL), :], ta_ref.at[p], sems.at[2]
            ).start()
            pltpu.make_async_copy(
                gb.at[pl.ds(base_b + B_ROWS, B_TAIL), :], tb_ref.at[p], sems.at[3]
            ).start()

    pltpu.make_async_copy(own_ref, x_ref.at[0], sems.at[0]).start()
    pltpu.make_async_copy(other_ref, x_ref.at[1], sems.at[1]).start()
    for m, (ga, gb) in enumerate(sources):

        @pl.loop(0, 4)
        def _(n):
            base_a, base_b = bases(n)
            audio_at, low_at, high_at = spots(m * 4 + n)
            pltpu.make_async_copy(
                ga.at[pl.ds(base_a, audio_k), :], w_ref.at[pl.ds(audio_at, audio_k), :], sems.at[4]
            ).start()
            pltpu.make_async_copy(
                ga.at[pl.ds(base_a + audio_k, cut), :], w_ref.at[pl.ds(low_at, cut), :], sems.at[5]
            ).start()
            pltpu.make_async_copy(
                gb.at[pl.ds(base_b, B_ROWS), :], w_ref.at[pl.ds(high_at, B_ROWS), :], sems.at[5]
            ).start()

    count = cell_ref.shape[1]
    cells = out_ref.shape[0]
    line = lax.broadcasted_iota(jnp.int32, (cells, count), 0)
    first = jnp.where(line == cell_ref[0:1, :], 1.0, 0.0).astype(bf16)
    second = jnp.where(line == cell_ref[1:2, :], 1.0, 0.0).astype(bf16)

    pltpu.make_async_copy(ta_ref, ta_ref, sems.at[2]).wait()
    pltpu.make_async_copy(tb_ref, tb_ref, sems.at[3]).wait()

    @pl.loop(0, 16)
    def _(p):
        audio_at, low_at, high_at = spots(p)
        ta = jnp.concatenate([ta_ref[p, :, q * 128 : (q + 1) * 128] for q in range(3)], axis=0)
        wt_ref[pl.ds(audio_at, audio_k), :] = ta[:audio_k]
        wt_ref[pl.ds(low_at, 96 - audio_k), :] = ta[audio_k:]
        wt_ref[pl.ds(low_at + (96 - audio_k), 96), :] = roll_half(ta)
        tb = jnp.concatenate([tb_ref[p, :, q * 128 : (q + 1) * 128] for q in range(2)], axis=0)
        wt_ref[pl.ds(high_at, 96), :] = tb
        wt_ref[pl.ds(high_at + 96, 16), :] = tb_ref[p, :16, 256:]
        wt_ref[pl.ds(high_at + 112, 96), :] = roll_half(tb)

    halves, n_enc = x_ref.shape[:2]
    audio = 64
    vision = 32
    n_audio = halves * n_enc * audio
    n_vision = halves * n_enc * vision

    def weights(at):
        return jnp.concatenate([w_ref[at : at + audio_width, :], wt_ref[at : at + audio_width, :]], axis=1)

    pltpu.make_async_copy(own_ref, x_ref.at[0], sems.at[0]).wait()
    pltpu.make_async_copy(other_ref, x_ref.at[1], sems.at[1]).wait()
    pltpu.make_async_copy(w_ref.at[:audio_width], w_ref.at[:audio_width], sems.at[4]).wait()
    rows = x_ref[:, :, :audio, :].reshape(n_audio, audio_width)
    enc_ref[:n_audio, :] = dot(rows, weights(0)).astype(bf16)
    pltpu.make_async_copy(w_ref.at[audio_width:], w_ref.at[audio_width:], sems.at[5]).wait()
    total = jnp.zeros((n_vision, 512), f32)
    for i in range(4):
        rows = x_ref[:, :, audio + i * vision : audio + (i + 1) * vision, :]
        total = total + dot(rows.reshape(n_vision, audio_width), weights((i + 1) * audio_width))
    enc_ref[n_audio:, :] = total.astype(bf16)

    main = enc_ref[:, :384]
    out_ref[:, :384] = dot(first, main).astype(bf16)
    out_ref[:, 384:768] = dot(second, main).astype(bf16)
    last = enc_ref[:, 384:].astype(f32)
    lane = lax.broadcasted_iota(jnp.int32, last.shape, 1)
    last = jnp.where(lane < 64, last, 0.0)
    moved = pltpu.roll(last, 64, 1)
    out_ref[:, 768:] = (dot(first, last.astype(bf16)) + dot(second, moved.astype(bf16))).astype(bf16)


def encode(a_at, b_at, pieces_a, pieces_b, own, other, cells, n_cells):
    bf16 = jnp.bfloat16
    n_enc, rows, width = own.shape
    smem = pl.BlockSpec(memory_space=pltpu.SMEM)
    vmem = pl.BlockSpec(memory_space=pltpu.VMEM)
    anywhere = pl.BlockSpec(memory_space=pl.ANY)
    return pl.pallas_call(
        encode_kernel,
        out_shape=jax.ShapeDtypeStruct((n_cells, 896), bf16),
        in_specs=[smem, smem] + [anywhere] * 10 + [vmem],
        out_specs=vmem,
        scratch_shapes=[
            pltpu.VMEM((5 * width, 384), bf16),
            pltpu.VMEM((5 * width, 128), bf16),
            pltpu.VMEM((16, A_TAIL, 384), bf16),
            pltpu.VMEM((16, B_TAIL, 384), bf16),
            pltpu.VMEM((2, n_enc, rows, width), bf16),
            pltpu.VMEM((cells.shape[1], 512), bf16),
            pltpu.SemaphoreType.DMA((6,)),
        ],
        compiler_params=pltpu.CompilerParams(vmem_limit_bytes=BIG),
        cost_estimate=pl.CostEstimate(
            flops=3_000_000_000, bytes_accessed=11_000_000, transcendentals=0
        ),
    )(a_at, b_at, *pieces_a, *pieces_b, own, other, cells)


def place_kernel(e_row_ref, arrived_ref, text_hbm, filled_ref, out_ref, text_ref, sem):
    bf16, f32 = jnp.bfloat16, jnp.float32
    load = pltpu.make_async_copy(text_hbm, text_ref, sem)
    load.start()
    rows = out_ref.shape[0]
    each = arrived_ref.shape[0] // 4
    line = lax.broadcasted_iota(jnp.int32, (rows, each), 0)
    first = jnp.where(line == e_row_ref[0:1, :], 1.0, 0.0).astype(bf16)
    second = jnp.where(line == e_row_ref[1:2, :], 1.0, 0.0).astype(bf16)
    both = jnp.concatenate([first, second], axis=1)
    taken = filled_ref[...] > 0.5
    lane = lax.broadcasted_iota(jnp.int32, (rows, 128), 1)
    low = []
    high = []
    load.wait()
    for e in range(4):
        at = slice(e * each, (e + 1) * each)
        main = jnp.concatenate([arrived_ref[at, :384], arrived_ref[at, 384:768]], axis=0)
        cols = slice(e * 384, (e + 1) * 384)
        text = text_ref[:, cols].astype(f32)
        out_ref[:, cols] = jnp.where(taken, dot(both, main), text).astype(bf16)
        last = arrived_ref[at, 768:]
        low.append(dot(first, last))
        high.append(dot(second, last))
    for q in range(2):
        left = low[2 * q] + pltpu.roll(high[2 * q], 64, 1)
        right = pltpu.roll(low[2 * q + 1], 64, 1) + high[2 * q + 1]
        cols = slice(1536 + q * 128, 1536 + (q + 1) * 128)
        text = text_ref[:, cols].astype(f32)
        out_ref[:, cols] = jnp.where(taken, jnp.where(lane < 64, left, right), text).astype(bf16)


def place(spots, arrived, text, filled):
    vmem = pl.BlockSpec(memory_space=pltpu.VMEM)
    return pl.pallas_call(
        place_kernel,
        out_shape=jax.ShapeDtypeStruct(text.shape, text.dtype),
        in_specs=[vmem, vmem, pl.BlockSpec(memory_space=pl.ANY), vmem],
        out_specs=vmem,
        scratch_shapes=[pltpu.VMEM(text.shape, text.dtype), pltpu.SemaphoreType.DMA],
        compiler_params=pltpu.CompilerParams(vmem_limit_bytes=12 * 1024 * 1024),
        cost_estimate=pl.CostEstimate(flops=300_000_000, bytes_accessed=3_000_000, transcendentals=0),
    )(spots, arrived, text, filled)


def finish_kernel(
    half_ref,
    rows_hbm,
    keep_hbm,
    taken_hbm,
    inv_ref,
    stat_ref,
    gain_ref,
    spot_ref,
    out_ref,
    rows_ref,
    keep_ref,
    taken_ref,
    grad_ref,
    sems,
):
    bf16, f32 = jnp.bfloat16, jnp.float32
    copies = [
        pltpu.make_async_copy(taken_hbm, taken_ref, sems.at[0]),
        pltpu.make_async_copy(rows_hbm, rows_ref, sems.at[1]),
        pltpu.make_async_copy(keep_hbm, keep_ref, sems.at[2]),
    ]
    for copy in copies:
        copy.start()
    rows, slab = rows_ref.shape
    cells = out_ref.shape[0]
    half = slab // 2
    inv = inv_ref[...]
    gain = gain_ref[pl.ds(half_ref[0], 1), :]
    line = lax.broadcasted_iota(jnp.int32, (cells, rows), 1)
    first = jnp.where(line == spot_ref[:, 0:1], 1.0, 0.0).astype(bf16)
    second = jnp.where(line == spot_ref[:, 1:2], 1.0, 0.0).astype(bf16)
    both = jnp.concatenate([first, second], axis=1)
    for copy in copies:
        copy.wait()
    sent = taken_ref[:, slab:].astype(f32)
    stat = stat_ref[...] + sent[:, 0:1] + sent[:, 1:2]
    factor = inv * inv * inv / (2 * slab) * stat
    for c in range(0, slab, 128):
        cols = slice(c, c + 128)
        total = keep_ref[:, cols].astype(f32) + taken_ref[:, cols].astype(f32)
        value = (gain[:, cols] * total - rows_ref[:, cols].astype(f32) * factor).astype(bf16)
        at = c // half
        grad_ref[at * rows : (at + 1) * rows, c - at * half : c - at * half + 128] = value
    out_ref[...] = dot(both, grad_ref[...]).astype(bf16)


def finish(half, rows, keep, taken, inv, stat, gain, spots):
    bf16 = jnp.bfloat16
    vmem = pl.BlockSpec(memory_space=pltpu.VMEM)
    anywhere = pl.BlockSpec(memory_space=pl.ANY)
    cells = spots.shape[0]
    count, slab = rows.shape
    return pl.pallas_call(
        finish_kernel,
        out_shape=jax.ShapeDtypeStruct((cells, slab // 2), bf16),
        in_specs=[pl.BlockSpec(memory_space=pltpu.SMEM)] + [anywhere] * 3 + [vmem] * 4,
        out_specs=vmem,
        scratch_shapes=[
            pltpu.VMEM((count, slab), bf16),
            pltpu.VMEM((count, slab), bf16),
            pltpu.VMEM((count, slab + TAIL), bf16),
            pltpu.VMEM((2 * count, slab // 2), bf16),
            pltpu.SemaphoreType.DMA((3,)),
        ],
        compiler_params=pltpu.CompilerParams(vmem_limit_bytes=BIG),
        cost_estimate=pl.CostEstimate(flops=500_000_000, bytes_accessed=4_000_000, transcendentals=0),
    )(half.reshape(1), rows, keep, taken, inv, stat, gain, spots)


def collect_kernel(cell_ref, returned_ref, audio_ref, vision_ref):
    bf16 = jnp.bfloat16
    count = cell_ref.shape[0]
    cells, half = returned_ref.shape
    audio = audio_ref.shape[0]
    line = lax.broadcasted_iota(jnp.int32, (count, cells), 1)
    for h in range(2):
        hot = jnp.where(line == cell_ref[...] + 4 * h, 1.0, 0.0).astype(bf16)
        value = dot(hot, returned_ref[...]).astype(bf16)
        cols = slice(h * half, (h + 1) * half)
        audio_ref[:, cols] = value[:audio]
        vision_ref[:, cols] = value[audio:]


def collect(cell, returned, audio):
    vmem = pl.BlockSpec(memory_space=pltpu.VMEM)
    count = cell.shape[0]
    width = 2 * returned.shape[1]
    return pl.pallas_call(
        collect_kernel,
        out_shape=(
            jax.ShapeDtypeStruct((audio, width), jnp.bfloat16),
            jax.ShapeDtypeStruct((count - audio, width), jnp.bfloat16),
        ),
        in_specs=[vmem] * 2,
        out_specs=(vmem,) * 2,
        compiler_params=pltpu.CompilerParams(vmem_limit_bytes=12 * 1024 * 1024),
        cost_estimate=pl.CostEstimate(flops=400_000_000, bytes_accessed=2_000_000, transcendentals=0),
    )(cell, returned)


def swap(x):
    return lax.ppermute(x, "tp", [(0, 1), (1, 0)])


def shift_y(x, k):
    return lax.ppermute(x, "seq", [(i, i // 4 * 4 + (i % 4 + k) % 4) for i in range(16)])


def shift_z(x, k):
    return lax.ppermute(x, "seq", [(i, (i // 4 + k) % 4 * 4 + i % 4) for i in range(16)])


def ranks(dest):
    count = dest.shape[1]
    same = dest[:, :, None] == dest[:, None, :]
    earlier = jnp.arange(count)[None, :] < jnp.arange(count)[:, None]
    return jnp.sum((same & earlier[None]).astype(jnp.int32), axis=2)


def local(
    audio_rows,
    vision_rows,
    audio_weight,
    vision_weight,
    text_rows,
    row_target,
    segment_ids,
    norm_gain,
    qkv_weight,
    attn_grad,
):
    bf16, f32 = jnp.bfloat16, jnp.float32
    t = lax.axis_index("tp")
    e = lax.axis_index("enc")
    j = lax.axis_index("seq")
    n_enc = 4
    n_seq = 16
    self_index = e * n_seq + j
    senders, enc_rows = row_target.shape
    length, slab = text_rows.shape
    audio_count, audio_width = audio_rows.shape
    vision_count = vision_rows.shape[0]
    merge = vision_weight.shape[1]
    cap = 4
    wide = slab // 128 // n_enc * 128

    piece_a, piece_b, packed = pack(
        jnp.stack([e, t]),
        audio_weight,
        vision_weight,
        audio_rows,
        vision_rows,
    )
    hops = (1, 3, 2)
    along_y = [piece_a] + [shift_y(piece_a, k) for k in hops]
    along_z = [piece_b] + [shift_z(piece_b, k) for k in hops]
    along_y, along_z = lax.optimization_barrier((along_y, along_z))
    stack_a = jnp.concatenate(along_y, axis=0)
    stack_b = jnp.concatenate(along_z, axis=0)
    stack_a, stack_b = lax.optimization_barrier((stack_a, stack_b))
    pieces_a = [stack_a] + [shift_z(stack_a, k) for k in hops]
    pieces_b = [stack_b] + [shift_y(stack_b, k) for k in hops]
    own = lax.all_gather(packed, "enc", axis=0, tiled=False)
    z, y = j // 4, j % 4
    back = jnp.array((0,) + hops, jnp.int32)
    a_at = (((z - back) % 4)[:, None] * 4 + ((y - back) % 4)[None, :]).reshape(-1)
    b_at = (((y - back) % 4)[:, None] + ((z - back) % 4)[None, :] * 4).reshape(-1)

    ah, vh = audio_count // 2, vision_count // 2

    line = row_target.reshape(n_enc, n_seq, enc_rows)[:, j]
    line_dest = line // length
    line_slot = line_dest * (n_enc * cap) + jnp.arange(n_enc)[:, None] * cap + ranks(line_dest)
    a_slot = line_slot[:, :audio_count].reshape(n_enc, 2, ah)
    v_slot = line_slot[:, audio_count:].reshape(n_enc, 2, vh)
    halves = jnp.stack([t, 1 - t])
    a_slot = jnp.moveaxis(a_slot, 1, 0)[halves].reshape(-1)
    v_slot = jnp.moveaxis(v_slot, 1, 0)[halves].reshape(-1)
    row_slot = jnp.concatenate([a_slot, v_slot])
    cell = row_slot // 16 * 8 + row_slot % 8
    part = row_slot // 8 % 2
    cells = jnp.stack([jnp.where(part == 0, cell, -1), jnp.where(part == 1, cell, -1)])

    dest = row_target // length
    mine = (dest == self_index).astype(jnp.int32)
    rank_all = jnp.cumsum(mine, axis=1) - 1
    hot = (rank_all[:, :, None] == jnp.arange(cap)[None, None, :]) & (mine[:, :, None] == 1)
    incoming = jnp.sum(jnp.where(hot, (row_target % length)[:, :, None] + 1, 0), axis=1) - 1
    by_line = incoming.reshape(2, 2, n_seq, cap).transpose(0, 2, 1, 3).reshape(2, -1)
    filled = jnp.max(
        (jnp.arange(length)[:, None] == incoming.reshape(1, -1)).astype(jnp.float32), axis=1, keepdims=True
    )
    half = slab // 2
    nowhere = jnp.full_like(incoming, -1)
    spots = jnp.stack(
        [
            jnp.stack([incoming, nowhere], axis=1).reshape(-1),
            jnp.stack([nowhere, incoming], axis=1).reshape(-1),
        ],
        axis=1,
    )
    own_target = lax.dynamic_index_in_dim(row_target, self_index, 0, keepdims=True)
    own_dest = own_target // length
    own_cell = (own_dest * (2 * cap) + ranks(own_dest)).reshape(-1, 1)
    gain = norm_gain.reshape(2, slab)
    seg_row = segment_ids
    seg_col = segment_ids.reshape(length, 1)
    pieces_a, pieces_b, own, cells, by_line, filled, spots, own_cell, gain, seg_col, a_at, b_at = (
        lax.optimization_barrier(
            (pieces_a, pieces_b, own, cells, by_line, filled, spots, own_cell, gain, seg_col, a_at, b_at)
        )
    )
    other = swap(own)
    outgoing = encode(a_at, b_at, pieces_a, pieces_b, own, other, cells, senders * 8)
    arrived = lax.all_to_all(
        outgoing.reshape(senders, 8, slab // 2), ("enc", "seq"), split_axis=0, concat_axis=0, tiled=True
    )
    row_slab = place(by_line, arrived.reshape(senders * 8, slab // 2), text_rows, filled)

    other_slab = swap(row_slab)
    give, keep, inv_rms, row_part = attend(
        t, row_slab, other_slab, gain, qkv_weight, attn_grad, seg_row, seg_col
    )
    taken = swap(give)

    out8 = finish(t, row_slab, keep, taken, inv_rms, row_part, gain, spots)
    returned = lax.all_to_all(
        out8.reshape(senders, 2 * cap, half), ("enc", "seq"), split_axis=0, concat_axis=0, tiled=True
    )
    return collect(own_cell, returned.reshape(senders * 2 * cap, half), audio_count)


def solution(mesh):
    in_specs = (
        P(("enc", "seq"), None),
        P(("enc", "seq"), None),
        P("seq", "tp"),
        P("seq", None, "tp"),
        P(("enc", "seq"), "tp"),
        P(),
        P(("enc", "seq"), None),
        P(),
        P(None, "tp"),
        P(("enc", "seq"), "tp"),
    )
    out_specs = (P(("enc", "seq"), "tp"), P(("enc", "seq"), "tp"))
    return jax.shard_map(local, mesh=mesh, in_specs=in_specs, out_specs=out_specs, check_vma=False)
```

```python
import jax
import jax.numpy as jnp
from jax import lax
from jax.experimental import pallas as pl
from jax.experimental.pallas import tpu as pltpu
from jax.sharding import Mesh
from jax.sharding import PartitionSpec as P

HEAD_DIM = 128

epsilon = 1e-06


NT = (((1,), (1,)), ((), ()))
NN = (((1,), (0,)), ((), ()))
TAIL = 128
BIG = 26 * 1024 * 1024


def in_hbm(x):
    return pltpu.with_memory_space_constraint(x, pltpu.HBM)


def dot(x, y, dims=NN):
    return lax.dot_general(x, y, dims, preferred_element_type=jnp.float32)


def attend_kernel(
    half_ref,
    own_ref,
    other_ref,
    gain_ref,
    weight_ref,
    upstream_hbm,
    seg_row_ref,
    seg_col_ref,
    give_ref,
    keep_ref,
    inv_ref,
    stat_ref,
    normed_ref,
    unscaled_ref,
    scaled_ref,
    sgrad_ref,
    bias_ref,
    held_ref,
    upstream_ref,
    sems,
):
    bf16, f32 = jnp.bfloat16, jnp.float32
    rows, slab = own_ref.shape
    group = weight_ref.shape[1]
    heads = group // HEAD_DIM - 2
    chunks = [(at, min(512, group - at)) for at in range(0, group, 512)]
    pieces = len(chunks)
    copies = [
        pltpu.make_async_copy(
            weight_ref.at[:, at : at + size], held_ref.at[:, at : at + size], sems.at[n]
        )
        for n, (at, size) in enumerate(chunks)
    ]
    last = pltpu.make_async_copy(upstream_hbm, upstream_ref, sems.at[pieces])
    for copy in copies + [last]:
        copy.start()
    place_u = lax.broadcasted_iota(jnp.int32, (rows, rows), 0)
    place_t = lax.broadcasted_iota(jnp.int32, (rows, rows), 1)
    allowed = (seg_col_ref[...] == seg_row_ref[...]) & (place_u <= place_t)
    bias_ref[...] = jnp.where(allowed, 0.0, -1e30)

    t = half_ref[0]
    own_at = pl.multiple_of(t * slab, HEAD_DIM)
    other_at = pl.multiple_of((1 - t) * slab, HEAD_DIM)
    score_scale = HEAD_DIM ** (-0.5)

    squares = jnp.zeros((rows, HEAD_DIM), f32)
    for part, ref in ((t, own_ref), (1 - t, other_ref)):
        gain = gain_ref[pl.ds(part, 1), :]
        for c in range(0, slab, HEAD_DIM):
            x = ref[:, c : c + HEAD_DIM].astype(f32)
            squares = squares + x * x
            at = pl.multiple_of(part * slab + c, HEAD_DIM)
            normed_ref[:, pl.ds(at, HEAD_DIM)] = (x * gain[:, c : c + HEAD_DIM]).astype(bf16)
    inv = lax.rsqrt(jnp.sum(squares, axis=1, keepdims=True) / (2 * slab) + epsilon)
    inv_ref[...] = inv

    for n, (at, size) in enumerate(chunks):
        copies[n].wait()
        value = dot(normed_ref[...], held_ref[:, at : at + size])
        unscaled_ref[:, at : at + size] = value
        scaled_ref[:, at : at + size] = (value * inv).astype(bf16)

    last.wait()
    key = scaled_ref[:, heads * HEAD_DIM : (heads + 1) * HEAD_DIM]
    val = scaled_ref[:, (heads + 1) * HEAD_DIM :]
    grad_key = jnp.zeros((rows, HEAD_DIM), f32)
    grad_val = jnp.zeros((rows, HEAD_DIM), f32)
    stat = jnp.zeros((rows, HEAD_DIM), f32)
    for h in range(heads):
        cols = slice(h * HEAD_DIM, (h + 1) * HEAD_DIM)
        query = scaled_ref[:, cols]
        up = upstream_ref[:, cols]
        scores = dot(key, query, NT) * score_scale + bias_ref[...]
        scores = jnp.exp(scores - jnp.max(scores, axis=0, keepdims=True))
        probs = scores * (1.0 / jnp.sum(scores, axis=0, keepdims=True))
        dprobs = dot(val, up, NT)
        delta = jnp.sum(probs * dprobs, axis=0, keepdims=True)
        sgrad = (probs * (dprobs - delta) * score_scale).astype(bf16)
        grad_val = grad_val + dot(probs.astype(bf16), up)
        grad_key = grad_key + dot(sgrad, query)
        grad_query = dot(sgrad.T, key)
        stat = stat + grad_query * unscaled_ref[:, cols]
        sgrad_ref[:, cols] = (grad_query * inv).astype(bf16)
    cols = slice(heads * HEAD_DIM, (heads + 1) * HEAD_DIM)
    stat = stat + grad_key * unscaled_ref[:, cols]
    sgrad_ref[:, cols] = (grad_key * inv).astype(bf16)
    cols = slice((heads + 1) * HEAD_DIM, (heads + 2) * HEAD_DIM)
    stat = stat + grad_val * unscaled_ref[:, cols]
    sgrad_ref[:, cols] = (grad_val * inv).astype(bf16)
    total = jnp.sum(stat, axis=1, keepdims=True)
    stat_ref[...] = total
    lane = lax.broadcasted_iota(jnp.int32, (rows, TAIL), 1)
    high = total.astype(bf16)
    low = (total - high.astype(f32)).astype(bf16)
    give_ref[:, slab:] = jnp.where(lane == 0, high.astype(f32), low.astype(f32)).astype(bf16)

    keep_ref[...] = dot(sgrad_ref[...], held_ref[pl.ds(own_at, slab), :], NT).astype(bf16)
    give_ref[:, :slab] = dot(sgrad_ref[...], held_ref[pl.ds(other_at, slab), :], NT).astype(bf16)


def attend(half, own, other, gain, qkv_weight, upstream, seg_row, seg_col):
    rows, slab = own.shape
    group = qkv_weight.shape[1]
    f32, bf16 = jnp.float32, jnp.bfloat16
    vmem = pl.BlockSpec(memory_space=pltpu.VMEM)
    anywhere = pl.BlockSpec(memory_space=pl.ANY)
    return pl.pallas_call(
        attend_kernel,
        out_shape=(
            jax.ShapeDtypeStruct((rows, slab + TAIL), bf16),
            jax.ShapeDtypeStruct((rows, slab), bf16),
            jax.ShapeDtypeStruct((rows, 1), f32),
            jax.ShapeDtypeStruct((rows, 1), f32),
        ),
        in_specs=[pl.BlockSpec(memory_space=pltpu.SMEM), vmem, vmem, vmem]
        + [anywhere, anywhere, vmem, vmem],
        out_specs=(vmem,) * 4,
        scratch_shapes=[
            pltpu.VMEM((rows, 2 * slab), bf16),
            pltpu.VMEM((rows, group), f32),
            pltpu.VMEM((rows, group), bf16),
            pltpu.VMEM((rows, group), bf16),
            pltpu.VMEM((rows, rows), f32),
            pltpu.VMEM((2 * slab, group), bf16),
            pltpu.VMEM(upstream.shape, bf16),
            pltpu.SemaphoreType.DMA((4,)),
        ],
        compiler_params=pltpu.CompilerParams(vmem_limit_bytes=BIG),
        cost_estimate=pl.CostEstimate(flops=5_000_000_000, bytes_accessed=14_000_000, transcendentals=500_000),
    )(
        half.reshape(1),
        own,
        other,
        gain,
        in_hbm(qkv_weight),
        in_hbm(upstream),
        seg_row,
        seg_col,
    )


def roll_half(x):
    return pltpu.roll(x.astype(jnp.float32), 64, 1).astype(x.dtype)


A_ROWS, A_TAIL = 192, 32
B_ROWS, B_TAIL = 208, 48
A_PIECE = A_ROWS + A_TAIL
B_PIECE = B_ROWS + B_TAIL


def pack_kernel(
    place_ref,
    audio_w_ref,
    vision_w_ref,
    audio_ref,
    vision_ref,
    a_ref,
    b_ref,
    rows_ref,
    am_ref,
    at_ref,
    vm_ref,
    vt_ref,
    sems,
    row_sems,
):
    e = place_ref[0]
    t = place_ref[1]
    main_at = pl.multiple_of(e * 384, 128)
    tail_at = pl.multiple_of(1536 + e // 2 * 128, 128)
    loads = [
        pltpu.make_async_copy(vision_w_ref.at[:, :, pl.ds(main_at, 384)], vm_ref, sems.at[0]),
        pltpu.make_async_copy(vision_w_ref.at[:, :, pl.ds(tail_at, 128)], vt_ref, sems.at[1]),
        pltpu.make_async_copy(audio_w_ref.at[:, pl.ds(main_at, 384)], am_ref, sems.at[2]),
        pltpu.make_async_copy(audio_w_ref.at[:, pl.ds(tail_at, 128)], at_ref, sems.at[3]),
    ]
    for copy in loads:
        copy.start()
    width = rows_ref.shape[1]
    ah, vh = audio_ref.shape[0] // 2, vision_ref.shape[0] // 2
    copies = [
        pltpu.make_async_copy(
            audio_ref.at[pl.ds(pl.multiple_of(t * ah, 16), ah), :], rows_ref.at[:ah], row_sems.at[0]
        )
    ] + [
        pltpu.make_async_copy(
            vision_ref.at[pl.ds(pl.multiple_of(t * vh, 16), vh), i * width : (i + 1) * width],
            rows_ref.at[ah + i * vh : ah + (i + 1) * vh],
            row_sems.at[1 + i],
        )
        for i in range(4)
    ]
    for copy in copies:
        copy.start()
    for copy in loads:
        copy.wait()
    k = am_ref.shape[0]
    cut = A_ROWS - k
    vision_main = vm_ref[...].reshape(4 * k, 384)
    a_ref[:k, :] = am_ref[...]
    a_ref[k:A_ROWS, :] = vision_main[:cut]
    b_ref[:B_ROWS, :] = vision_main[cut:]
    odd = e % 2 == 1
    vision_tail = vt_ref[...].reshape(4 * k, 128)
    tail = jnp.concatenate([at_ref[...], vision_tail], axis=0).astype(jnp.float32)
    moved = pltpu.roll(tail, 64, 1)
    first = jnp.where(odd, moved, tail)
    second = jnp.where(odd, tail, moved)
    lane = lax.broadcasted_iota(jnp.int32, (B_TAIL, 128), 1)
    for q in range(3):
        cols = slice(q * 128, (q + 1) * 128)
        low = first[q * A_TAIL : (q + 1) * A_TAIL]
        high = second[96 + q * A_TAIL : 96 + (q + 1) * A_TAIL]
        a_ref[A_ROWS:, cols] = jnp.where(lane[:A_TAIL] < 64, low, high).astype(a_ref.dtype)
    base = A_ROWS
    for q in range(2):
        cols = slice(q * 128, (q + 1) * 128)
        low = first[base + q * B_TAIL : base + (q + 1) * B_TAIL]
        high = second[base + 112 + q * B_TAIL : base + 112 + (q + 1) * B_TAIL]
        b_ref[B_ROWS:, cols] = jnp.where(lane < 64, low, high).astype(b_ref.dtype)
    b_ref[B_ROWS : B_ROWS + 16, 256:] = first[base + 96 : base + 112].astype(b_ref.dtype)
    b_ref[B_ROWS + 16 :, 256:] = jnp.zeros((B_TAIL - 16, 128), b_ref.dtype)
    for copy in copies:
        copy.wait()


def pack(where, audio_weight, vision_weight, audio_rows, vision_rows):
    bf16 = jnp.bfloat16
    vmem = pl.BlockSpec(memory_space=pltpu.VMEM)
    anywhere = pl.BlockSpec(memory_space=pl.ANY)
    k = audio_weight.shape[0]
    return pl.pallas_call(
        pack_kernel,
        out_shape=(
            jax.ShapeDtypeStruct((A_PIECE, 384), bf16),
            jax.ShapeDtypeStruct((B_PIECE, 384), bf16),
            jax.ShapeDtypeStruct(
                (audio_rows.shape[0] // 2 + 2 * vision_rows.shape[0], audio_rows.shape[1]), bf16
            ),
        ),
        in_specs=[pl.BlockSpec(memory_space=pltpu.SMEM)] + [anywhere] * 4,
        out_specs=(vmem, vmem, vmem),
        scratch_shapes=[
            pltpu.VMEM((k, 384), bf16),
            pltpu.VMEM((k, 128), bf16),
            pltpu.VMEM((k, 4, 384), bf16),
            pltpu.VMEM((k, 4, 128), bf16),
            pltpu.SemaphoreType.DMA((4,)),
            pltpu.SemaphoreType.DMA((5,)),
        ],
        compiler_params=pltpu.CompilerParams(vmem_limit_bytes=BIG),
        cost_estimate=pl.CostEstimate(flops=0, bytes_accessed=1_800_000, transcendentals=0),
    )(where, in_hbm(audio_weight), in_hbm(vision_weight), in_hbm(audio_rows), in_hbm(vision_rows))


def encode_kernel(
    b_at_ref,
    ga,
    gb0,
    gb1,
    gb2,
    gb3,
    own_ref,
    other_ref,
    cell_ref,
    out_ref,
    wa_ref,
    wv_ref,
    ta_ref,
    tv_ref,
    ra_ref,
    rb_ref,
    x_ref,
    enc_ref,
    sems,
):
    bf16, f32 = jnp.bfloat16, jnp.float32
    audio_width = x_ref.shape[3]
    audio_k = wa_ref.shape[1]
    cut = A_ROWS - audio_k
    shards_b = (gb0, gb1, gb2, gb3)
    pltpu.make_async_copy(ga.at[:, A_ROWS:, :], ra_ref, sems.at[2]).start()
    for m, gb in enumerate(shards_b):
        pltpu.make_async_copy(
            gb.at[:, B_ROWS:, :], rb_ref.at[4 * m : 4 * m + 4], sems.at[3]
        ).start()
    pltpu.make_async_copy(own_ref, x_ref.at[0], sems.at[0]).start()
    pltpu.make_async_copy(other_ref, x_ref.at[1], sems.at[1]).start()
    audio_copy = pltpu.make_async_copy(ga.at[:, :audio_k, :], wa_ref, sems.at[4])
    audio_copy.start()
    low_copy = pltpu.make_async_copy(ga.at[:, audio_k:A_ROWS, :], wv_ref.at[:, :cut, :], sems.at[5])
    low_copy.start()
    for m, gb in enumerate(shards_b):
        for n in range(4):
            pltpu.make_async_copy(
                gb.at[n, :B_ROWS, :], wv_ref.at[b_at_ref[4 * m + n], cut:, :], sems.at[6]
            ).start()

    count = cell_ref.shape[1]
    cells = out_ref.shape[0]
    line = lax.broadcasted_iota(jnp.int32, (cells, count), 0)
    first = jnp.where(line == cell_ref[0:1, :], 1.0, 0.0).astype(bf16)
    second = jnp.where(line == cell_ref[1:2, :], 1.0, 0.0).astype(bf16)

    pltpu.make_async_copy(ra_ref, ra_ref, sems.at[2]).wait()

    @pl.loop(0, 16)
    def _(p):
        ta = jnp.concatenate([ra_ref[p, :, q * 128 : (q + 1) * 128] for q in range(3)], axis=0)
        ta_ref[p, :, :] = ta[:audio_k]
        tv_ref[p, : 96 - audio_k, :] = ta[audio_k:]
        tv_ref[p, 96 - audio_k : cut, :] = roll_half(ta)

    pltpu.make_async_copy(rb_ref, rb_ref, sems.at[3]).wait()

    @pl.loop(0, 16)
    def _(p):
        at = b_at_ref[p]
        tb = jnp.concatenate([rb_ref[p, :, q * 128 : (q + 1) * 128] for q in range(2)], axis=0)
        tv_ref[at, cut : cut + 96, :] = tb
        tv_ref[at, cut + 96 : cut + 112, :] = rb_ref[p, :16, 256:]
        tv_ref[at, cut + 112 :, :] = roll_half(tb)

    halves, n_enc = x_ref.shape[:2]
    audio = 64
    vision = 32
    n_audio = halves * n_enc * audio
    n_vision = halves * n_enc * vision

    def weights(main, last):
        size = main.shape[0] * main.shape[1]
        return jnp.concatenate([main.reshape(size, 384), last.reshape(size, 128)], axis=1)

    def keep_rows(value, base, each):
        run = 2 * each
        for h in range(2):
            for g in range(2):
                at = g * count + base + h * run
                enc_ref[at : at + run, :] = value[(2 * h + g) * run : (2 * h + g + 1) * run]

    pltpu.make_async_copy(own_ref, x_ref.at[0], sems.at[0]).wait()
    pltpu.make_async_copy(other_ref, x_ref.at[1], sems.at[1]).wait()
    audio_copy.wait()
    rows = x_ref[:, :, :audio, :].reshape(n_audio, audio_width)
    keep_rows(dot(rows, weights(wa_ref[...], ta_ref[...])).astype(bf16), 0, audio)
    low_copy.wait()
    pltpu.make_async_copy(wv_ref.at[:, cut:, :], wv_ref.at[:, cut:, :], sems.at[6]).wait()
    total = jnp.zeros((n_vision, 512), f32)
    for i in range(4):
        rows = x_ref[:, :, audio + i * vision : audio + (i + 1) * vision, :]
        part = weights(wv_ref[4 * i : 4 * i + 4], tv_ref[4 * i : 4 * i + 4])
        total = total + dot(rows.reshape(n_vision, audio_width), part)
    keep_rows(total.astype(bf16), 4 * audio, vision)

    out_ref[:, :384] = dot(first, enc_ref[:count, :384]).astype(bf16)
    out_ref[:, 384:768] = dot(second, enc_ref[count:, :384]).astype(bf16)
    low = dot(first, enc_ref[:count, 384:])
    high = dot(second, enc_ref[count:, 384:])
    lane = lax.broadcasted_iota(jnp.int32, low.shape, 1)
    out_ref[:, 768:] = jnp.where(lane < 64, low, pltpu.roll(high, 64, 1)).astype(bf16)


def encode(b_at, shards_a, shards_b, own, other, cells, n_cells):
    bf16 = jnp.bfloat16
    n_enc, rows, width = own.shape
    smem = pl.BlockSpec(memory_space=pltpu.SMEM)
    vmem = pl.BlockSpec(memory_space=pltpu.VMEM)
    anywhere = pl.BlockSpec(memory_space=pl.ANY)
    k = width // 16
    return pl.pallas_call(
        encode_kernel,
        out_shape=jax.ShapeDtypeStruct((n_cells, 896), bf16),
        in_specs=[smem] + [anywhere] * 7 + [vmem],
        out_specs=vmem,
        scratch_shapes=[
            pltpu.VMEM((16, k, 384), bf16),
            pltpu.VMEM((16, 4 * k, 384), bf16),
            pltpu.VMEM((16, k, 128), bf16),
            pltpu.VMEM((16, 4 * k, 128), bf16),
            pltpu.VMEM((16, A_TAIL, 384), bf16),
            pltpu.VMEM((16, B_TAIL, 384), bf16),
            pltpu.VMEM((2, n_enc, rows, width), bf16),
            pltpu.VMEM((2 * cells.shape[1], 512), bf16),
            pltpu.SemaphoreType.DMA((7,)),
        ],
        compiler_params=pltpu.CompilerParams(vmem_limit_bytes=BIG),
        cost_estimate=pl.CostEstimate(
            flops=3_000_000_000, bytes_accessed=11_000_000, transcendentals=0
        ),
    )(b_at, in_hbm(shards_a), *(in_hbm(x) for x in shards_b), in_hbm(own), other, cells)


def place_kernel(e_row_ref, arrived_ref, text_hbm, filled_ref, out_ref, text_ref, sem):
    bf16, f32 = jnp.bfloat16, jnp.float32
    load = pltpu.make_async_copy(text_hbm, text_ref, sem)
    load.start()
    rows = out_ref.shape[0]
    each = arrived_ref.shape[0] // 4
    line = lax.broadcasted_iota(jnp.int32, (rows, each), 0)
    first = jnp.where(line == e_row_ref[0:1, :], 1.0, 0.0).astype(bf16)
    second = jnp.where(line == e_row_ref[1:2, :], 1.0, 0.0).astype(bf16)
    both = jnp.concatenate([first, second], axis=1)
    taken = filled_ref[...] > 0.5
    lane = lax.broadcasted_iota(jnp.int32, (rows, 128), 1)
    low = []
    high = []
    load.wait()
    for e in range(4):
        at = slice(e * each, (e + 1) * each)
        main = jnp.concatenate([arrived_ref[at, :384], arrived_ref[at, 384:768]], axis=0)
        cols = slice(e * 384, (e + 1) * 384)
        text = text_ref[:, cols].astype(f32)
        out_ref[:, cols] = jnp.where(taken, dot(both, main), text).astype(bf16)
        last = arrived_ref[at, 768:]
        low.append(dot(first, last))
        high.append(dot(second, last))
    for q in range(2):
        left = low[2 * q] + pltpu.roll(high[2 * q], 64, 1)
        right = pltpu.roll(low[2 * q + 1], 64, 1) + high[2 * q + 1]
        cols = slice(1536 + q * 128, 1536 + (q + 1) * 128)
        text = text_ref[:, cols].astype(f32)
        out_ref[:, cols] = jnp.where(taken, jnp.where(lane < 64, left, right), text).astype(bf16)


def place(spots, arrived, text, filled):
    vmem = pl.BlockSpec(memory_space=pltpu.VMEM)
    return pl.pallas_call(
        place_kernel,
        out_shape=jax.ShapeDtypeStruct(text.shape, text.dtype),
        in_specs=[vmem, vmem, pl.BlockSpec(memory_space=pl.ANY), vmem],
        out_specs=vmem,
        scratch_shapes=[pltpu.VMEM(text.shape, text.dtype), pltpu.SemaphoreType.DMA],
        compiler_params=pltpu.CompilerParams(vmem_limit_bytes=12 * 1024 * 1024),
        cost_estimate=pl.CostEstimate(flops=300_000_000, bytes_accessed=3_000_000, transcendentals=0),
    )(spots, arrived, text, filled)


def finish_kernel(
    half_ref,
    rows_ref,
    keep_ref,
    taken_ref,
    inv_ref,
    stat_ref,
    gain_ref,
    spot_ref,
    out_ref,
    grad_ref,
):
    bf16, f32 = jnp.bfloat16, jnp.float32
    rows, slab = rows_ref.shape
    cells = out_ref.shape[0]
    half = slab // 2
    inv = inv_ref[...]
    gain = gain_ref[pl.ds(half_ref[0], 1), :]
    line = lax.broadcasted_iota(jnp.int32, (cells, rows), 1)
    first = jnp.where(line == spot_ref[:, 0:1], 1.0, 0.0).astype(bf16)
    second = jnp.where(line == spot_ref[:, 1:2], 1.0, 0.0).astype(bf16)
    both = jnp.concatenate([first, second], axis=1)
    sent = taken_ref[:, slab:].astype(f32)
    stat = stat_ref[...] + sent[:, 0:1] + sent[:, 1:2]
    factor = inv * inv * inv / (2 * slab) * stat
    for c in range(0, slab, 128):
        cols = slice(c, c + 128)
        total = keep_ref[:, cols].astype(f32) + taken_ref[:, cols].astype(f32)
        value = (gain[:, cols] * total - rows_ref[:, cols].astype(f32) * factor).astype(bf16)
        at = c // half
        grad_ref[at * rows : (at + 1) * rows, c - at * half : c - at * half + 128] = value
    out_ref[...] = dot(both, grad_ref[...]).astype(bf16)


def finish(half, rows, keep, taken, inv, stat, gain, spots):
    bf16 = jnp.bfloat16
    vmem = pl.BlockSpec(memory_space=pltpu.VMEM)
    cells = spots.shape[0]
    count, slab = rows.shape
    return pl.pallas_call(
        finish_kernel,
        out_shape=jax.ShapeDtypeStruct((cells, slab // 2), bf16),
        in_specs=[pl.BlockSpec(memory_space=pltpu.SMEM)] + [vmem] * 7,
        out_specs=vmem,
        scratch_shapes=[pltpu.VMEM((2 * count, slab // 2), bf16)],
        compiler_params=pltpu.CompilerParams(vmem_limit_bytes=16 * 1024 * 1024),
        cost_estimate=pl.CostEstimate(flops=500_000_000, bytes_accessed=4_000_000, transcendentals=0),
    )(half.reshape(1), rows, keep, taken, inv, stat, gain, spots)


def collect_kernel(cell_ref, returned_ref, audio_ref, vision_ref):
    bf16 = jnp.bfloat16
    count = cell_ref.shape[0]
    cells, half = returned_ref.shape
    audio = audio_ref.shape[0]
    line = lax.broadcasted_iota(jnp.int32, (count, cells), 1)
    for h in range(2):
        hot = jnp.where(line == cell_ref[...] + 4 * h, 1.0, 0.0).astype(bf16)
        value = dot(hot, returned_ref[...]).astype(bf16)
        cols = slice(h * half, (h + 1) * half)
        audio_ref[:, cols] = value[:audio]
        vision_ref[:, cols] = value[audio:]


def collect(cell, returned, audio):
    vmem = pl.BlockSpec(memory_space=pltpu.VMEM)
    count = cell.shape[0]
    width = 2 * returned.shape[1]
    return pl.pallas_call(
        collect_kernel,
        out_shape=(
            jax.ShapeDtypeStruct((audio, width), jnp.bfloat16),
            jax.ShapeDtypeStruct((count - audio, width), jnp.bfloat16),
        ),
        in_specs=[vmem] * 2,
        out_specs=(vmem,) * 2,
        compiler_params=pltpu.CompilerParams(vmem_limit_bytes=12 * 1024 * 1024),
        cost_estimate=pl.CostEstimate(flops=400_000_000, bytes_accessed=2_000_000, transcendentals=0),
    )(cell, returned)


def swap(x):
    return lax.ppermute(x, "tp", [(0, 1), (1, 0)])


def shift(x, axis, k):
    return lax.ppermute(x, axis, [(i, (i + k) % 4) for i in range(4)])


def ranks(dest):
    count = dest.shape[1]
    same = dest[:, :, None] == dest[:, None, :]
    earlier = jnp.arange(count)[None, :] < jnp.arange(count)[:, None]
    return jnp.sum((same & earlier[None]).astype(jnp.int32), axis=2)


def local(
    audio_rows,
    vision_rows,
    audio_weight,
    vision_weight,
    text_rows,
    row_target,
    segment_ids,
    norm_gain,
    qkv_weight,
    attn_grad,
):
    bf16, f32 = jnp.bfloat16, jnp.float32
    t = lax.axis_index("tp")
    e = lax.axis_index("enc")
    j = lax.axis_index(("z", "y"))
    n_enc = 4
    n_seq = 16
    self_index = e * n_seq + j
    senders, enc_rows = row_target.shape
    length, slab = text_rows.shape
    audio_count, audio_width = audio_rows.shape
    vision_count = vision_rows.shape[0]
    merge = vision_weight.shape[1]
    cap = 4
    wide = slab // 128 // n_enc * 128

    piece_a, piece_b, packed = pack(
        jnp.stack([e, t]),
        audio_weight,
        vision_weight,
        audio_rows,
        vision_rows,
    )
    z, y = lax.axis_index("z"), lax.axis_index("y")
    hops = (1, 3, 2)
    back = jnp.array((0,) + hops, jnp.int32)
    b_at = (((y - back) % 4)[:, None] + ((z - back) % 4)[None, :] * 4).reshape(-1)
    ah, vh = audio_count // 2, vision_count // 2

    line = row_target.reshape(n_enc, n_seq, enc_rows)[:, j]
    line_dest = line // length
    line_slot = line_dest * (n_enc * cap) + jnp.arange(n_enc)[:, None] * cap + ranks(line_dest)
    a_slot = line_slot[:, :audio_count].reshape(2, 2, 2, ah)
    v_slot = line_slot[:, audio_count:].reshape(2, 2, 2, vh)
    halves = jnp.stack([t, 1 - t])
    a_slot = jnp.moveaxis(a_slot, 2, 1)[:, halves].reshape(2, -1)
    v_slot = jnp.moveaxis(v_slot, 2, 1)[:, halves].reshape(2, -1)
    row_slot = jnp.concatenate([a_slot, v_slot], axis=1)
    cells = row_slot // 16 * 8 + row_slot % 8

    dest = row_target // length
    mine = (dest == self_index).astype(jnp.int32)
    rank_all = jnp.cumsum(mine, axis=1) - 1
    hot = (rank_all[:, :, None] == jnp.arange(cap)[None, None, :]) & (mine[:, :, None] == 1)
    incoming = jnp.sum(jnp.where(hot, (row_target % length)[:, :, None] + 1, 0), axis=1) - 1
    by_line = incoming.reshape(2, 2, n_seq, cap).transpose(0, 2, 1, 3).reshape(2, -1)
    filled = jnp.max(
        (jnp.arange(length)[:, None] == incoming.reshape(1, -1)).astype(jnp.float32), axis=1, keepdims=True
    )
    half = slab // 2
    nowhere = jnp.full_like(incoming, -1)
    spots = jnp.stack(
        [
            jnp.stack([incoming, nowhere], axis=1).reshape(-1),
            jnp.stack([nowhere, incoming], axis=1).reshape(-1),
        ],
        axis=1,
    )
    own_target = lax.dynamic_index_in_dim(row_target, self_index, 0, keepdims=True)
    own_dest = own_target // length
    own_cell = (own_dest * (2 * cap) + ranks(own_dest)).reshape(-1, 1)
    gain = norm_gain.reshape(2, slab)
    seg_row = segment_ids
    seg_col = segment_ids.reshape(length, 1)

    def gather(x, axis):
        return lax.all_to_all(
            jnp.broadcast_to(x[None], (4,) + x.shape), axis, split_axis=0, concat_axis=0, tiled=True
        )

    along_z = [piece_b] + [shift(piece_b, "z", k) for k in hops]
    along_y = gather(piece_a, "y")
    along_y, along_z, cells, by_line, filled, spots, own_cell, gain, seg_col, b_at = (
        lax.optimization_barrier(
            (along_y, along_z, cells, by_line, filled, spots, own_cell, gain, seg_col, b_at)
        )
    )
    along_y, stack_b = lax.optimization_barrier((along_y, jnp.stack(along_z)))
    shards_b = [stack_b] + [shift(stack_b, "y", k) for k in hops]
    shards_a = gather(along_y.reshape(4 * A_PIECE, 384), "z").reshape(n_seq, A_PIECE, 384)
    own = lax.all_gather(packed, "enc", axis=0, tiled=False)
    shards_a, shards_b, own = lax.optimization_barrier((shards_a, shards_b, own))
    other = swap(own)
    outgoing = encode(b_at, shards_a, shards_b, own, other, cells, senders * 8)
    arrived = lax.all_to_all(
        outgoing.reshape(senders, 8, slab // 2), SPREAD, split_axis=0, concat_axis=0, tiled=True
    )
    row_slab = place(by_line, arrived.reshape(senders * 8, slab // 2), text_rows, filled)

    other_slab = swap(row_slab)
    give, keep, inv_rms, row_part = attend(
        t, row_slab, other_slab, gain, qkv_weight, attn_grad, seg_row, seg_col
    )
    taken = swap(give)

    out8 = finish(t, row_slab, keep, taken, inv_rms, row_part, gain, spots)
    returned = lax.all_to_all(
        out8.reshape(senders, 2 * cap, half), SPREAD, split_axis=0, concat_axis=0, tiled=True
    )
    return collect(own_cell, returned.reshape(senders * 2 * cap, half), audio_count)


SPREAD = ("enc", "z", "y")


def solution(mesh):
    torus = Mesh(mesh.devices.reshape(4, 4, 4, 2), ("enc", "z", "y", "tp"))
    in_specs = (
        P(SPREAD, None),
        P(SPREAD, None),
        P(("z", "y"), "tp"),
        P(("z", "y"), None, "tp"),
        P(SPREAD, "tp"),
        P(),
        P(SPREAD, None),
        P(),
        P(None, "tp"),
        P(SPREAD, "tp"),
    )
    out_specs = (P(SPREAD, "tp"), P(SPREAD, "tp"))
    return jax.shard_map(local, mesh=torus, in_specs=in_specs, out_specs=out_specs, check_vma=False)
```

```python
import jax
import jax.numpy as jnp
from jax import lax
from jax.experimental import pallas as pl
from jax.experimental.pallas import tpu as pltpu
from jax.sharding import Mesh
from jax.sharding import PartitionSpec as P

HEAD_DIM = 128

epsilon = 1e-06


NT = (((1,), (1,)), ((), ()))
NN = (((1,), (0,)), ((), ()))
TAIL = 128
BIG = 26 * 1024 * 1024


def in_hbm(x):
    return pltpu.with_memory_space_constraint(x, pltpu.HBM)


def dot(x, y, dims=NN):
    return lax.dot_general(x, y, dims, preferred_element_type=jnp.float32)


def attend_kernel(
    half_ref,
    own_ref,
    other_ref,
    gain_ref,
    weight_ref,
    upstream_hbm,
    seg_row_ref,
    seg_col_ref,
    give_ref,
    keep_ref,
    inv_ref,
    stat_ref,
    normed_ref,
    unscaled_ref,
    scaled_ref,
    sgrad_ref,
    bias_ref,
    held_ref,
    upstream_ref,
    sems,
):
    bf16, f32 = jnp.bfloat16, jnp.float32
    rows, slab = own_ref.shape
    group = weight_ref.shape[1]
    heads = group // HEAD_DIM - 2
    chunks = [(at, min(512, group - at)) for at in range(0, group, 512)]
    pieces = len(chunks)
    copies = [
        pltpu.make_async_copy(
            weight_ref.at[:, at : at + size], held_ref.at[:, at : at + size], sems.at[n]
        )
        for n, (at, size) in enumerate(chunks)
    ]
    last = pltpu.make_async_copy(upstream_hbm, upstream_ref, sems.at[pieces])
    for copy in copies + [last]:
        copy.start()
    place_u = lax.broadcasted_iota(jnp.int32, (rows, rows), 0)
    place_t = lax.broadcasted_iota(jnp.int32, (rows, rows), 1)
    allowed = (seg_col_ref[...] == seg_row_ref[...]) & (place_u <= place_t)
    bias_ref[...] = jnp.where(allowed, 0.0, -1e30)

    t = half_ref[0]
    own_at = pl.multiple_of(t * slab, HEAD_DIM)
    other_at = pl.multiple_of((1 - t) * slab, HEAD_DIM)
    score_scale = HEAD_DIM ** (-0.5)

    squares = jnp.zeros((rows, HEAD_DIM), f32)
    for part, ref in ((t, own_ref), (1 - t, other_ref)):
        gain = gain_ref[pl.ds(part, 1), :]
        for c in range(0, slab, HEAD_DIM):
            x = ref[:, c : c + HEAD_DIM].astype(f32)
            squares = squares + x * x
            at = pl.multiple_of(part * slab + c, HEAD_DIM)
            normed_ref[:, pl.ds(at, HEAD_DIM)] = (x * gain[:, c : c + HEAD_DIM]).astype(bf16)
    inv = lax.rsqrt(jnp.sum(squares, axis=1, keepdims=True) / (2 * slab) + epsilon)
    inv_ref[...] = inv

    for n, (at, size) in enumerate(chunks):
        copies[n].wait()
        value = dot(normed_ref[...], held_ref[:, at : at + size])
        unscaled_ref[:, at : at + size] = value
        scaled_ref[:, at : at + size] = (value * inv).astype(bf16)

    last.wait()
    key = scaled_ref[:, heads * HEAD_DIM : (heads + 1) * HEAD_DIM]
    val = scaled_ref[:, (heads + 1) * HEAD_DIM :]
    grad_key = jnp.zeros((rows, HEAD_DIM), f32)
    grad_val = jnp.zeros((rows, HEAD_DIM), f32)
    stat = jnp.zeros((rows, HEAD_DIM), f32)
    for h in range(heads):
        cols = slice(h * HEAD_DIM, (h + 1) * HEAD_DIM)
        query = scaled_ref[:, cols]
        up = upstream_ref[:, cols]
        scores = dot(key, query, NT) * score_scale + bias_ref[...]
        scores = jnp.exp(scores - jnp.max(scores, axis=0, keepdims=True))
        probs = scores * (1.0 / jnp.sum(scores, axis=0, keepdims=True))
        dprobs = dot(val, up, NT)
        delta = jnp.sum(probs * dprobs, axis=0, keepdims=True)
        sgrad = (probs * (dprobs - delta) * score_scale).astype(bf16)
        grad_val = grad_val + dot(probs.astype(bf16), up)
        grad_key = grad_key + dot(sgrad, query)
        grad_query = dot(sgrad.T, key)
        stat = stat + grad_query * unscaled_ref[:, cols]
        sgrad_ref[:, cols] = (grad_query * inv).astype(bf16)
    cols = slice(heads * HEAD_DIM, (heads + 1) * HEAD_DIM)
    stat = stat + grad_key * unscaled_ref[:, cols]
    sgrad_ref[:, cols] = (grad_key * inv).astype(bf16)
    cols = slice((heads + 1) * HEAD_DIM, (heads + 2) * HEAD_DIM)
    stat = stat + grad_val * unscaled_ref[:, cols]
    sgrad_ref[:, cols] = (grad_val * inv).astype(bf16)
    total = jnp.sum(stat, axis=1, keepdims=True)
    stat_ref[...] = total
    lane = lax.broadcasted_iota(jnp.int32, (rows, TAIL), 1)
    high = total.astype(bf16)
    low = (total - high.astype(f32)).astype(bf16)
    give_ref[:, slab:] = jnp.where(lane == 0, high.astype(f32), low.astype(f32)).astype(bf16)

    keep_ref[...] = dot(sgrad_ref[...], held_ref[pl.ds(own_at, slab), :], NT).astype(bf16)
    give_ref[:, :slab] = dot(sgrad_ref[...], held_ref[pl.ds(other_at, slab), :], NT).astype(bf16)


def attend(half, own, other, gain, qkv_weight, upstream, seg_row, seg_col):
    rows, slab = own.shape
    group = qkv_weight.shape[1]
    f32, bf16 = jnp.float32, jnp.bfloat16
    vmem = pl.BlockSpec(memory_space=pltpu.VMEM)
    anywhere = pl.BlockSpec(memory_space=pl.ANY)
    return pl.pallas_call(
        attend_kernel,
        out_shape=(
            jax.ShapeDtypeStruct((rows, slab + TAIL), bf16),
            jax.ShapeDtypeStruct((rows, slab), bf16),
            jax.ShapeDtypeStruct((rows, 1), f32),
            jax.ShapeDtypeStruct((rows, 1), f32),
        ),
        in_specs=[pl.BlockSpec(memory_space=pltpu.SMEM), vmem, vmem, vmem]
        + [anywhere, anywhere, vmem, vmem],
        out_specs=(vmem,) * 4,
        scratch_shapes=[
            pltpu.VMEM((rows, 2 * slab), bf16),
            pltpu.VMEM((rows, group), f32),
            pltpu.VMEM((rows, group), bf16),
            pltpu.VMEM((rows, group), bf16),
            pltpu.VMEM((rows, rows), f32),
            pltpu.VMEM((2 * slab, group), bf16),
            pltpu.VMEM(upstream.shape, bf16),
            pltpu.SemaphoreType.DMA((4,)),
        ],
        compiler_params=pltpu.CompilerParams(vmem_limit_bytes=BIG),
        cost_estimate=pl.CostEstimate(flops=5_000_000_000, bytes_accessed=14_000_000, transcendentals=500_000),
    )(
        half.reshape(1),
        own,
        other,
        gain,
        in_hbm(qkv_weight),
        in_hbm(upstream),
        seg_row,
        seg_col,
    )


def roll_half(x):
    return pltpu.roll(x.astype(jnp.float32), 64, 1).astype(x.dtype)


A_ROWS, A_TAIL = 192, 32
B_ROWS, B_TAIL = 208, 48
A_PIECE = A_ROWS + A_TAIL
B_PIECE = B_ROWS + B_TAIL


def pack_kernel(
    place_ref,
    audio_w_ref,
    vision_w_ref,
    audio_ref,
    vision_ref,
    a_ref,
    b_ref,
    rows_ref,
    am_ref,
    at_ref,
    vm_ref,
    vt_ref,
    sems,
    row_sems,
):
    e = place_ref[0]
    t = place_ref[1]
    main_at = pl.multiple_of(e * 384, 128)
    tail_at = pl.multiple_of(1536 + e // 2 * 128, 128)
    loads = [
        pltpu.make_async_copy(vision_w_ref.at[:, :, pl.ds(main_at, 384)], vm_ref, sems.at[0]),
        pltpu.make_async_copy(vision_w_ref.at[:, :, pl.ds(tail_at, 128)], vt_ref, sems.at[1]),
        pltpu.make_async_copy(audio_w_ref.at[:, pl.ds(main_at, 384)], am_ref, sems.at[2]),
        pltpu.make_async_copy(audio_w_ref.at[:, pl.ds(tail_at, 128)], at_ref, sems.at[3]),
    ]
    for copy in loads:
        copy.start()
    width = rows_ref.shape[1]
    ah, vh = audio_ref.shape[0] // 2, vision_ref.shape[0] // 2
    copies = [
        pltpu.make_async_copy(
            audio_ref.at[pl.ds(pl.multiple_of(t * ah, 16), ah), :], rows_ref.at[:ah], row_sems.at[0]
        )
    ] + [
        pltpu.make_async_copy(
            vision_ref.at[pl.ds(pl.multiple_of(t * vh, 16), vh), i * width : (i + 1) * width],
            rows_ref.at[ah + i * vh : ah + (i + 1) * vh],
            row_sems.at[1 + i],
        )
        for i in range(4)
    ]
    for copy in copies:
        copy.start()
    for copy in loads:
        copy.wait()
    k = am_ref.shape[0]
    cut = A_ROWS - k
    vision_main = vm_ref[...].reshape(4 * k, 384)
    a_ref[:k, :] = am_ref[...]
    a_ref[k:A_ROWS, :] = vision_main[:cut]
    b_ref[:B_ROWS, :] = vision_main[cut:]
    odd = e % 2 == 1
    vision_tail = vt_ref[...].reshape(4 * k, 128)
    tail = jnp.concatenate([at_ref[...], vision_tail], axis=0).astype(jnp.float32)
    moved = pltpu.roll(tail, 64, 1)
    first = jnp.where(odd, moved, tail)
    second = jnp.where(odd, tail, moved)
    lane = lax.broadcasted_iota(jnp.int32, (B_TAIL, 128), 1)
    for q in range(3):
        cols = slice(q * 128, (q + 1) * 128)
        low = first[q * A_TAIL : (q + 1) * A_TAIL]
        high = second[96 + q * A_TAIL : 96 + (q + 1) * A_TAIL]
        a_ref[A_ROWS:, cols] = jnp.where(lane[:A_TAIL] < 64, low, high).astype(a_ref.dtype)
    base = A_ROWS
    for q in range(2):
        cols = slice(q * 128, (q + 1) * 128)
        low = first[base + q * B_TAIL : base + (q + 1) * B_TAIL]
        high = second[base + 112 + q * B_TAIL : base + 112 + (q + 1) * B_TAIL]
        b_ref[B_ROWS:, cols] = jnp.where(lane < 64, low, high).astype(b_ref.dtype)
    b_ref[B_ROWS : B_ROWS + 16, 256:] = first[base + 96 : base + 112].astype(b_ref.dtype)
    b_ref[B_ROWS + 16 :, 256:] = jnp.zeros((B_TAIL - 16, 128), b_ref.dtype)
    for copy in copies:
        copy.wait()


def pack(where, audio_weight, vision_weight, audio_rows, vision_rows):
    bf16 = jnp.bfloat16
    vmem = pl.BlockSpec(memory_space=pltpu.VMEM)
    anywhere = pl.BlockSpec(memory_space=pl.ANY)
    k = audio_weight.shape[0]
    return pl.pallas_call(
        pack_kernel,
        out_shape=(
            jax.ShapeDtypeStruct((A_PIECE, 384), bf16),
            jax.ShapeDtypeStruct((B_PIECE, 384), bf16),
            jax.ShapeDtypeStruct(
                (audio_rows.shape[0] // 2 + 2 * vision_rows.shape[0], audio_rows.shape[1]), bf16
            ),
        ),
        in_specs=[pl.BlockSpec(memory_space=pltpu.SMEM)] + [anywhere] * 4,
        out_specs=(vmem, vmem, vmem),
        scratch_shapes=[
            pltpu.VMEM((k, 384), bf16),
            pltpu.VMEM((k, 128), bf16),
            pltpu.VMEM((k, 4, 384), bf16),
            pltpu.VMEM((k, 4, 128), bf16),
            pltpu.SemaphoreType.DMA((4,)),
            pltpu.SemaphoreType.DMA((5,)),
        ],
        compiler_params=pltpu.CompilerParams(vmem_limit_bytes=BIG),
        cost_estimate=pl.CostEstimate(flops=0, bytes_accessed=1_800_000, transcendentals=0),
    )(where, in_hbm(audio_weight), in_hbm(vision_weight), in_hbm(audio_rows), in_hbm(vision_rows))


def encode_kernel(
    a_at_ref,
    b_at_ref,
    ga0,
    ga1,
    ga2,
    ga3,
    ga4,
    gb0,
    gb1,
    gb2,
    gb3,
    gb4,
    own_ref,
    other_ref,
    cell_ref,
    out_ref,
    wa_ref,
    wv_ref,
    ta_ref,
    tv_ref,
    ra_ref,
    rb_ref,
    x_ref,
    enc_ref,
    sems,
):
    bf16, f32 = jnp.bfloat16, jnp.float32
    audio_width = x_ref.shape[3]
    audio_k = wa_ref.shape[1]
    cut = A_ROWS - audio_k
    sources = ((ga0, gb0, 0, 4), (ga1, gb1, 4, 4), (ga2, gb2, 8, 4), (ga3, gb3, 12, 2), (ga4, gb4, 14, 2))
    for ga, gb, start, size in sources:
        pltpu.make_async_copy(
            ga.at[:, A_ROWS:, :], ra_ref.at[start : start + size], sems.at[2]
        ).start()
        pltpu.make_async_copy(
            gb.at[:, B_ROWS:, :], rb_ref.at[start : start + size], sems.at[3]
        ).start()
    pltpu.make_async_copy(own_ref, x_ref.at[0], sems.at[0]).start()
    pltpu.make_async_copy(other_ref, x_ref.at[1], sems.at[1]).start()
    for ga, _, start, size in sources:
        for n in range(size):
            pltpu.make_async_copy(
                ga.at[n, :audio_k, :], wa_ref.at[a_at_ref[start + n]], sems.at[4]
            ).start()
    for ga, gb, start, size in sources:
        for n in range(size):
            pltpu.make_async_copy(
                ga.at[n, audio_k:A_ROWS, :], wv_ref.at[a_at_ref[start + n], :cut, :], sems.at[5]
            ).start()
            pltpu.make_async_copy(
                gb.at[n, :B_ROWS, :], wv_ref.at[b_at_ref[start + n], cut:, :], sems.at[6]
            ).start()

    count = cell_ref.shape[1]
    cells = out_ref.shape[0]
    line = lax.broadcasted_iota(jnp.int32, (cells, count), 0)
    first = jnp.where(line == cell_ref[0:1, :], 1.0, 0.0).astype(bf16)
    second = jnp.where(line == cell_ref[1:2, :], 1.0, 0.0).astype(bf16)

    pltpu.make_async_copy(ra_ref, ra_ref, sems.at[2]).wait()

    @pl.loop(0, 16)
    def _(p):
        ta = jnp.concatenate([ra_ref[p, :, q * 128 : (q + 1) * 128] for q in range(3)], axis=0)
        at = a_at_ref[p]
        ta_ref[at, :, :] = ta[:audio_k]
        tv_ref[at, : 96 - audio_k, :] = ta[audio_k:]
        tv_ref[at, 96 - audio_k : cut, :] = roll_half(ta)

    pltpu.make_async_copy(rb_ref, rb_ref, sems.at[3]).wait()

    @pl.loop(0, 16)
    def _(p):
        at = b_at_ref[p]
        tb = jnp.concatenate([rb_ref[p, :, q * 128 : (q + 1) * 128] for q in range(2)], axis=0)
        tv_ref[at, cut : cut + 96, :] = tb
        tv_ref[at, cut + 96 : cut + 112, :] = rb_ref[p, :16, 256:]
        tv_ref[at, cut + 112 :, :] = roll_half(tb)

    halves, n_enc = x_ref.shape[:2]
    audio = 64
    vision = 32
    n_audio = halves * n_enc * audio
    n_vision = halves * n_enc * vision

    def weights(main, last):
        size = main.shape[0] * main.shape[1]
        return jnp.concatenate([main.reshape(size, 384), last.reshape(size, 128)], axis=1)

    def keep_rows(value, base, each):
        run = 2 * each
        for h in range(2):
            for g in range(2):
                at = g * count + base + h * run
                enc_ref[at : at + run, :] = value[(2 * h + g) * run : (2 * h + g + 1) * run]

    pltpu.make_async_copy(own_ref, x_ref.at[0], sems.at[0]).wait()
    pltpu.make_async_copy(other_ref, x_ref.at[1], sems.at[1]).wait()
    pltpu.make_async_copy(wa_ref, wa_ref, sems.at[4]).wait()
    rows = x_ref[:, :, :audio, :].reshape(n_audio, audio_width)
    keep_rows(dot(rows, weights(wa_ref[...], ta_ref[...])).astype(bf16), 0, audio)
    pltpu.make_async_copy(wv_ref.at[:, :cut, :], wv_ref.at[:, :cut, :], sems.at[5]).wait()
    pltpu.make_async_copy(wv_ref.at[:, cut:, :], wv_ref.at[:, cut:, :], sems.at[6]).wait()
    total = jnp.zeros((n_vision, 512), f32)
    for i in range(4):
        rows = x_ref[:, :, audio + i * vision : audio + (i + 1) * vision, :]
        part = weights(wv_ref[4 * i : 4 * i + 4], tv_ref[4 * i : 4 * i + 4])
        total = total + dot(rows.reshape(n_vision, audio_width), part)
    keep_rows(total.astype(bf16), 4 * audio, vision)

    out_ref[:, :384] = dot(first, enc_ref[:count, :384]).astype(bf16)
    out_ref[:, 384:768] = dot(second, enc_ref[count:, :384]).astype(bf16)
    low = dot(first, enc_ref[:count, 384:])
    high = dot(second, enc_ref[count:, 384:])
    lane = lax.broadcasted_iota(jnp.int32, low.shape, 1)
    out_ref[:, 768:] = jnp.where(lane < 64, low, pltpu.roll(high, 64, 1)).astype(bf16)


def encode(a_at, b_at, shards_a, shards_b, own, other, cells, n_cells):
    bf16 = jnp.bfloat16
    n_enc, rows, width = own.shape
    smem = pl.BlockSpec(memory_space=pltpu.SMEM)
    vmem = pl.BlockSpec(memory_space=pltpu.VMEM)
    anywhere = pl.BlockSpec(memory_space=pl.ANY)
    k = width // 16
    return pl.pallas_call(
        encode_kernel,
        out_shape=jax.ShapeDtypeStruct((n_cells, 896), bf16),
        in_specs=[smem, smem] + [anywhere] * 12 + [vmem],
        out_specs=vmem,
        scratch_shapes=[
            pltpu.VMEM((16, k, 384), bf16),
            pltpu.VMEM((16, 4 * k, 384), bf16),
            pltpu.VMEM((16, k, 128), bf16),
            pltpu.VMEM((16, 4 * k, 128), bf16),
            pltpu.VMEM((16, A_TAIL, 384), bf16),
            pltpu.VMEM((16, B_TAIL, 384), bf16),
            pltpu.VMEM((2, n_enc, rows, width), bf16),
            pltpu.VMEM((2 * cells.shape[1], 512), bf16),
            pltpu.SemaphoreType.DMA((7,)),
        ],
        compiler_params=pltpu.CompilerParams(vmem_limit_bytes=BIG),
        cost_estimate=pl.CostEstimate(
            flops=3_000_000_000, bytes_accessed=11_000_000, transcendentals=0
        ),
    )(a_at, b_at, *shards_a, *shards_b, in_hbm(own), other, cells)


def place_kernel(e_row_ref, arrived_ref, text_hbm, filled_ref, out_ref, text_ref, sem):
    bf16, f32 = jnp.bfloat16, jnp.float32
    load = pltpu.make_async_copy(text_hbm, text_ref, sem)
    load.start()
    rows = out_ref.shape[0]
    each = arrived_ref.shape[0] // 4
    line = lax.broadcasted_iota(jnp.int32, (rows, each), 0)
    first = jnp.where(line == e_row_ref[0:1, :], 1.0, 0.0).astype(bf16)
    second = jnp.where(line == e_row_ref[1:2, :], 1.0, 0.0).astype(bf16)
    both = jnp.concatenate([first, second], axis=1)
    taken = filled_ref[...] > 0.5
    lane = lax.broadcasted_iota(jnp.int32, (rows, 128), 1)
    low = []
    high = []
    load.wait()
    for e in range(4):
        at = slice(e * each, (e + 1) * each)
        main = jnp.concatenate([arrived_ref[at, :384], arrived_ref[at, 384:768]], axis=0)
        cols = slice(e * 384, (e + 1) * 384)
        text = text_ref[:, cols].astype(f32)
        out_ref[:, cols] = jnp.where(taken, dot(both, main), text).astype(bf16)
        last = arrived_ref[at, 768:]
        low.append(dot(first, last))
        high.append(dot(second, last))
    for q in range(2):
        left = low[2 * q] + pltpu.roll(high[2 * q], 64, 1)
        right = pltpu.roll(low[2 * q + 1], 64, 1) + high[2 * q + 1]
        cols = slice(1536 + q * 128, 1536 + (q + 1) * 128)
        text = text_ref[:, cols].astype(f32)
        out_ref[:, cols] = jnp.where(taken, jnp.where(lane < 64, left, right), text).astype(bf16)


def place(spots, arrived, text, filled):
    vmem = pl.BlockSpec(memory_space=pltpu.VMEM)
    return pl.pallas_call(
        place_kernel,
        out_shape=jax.ShapeDtypeStruct(text.shape, text.dtype),
        in_specs=[vmem, vmem, pl.BlockSpec(memory_space=pl.ANY), vmem],
        out_specs=vmem,
        scratch_shapes=[pltpu.VMEM(text.shape, text.dtype), pltpu.SemaphoreType.DMA],
        compiler_params=pltpu.CompilerParams(vmem_limit_bytes=12 * 1024 * 1024),
        cost_estimate=pl.CostEstimate(flops=300_000_000, bytes_accessed=3_000_000, transcendentals=0),
    )(spots, arrived, text, filled)


def finish_kernel(
    half_ref,
    rows_ref,
    keep_ref,
    taken_ref,
    inv_ref,
    stat_ref,
    gain_ref,
    spot_ref,
    out_ref,
    grad_ref,
):
    bf16, f32 = jnp.bfloat16, jnp.float32
    rows, slab = rows_ref.shape
    cells = out_ref.shape[0]
    half = slab // 2
    inv = inv_ref[...]
    gain = gain_ref[pl.ds(half_ref[0], 1), :]
    line = lax.broadcasted_iota(jnp.int32, (cells, rows), 1)
    first = jnp.where(line == spot_ref[:, 0:1], 1.0, 0.0).astype(bf16)
    second = jnp.where(line == spot_ref[:, 1:2], 1.0, 0.0).astype(bf16)
    both = jnp.concatenate([first, second], axis=1)
    sent = taken_ref[:, slab:].astype(f32)
    stat = stat_ref[...] + sent[:, 0:1] + sent[:, 1:2]
    factor = inv * inv * inv / (2 * slab) * stat
    for c in range(0, slab, 128):
        cols = slice(c, c + 128)
        total = keep_ref[:, cols].astype(f32) + taken_ref[:, cols].astype(f32)
        value = (gain[:, cols] * total - rows_ref[:, cols].astype(f32) * factor).astype(bf16)
        at = c // half
        grad_ref[at * rows : (at + 1) * rows, c - at * half : c - at * half + 128] = value
    out_ref[...] = dot(both, grad_ref[...]).astype(bf16)


def finish(half, rows, keep, taken, inv, stat, gain, spots):
    bf16 = jnp.bfloat16
    vmem = pl.BlockSpec(memory_space=pltpu.VMEM)
    cells = spots.shape[0]
    count, slab = rows.shape
    return pl.pallas_call(
        finish_kernel,
        out_shape=jax.ShapeDtypeStruct((cells, slab // 2), bf16),
        in_specs=[pl.BlockSpec(memory_space=pltpu.SMEM)] + [vmem] * 7,
        out_specs=vmem,
        scratch_shapes=[pltpu.VMEM((2 * count, slab // 2), bf16)],
        compiler_params=pltpu.CompilerParams(vmem_limit_bytes=16 * 1024 * 1024),
        cost_estimate=pl.CostEstimate(flops=500_000_000, bytes_accessed=4_000_000, transcendentals=0),
    )(half.reshape(1), rows, keep, taken, inv, stat, gain, spots)


def collect_kernel(cell_ref, returned_ref, audio_ref, vision_ref):
    bf16 = jnp.bfloat16
    count = cell_ref.shape[0]
    cells, half = returned_ref.shape
    audio = audio_ref.shape[0]
    line = lax.broadcasted_iota(jnp.int32, (count, cells), 1)
    for h in range(2):
        hot = jnp.where(line == cell_ref[...] + 4 * h, 1.0, 0.0).astype(bf16)
        value = dot(hot, returned_ref[...]).astype(bf16)
        cols = slice(h * half, (h + 1) * half)
        audio_ref[:, cols] = value[:audio]
        vision_ref[:, cols] = value[audio:]


def collect(cell, returned, audio):
    vmem = pl.BlockSpec(memory_space=pltpu.VMEM)
    count = cell.shape[0]
    width = 2 * returned.shape[1]
    return pl.pallas_call(
        collect_kernel,
        out_shape=(
            jax.ShapeDtypeStruct((audio, width), jnp.bfloat16),
            jax.ShapeDtypeStruct((count - audio, width), jnp.bfloat16),
        ),
        in_specs=[vmem] * 2,
        out_specs=(vmem,) * 2,
        compiler_params=pltpu.CompilerParams(vmem_limit_bytes=12 * 1024 * 1024),
        cost_estimate=pl.CostEstimate(flops=400_000_000, bytes_accessed=2_000_000, transcendentals=0),
    )(cell, returned)


def swap(x):
    return lax.ppermute(x, "tp", [(0, 1), (1, 0)])


def shift(x, axis, k):
    return lax.ppermute(x, axis, [(i, (i + k) % 4) for i in range(4)])


def ranks(dest):
    count = dest.shape[1]
    same = dest[:, :, None] == dest[:, None, :]
    earlier = jnp.arange(count)[None, :] < jnp.arange(count)[:, None]
    return jnp.sum((same & earlier[None]).astype(jnp.int32), axis=2)


def local(
    audio_rows,
    vision_rows,
    audio_weight,
    vision_weight,
    text_rows,
    row_target,
    segment_ids,
    norm_gain,
    qkv_weight,
    attn_grad,
):
    bf16, f32 = jnp.bfloat16, jnp.float32
    t = lax.axis_index("tp")
    e = lax.axis_index("enc")
    j = lax.axis_index(("z", "y"))
    n_enc = 4
    n_seq = 16
    self_index = e * n_seq + j
    senders, enc_rows = row_target.shape
    length, slab = text_rows.shape
    audio_count, audio_width = audio_rows.shape
    vision_count = vision_rows.shape[0]
    merge = vision_weight.shape[1]
    cap = 4
    wide = slab // 128 // n_enc * 128

    piece_a, piece_b, packed = pack(
        jnp.stack([e, t]),
        audio_weight,
        vision_weight,
        audio_rows,
        vision_rows,
    )
    z, y = lax.axis_index("z"), lax.axis_index("y")
    hops = (1, 3, 2)
    back = jnp.array((0,) + hops, jnp.int32)
    a_at = (((z - back) % 4)[:, None] * 4 + ((y - back) % 4)[None, :]).reshape(-1)
    b_at = (((y - back) % 4)[:, None] + ((z - back) % 4)[None, :] * 4).reshape(-1)
    ah, vh = audio_count // 2, vision_count // 2

    line = row_target.reshape(n_enc, n_seq, enc_rows)[:, j]
    line_dest = line // length
    line_slot = line_dest * (n_enc * cap) + jnp.arange(n_enc)[:, None] * cap + ranks(line_dest)
    a_slot = line_slot[:, :audio_count].reshape(2, 2, 2, ah)
    v_slot = line_slot[:, audio_count:].reshape(2, 2, 2, vh)
    halves = jnp.stack([t, 1 - t])
    a_slot = jnp.moveaxis(a_slot, 2, 1)[:, halves].reshape(2, -1)
    v_slot = jnp.moveaxis(v_slot, 2, 1)[:, halves].reshape(2, -1)
    row_slot = jnp.concatenate([a_slot, v_slot], axis=1)
    cells = row_slot // 16 * 8 + row_slot % 8

    dest = row_target // length
    mine = (dest == self_index).astype(jnp.int32)
    rank_all = jnp.cumsum(mine, axis=1) - 1
    hot = (rank_all[:, :, None] == jnp.arange(cap)[None, None, :]) & (mine[:, :, None] == 1)
    incoming = jnp.sum(jnp.where(hot, (row_target % length)[:, :, None] + 1, 0), axis=1) - 1
    by_line = incoming.reshape(2, 2, n_seq, cap).transpose(0, 2, 1, 3).reshape(2, -1)
    filled = jnp.max(
        (jnp.arange(length)[:, None] == incoming.reshape(1, -1)).astype(jnp.float32), axis=1, keepdims=True
    )
    half = slab // 2
    nowhere = jnp.full_like(incoming, -1)
    spots = jnp.stack(
        [
            jnp.stack([incoming, nowhere], axis=1).reshape(-1),
            jnp.stack([nowhere, incoming], axis=1).reshape(-1),
        ],
        axis=1,
    )
    own_target = lax.dynamic_index_in_dim(row_target, self_index, 0, keepdims=True)
    own_dest = own_target // length
    own_cell = (own_dest * (2 * cap) + ranks(own_dest)).reshape(-1, 1)
    gain = norm_gain.reshape(2, slab)
    seg_row = segment_ids
    seg_col = segment_ids.reshape(length, 1)
    along_y = [piece_a] + [shift(piece_a, "y", k) for k in hops]
    along_z = [piece_b] + [shift(piece_b, "z", k) for k in hops]
    along_y, along_z, cells, by_line, filled, spots, own_cell, gain, seg_col, a_at, b_at = (
        lax.optimization_barrier(
            (along_y, along_z, cells, by_line, filled, spots, own_cell, gain, seg_col, a_at, b_at)
        )
    )
    stack_a, stack_b = lax.optimization_barrier((jnp.stack(along_y), jnp.stack(along_z)))
    near_a = [shift(stack_a, "z", 1), shift(stack_a, "z", 3)]
    near_b = [shift(stack_b, "y", 1), shift(stack_b, "y", 3)]
    own = lax.all_gather(packed, "enc", axis=0, tiled=False)
    near_a, near_b, own = lax.optimization_barrier((near_a, near_b, own))
    far_a = [shift(near_a[0][:2], "z", 1), shift(near_a[1][2:], "z", 3)]
    far_b = [shift(near_b[0][:2], "y", 1), shift(near_b[1][2:], "y", 3)]
    shards_a = [stack_a] + near_a + far_a
    shards_b = [stack_b] + near_b + far_b
    other = swap(own)
    outgoing = encode(a_at, b_at, shards_a, shards_b, own, other, cells, senders * 8)
    arrived = lax.all_to_all(
        outgoing.reshape(senders, 8, slab // 2), SPREAD, split_axis=0, concat_axis=0, tiled=True
    )
    row_slab = place(by_line, arrived.reshape(senders * 8, slab // 2), text_rows, filled)

    other_slab = swap(row_slab)
    give, keep, inv_rms, row_part = attend(
        t, row_slab, other_slab, gain, qkv_weight, attn_grad, seg_row, seg_col
    )
    taken = swap(give)

    out8 = finish(t, row_slab, keep, taken, inv_rms, row_part, gain, spots)
    returned = lax.all_to_all(
        out8.reshape(senders, 2 * cap, half), SPREAD, split_axis=0, concat_axis=0, tiled=True
    )
    return collect(own_cell, returned.reshape(senders * 2 * cap, half), audio_count)


SPREAD = ("enc", "z", "y")


def solution(mesh):
    torus = Mesh(mesh.devices.reshape(4, 4, 4, 2), ("enc", "z", "y", "tp"))
    in_specs = (
        P(SPREAD, None),
        P(SPREAD, None),
        P(("z", "y"), "tp"),
        P(("z", "y"), None, "tp"),
        P(SPREAD, "tp"),
        P(),
        P(SPREAD, None),
        P(),
        P(None, "tp"),
        P(SPREAD, "tp"),
    )
    out_specs = (P(SPREAD, "tp"), P(SPREAD, "tp"))
    return jax.shard_map(local, mesh=torus, in_specs=in_specs, out_specs=out_specs, check_vma=False)
```

```python
import jax
import jax.numpy as jnp
from jax import lax
from jax.experimental import pallas as pl
from jax.experimental.pallas import tpu as pltpu
from jax.sharding import Mesh
from jax.sharding import PartitionSpec as P

HEAD_DIM = 128

epsilon = 1e-06


NT = (((1,), (1,)), ((), ()))
NN = (((1,), (0,)), ((), ()))
TAIL = 128
BIG = 26 * 1024 * 1024


def in_hbm(x):
    return pltpu.with_memory_space_constraint(x, pltpu.HBM)


def dot(x, y, dims=NN):
    return lax.dot_general(x, y, dims, preferred_element_type=jnp.float32)


def attend_kernel(
    half_ref,
    own_ref,
    other_ref,
    gain_ref,
    weight_ref,
    upstream_hbm,
    seg_row_ref,
    seg_col_ref,
    give_ref,
    keep_ref,
    inv_ref,
    stat_ref,
    normed_ref,
    unscaled_ref,
    scaled_ref,
    sgrad_ref,
    bias_ref,
    held_ref,
    upstream_ref,
    sems,
):
    bf16, f32 = jnp.bfloat16, jnp.float32
    rows, slab = own_ref.shape
    group = weight_ref.shape[1]
    heads = group // HEAD_DIM - 2
    chunks = [(at, min(512, group - at)) for at in range(0, group, 512)]
    pieces = len(chunks)
    copies = [
        pltpu.make_async_copy(
            weight_ref.at[:, at : at + size], held_ref.at[:, at : at + size], sems.at[n]
        )
        for n, (at, size) in enumerate(chunks)
    ]
    last = pltpu.make_async_copy(upstream_hbm, upstream_ref, sems.at[pieces])
    for copy in copies + [last]:
        copy.start()
    place_u = lax.broadcasted_iota(jnp.int32, (rows, rows), 0)
    place_t = lax.broadcasted_iota(jnp.int32, (rows, rows), 1)
    allowed = (seg_col_ref[...] == seg_row_ref[...]) & (place_u <= place_t)
    bias_ref[...] = jnp.where(allowed, 0.0, -1e30)

    t = half_ref[0]
    own_at = pl.multiple_of(t * slab, HEAD_DIM)
    other_at = pl.multiple_of((1 - t) * slab, HEAD_DIM)
    score_scale = HEAD_DIM ** (-0.5)

    squares = jnp.zeros((rows, HEAD_DIM), f32)
    for part, ref in ((t, own_ref), (1 - t, other_ref)):
        gain = gain_ref[pl.ds(part, 1), :]
        for c in range(0, slab, HEAD_DIM):
            x = ref[:, c : c + HEAD_DIM].astype(f32)
            squares = squares + x * x
            at = pl.multiple_of(part * slab + c, HEAD_DIM)
            normed_ref[:, pl.ds(at, HEAD_DIM)] = (x * gain[:, c : c + HEAD_DIM]).astype(bf16)
    inv = lax.rsqrt(jnp.sum(squares, axis=1, keepdims=True) / (2 * slab) + epsilon)
    inv_ref[...] = inv

    for n, (at, size) in enumerate(chunks):
        copies[n].wait()
        value = dot(normed_ref[...], held_ref[:, at : at + size])
        unscaled_ref[:, at : at + size] = value
        scaled_ref[:, at : at + size] = (value * inv).astype(bf16)

    last.wait()
    key = scaled_ref[:, heads * HEAD_DIM : (heads + 1) * HEAD_DIM]
    val = scaled_ref[:, (heads + 1) * HEAD_DIM :]
    grad_key = jnp.zeros((rows, HEAD_DIM), f32)
    grad_val = jnp.zeros((rows, HEAD_DIM), f32)
    stat = jnp.zeros((rows, HEAD_DIM), f32)
    for h in range(heads):
        cols = slice(h * HEAD_DIM, (h + 1) * HEAD_DIM)
        query = scaled_ref[:, cols]
        up = upstream_ref[:, cols]
        scores = dot(key, query, NT) * score_scale + bias_ref[...]
        scores = jnp.exp(scores - jnp.max(scores, axis=0, keepdims=True))
        probs = scores * (1.0 / jnp.sum(scores, axis=0, keepdims=True))
        dprobs = dot(val, up, NT)
        delta = jnp.sum(probs * dprobs, axis=0, keepdims=True)
        sgrad = (probs * (dprobs - delta) * score_scale).astype(bf16)
        grad_val = grad_val + dot(probs.astype(bf16), up)
        grad_key = grad_key + dot(sgrad, query)
        grad_query = dot(sgrad.T, key)
        stat = stat + grad_query * unscaled_ref[:, cols]
        sgrad_ref[:, cols] = (grad_query * inv).astype(bf16)
    cols = slice(heads * HEAD_DIM, (heads + 1) * HEAD_DIM)
    stat = stat + grad_key * unscaled_ref[:, cols]
    sgrad_ref[:, cols] = (grad_key * inv).astype(bf16)
    cols = slice((heads + 1) * HEAD_DIM, (heads + 2) * HEAD_DIM)
    stat = stat + grad_val * unscaled_ref[:, cols]
    sgrad_ref[:, cols] = (grad_val * inv).astype(bf16)
    total = jnp.sum(stat, axis=1, keepdims=True)
    stat_ref[...] = total
    lane = lax.broadcasted_iota(jnp.int32, (rows, TAIL), 1)
    high = total.astype(bf16)
    low = (total - high.astype(f32)).astype(bf16)
    give_ref[:, slab:] = jnp.where(lane == 0, high.astype(f32), low.astype(f32)).astype(bf16)

    keep_ref[...] = dot(sgrad_ref[...], held_ref[pl.ds(own_at, slab), :], NT).astype(bf16)
    give_ref[:, :slab] = dot(sgrad_ref[...], held_ref[pl.ds(other_at, slab), :], NT).astype(bf16)


def attend(half, own, other, gain, qkv_weight, upstream, seg_row, seg_col):
    rows, slab = own.shape
    group = qkv_weight.shape[1]
    f32, bf16 = jnp.float32, jnp.bfloat16
    vmem = pl.BlockSpec(memory_space=pltpu.VMEM)
    anywhere = pl.BlockSpec(memory_space=pl.ANY)
    return pl.pallas_call(
        attend_kernel,
        out_shape=(
            jax.ShapeDtypeStruct((rows, slab + TAIL), bf16),
            jax.ShapeDtypeStruct((rows, slab), bf16),
            jax.ShapeDtypeStruct((rows, 1), f32),
            jax.ShapeDtypeStruct((rows, 1), f32),
        ),
        in_specs=[pl.BlockSpec(memory_space=pltpu.SMEM), vmem, vmem, vmem]
        + [anywhere, anywhere, vmem, vmem],
        out_specs=(vmem,) * 4,
        scratch_shapes=[
            pltpu.VMEM((rows, 2 * slab), bf16),
            pltpu.VMEM((rows, group), f32),
            pltpu.VMEM((rows, group), bf16),
            pltpu.VMEM((rows, group), bf16),
            pltpu.VMEM((rows, rows), f32),
            pltpu.VMEM((2 * slab, group), bf16),
            pltpu.VMEM(upstream.shape, bf16),
            pltpu.SemaphoreType.DMA((4,)),
        ],
        compiler_params=pltpu.CompilerParams(vmem_limit_bytes=BIG),
        cost_estimate=pl.CostEstimate(flops=5_000_000_000, bytes_accessed=14_000_000, transcendentals=500_000),
    )(
        half.reshape(1),
        own,
        other,
        gain,
        in_hbm(qkv_weight),
        in_hbm(upstream),
        seg_row,
        seg_col,
    )


def roll_half(x):
    return pltpu.roll(x.astype(jnp.float32), 64, 1).astype(x.dtype)


A_ROWS, A_TAIL = 192, 32
B_ROWS, B_TAIL = 208, 48
A_PIECE = A_ROWS + A_TAIL
B_PIECE = B_ROWS + B_TAIL


def pack_kernel(
    place_ref,
    audio_w_ref,
    vision_w_ref,
    audio_ref,
    vision_ref,
    a_ref,
    b_ref,
    rows_ref,
    am_ref,
    at_ref,
    vm_ref,
    vt_ref,
    sems,
    row_sems,
):
    e = place_ref[0]
    t = place_ref[1]
    main_at = pl.multiple_of(e * 384, 128)
    tail_at = pl.multiple_of(1536 + e // 2 * 128, 128)
    loads = [
        pltpu.make_async_copy(vision_w_ref.at[:, :, pl.ds(main_at, 384)], vm_ref, sems.at[0]),
        pltpu.make_async_copy(vision_w_ref.at[:, :, pl.ds(tail_at, 128)], vt_ref, sems.at[1]),
        pltpu.make_async_copy(audio_w_ref.at[:, pl.ds(main_at, 384)], am_ref, sems.at[2]),
        pltpu.make_async_copy(audio_w_ref.at[:, pl.ds(tail_at, 128)], at_ref, sems.at[3]),
    ]
    for copy in loads:
        copy.start()
    width = rows_ref.shape[1]
    ah, vh = audio_ref.shape[0] // 2, vision_ref.shape[0] // 2
    copies = [
        pltpu.make_async_copy(
            audio_ref.at[pl.ds(pl.multiple_of(t * ah, 16), ah), :], rows_ref.at[:ah], row_sems.at[0]
        )
    ] + [
        pltpu.make_async_copy(
            vision_ref.at[pl.ds(pl.multiple_of(t * vh, 16), vh), i * width : (i + 1) * width],
            rows_ref.at[ah + i * vh : ah + (i + 1) * vh],
            row_sems.at[1 + i],
        )
        for i in range(4)
    ]
    for copy in copies:
        copy.start()
    for copy in loads:
        copy.wait()
    k = am_ref.shape[0]
    cut = A_ROWS - k
    vision_main = vm_ref[...].reshape(4 * k, 384)
    a_ref[:k, :] = am_ref[...]
    a_ref[k:A_ROWS, :] = vision_main[:cut]
    b_ref[:B_ROWS, :] = vision_main[cut:]
    odd = e % 2 == 1
    vision_tail = vt_ref[...].reshape(4 * k, 128)
    tail = jnp.concatenate([at_ref[...], vision_tail], axis=0).astype(jnp.float32)
    moved = pltpu.roll(tail, 64, 1)
    first = jnp.where(odd, moved, tail)
    second = jnp.where(odd, tail, moved)
    lane = lax.broadcasted_iota(jnp.int32, (B_TAIL, 128), 1)
    for q in range(3):
        cols = slice(q * 128, (q + 1) * 128)
        low = first[q * A_TAIL : (q + 1) * A_TAIL]
        high = second[96 + q * A_TAIL : 96 + (q + 1) * A_TAIL]
        a_ref[A_ROWS:, cols] = jnp.where(lane[:A_TAIL] < 64, low, high).astype(a_ref.dtype)
    base = A_ROWS
    for q in range(2):
        cols = slice(q * 128, (q + 1) * 128)
        low = first[base + q * B_TAIL : base + (q + 1) * B_TAIL]
        high = second[base + 112 + q * B_TAIL : base + 112 + (q + 1) * B_TAIL]
        b_ref[B_ROWS:, cols] = jnp.where(lane < 64, low, high).astype(b_ref.dtype)
    b_ref[B_ROWS : B_ROWS + 16, 256:] = first[base + 96 : base + 112].astype(b_ref.dtype)
    b_ref[B_ROWS + 16 :, 256:] = jnp.zeros((B_TAIL - 16, 128), b_ref.dtype)
    for copy in copies:
        copy.wait()


def pack(where, audio_weight, vision_weight, audio_rows, vision_rows):
    bf16 = jnp.bfloat16
    vmem = pl.BlockSpec(memory_space=pltpu.VMEM)
    anywhere = pl.BlockSpec(memory_space=pl.ANY)
    k = audio_weight.shape[0]
    return pl.pallas_call(
        pack_kernel,
        out_shape=(
            jax.ShapeDtypeStruct((A_PIECE, 384), bf16),
            jax.ShapeDtypeStruct((B_PIECE, 384), bf16),
            jax.ShapeDtypeStruct(
                (audio_rows.shape[0] // 2 + 2 * vision_rows.shape[0], audio_rows.shape[1]), bf16
            ),
        ),
        in_specs=[pl.BlockSpec(memory_space=pltpu.SMEM)] + [anywhere] * 4,
        out_specs=(vmem, vmem, vmem),
        scratch_shapes=[
            pltpu.VMEM((k, 384), bf16),
            pltpu.VMEM((k, 128), bf16),
            pltpu.VMEM((k, 4, 384), bf16),
            pltpu.VMEM((k, 4, 128), bf16),
            pltpu.SemaphoreType.DMA((4,)),
            pltpu.SemaphoreType.DMA((5,)),
        ],
        compiler_params=pltpu.CompilerParams(vmem_limit_bytes=BIG),
        cost_estimate=pl.CostEstimate(flops=0, bytes_accessed=1_800_000, transcendentals=0),
    )(where, in_hbm(audio_weight), in_hbm(vision_weight), in_hbm(audio_rows), in_hbm(vision_rows))


def encode_kernel(
    a_at_ref,
    b_at_ref,
    ga0,
    ga1,
    ga2,
    ga3,
    ga4,
    gb0,
    gb1,
    gb2,
    gb3,
    gb4,
    own_ref,
    other_ref,
    cell_ref,
    out_ref,
    wa_ref,
    wv_ref,
    ta_ref,
    tv_ref,
    x_ref,
    enc_ref,
    sems,
):
    bf16, f32 = jnp.bfloat16, jnp.float32
    audio_width = x_ref.shape[2]
    audio_k = wa_ref.shape[1]
    cut = A_ROWS - audio_k
    sources = ((ga0, gb0, 0, 4), (ga1, gb1, 4, 4), (ga2, gb2, 8, 4), (ga3, gb3, 12, 2), (ga4, gb4, 14, 2))
    own_copy = pltpu.make_async_copy(own_ref, x_ref, sems.at[0])
    own_copy.start()

    for ga, gb, start, size in sources:

        @pl.loop(0, size)
        def _(n):
            at = a_at_ref[start + n]
            wa_ref[at] = ga[n, :audio_k, :]
            wv_ref[at, :cut, :] = ga[n, audio_k:A_ROWS, :]
            ta = jnp.concatenate([ga[n, A_ROWS:, q * 128 : (q + 1) * 128] for q in range(3)], axis=0)
            ta_ref[at] = ta[:audio_k]
            tv_ref[at, : 96 - audio_k, :] = ta[audio_k:]
            tv_ref[at, 96 - audio_k : cut, :] = roll_half(ta)
            at = b_at_ref[start + n]
            wv_ref[at, cut:, :] = gb[n, :B_ROWS, :]
            tb = jnp.concatenate([gb[n, B_ROWS:, q * 128 : (q + 1) * 128] for q in range(2)], axis=0)
            tv_ref[at, cut : cut + 96, :] = tb
            tv_ref[at, cut + 96 : cut + 112, :] = gb[n, B_ROWS : B_ROWS + 16, 256:]
            tv_ref[at, cut + 112 :, :] = roll_half(tb)

    count = cell_ref.shape[1]
    cells = out_ref.shape[0]
    line = lax.broadcasted_iota(jnp.int32, (cells, count), 0)
    first = jnp.where(line == cell_ref[0:1, :], 1.0, 0.0).astype(bf16)
    second = jnp.where(line == cell_ref[1:2, :], 1.0, 0.0).astype(bf16)

    halves, n_enc = 2, x_ref.shape[0]
    audio = 64
    vision = 32
    n_vision = halves * n_enc * vision

    def weights(main, last):
        size = main.shape[0] * main.shape[1]
        return jnp.concatenate([main.reshape(size, 384), last.reshape(size, 128)], axis=1)

    def keep_rows(value, base, each):
        run = 2 * each
        for h in range(2):
            for g in range(2):
                at = g * count + base + h * run
                enc_ref[at : at + run, :] = value[(2 * h + g) * run : (2 * h + g + 1) * run]

    def rows(at, each):
        parts = [ref[:, at : at + each, :].reshape(n_enc * each, audio_width) for ref in (x_ref, other_ref)]
        return jnp.concatenate(parts, axis=0)

    own_copy.wait()
    keep_rows(dot(rows(0, audio), weights(wa_ref[...], ta_ref[...])).astype(bf16), 0, audio)
    total = jnp.zeros((n_vision, 512), f32)
    for i in range(4):
        part = weights(wv_ref[4 * i : 4 * i + 4], tv_ref[4 * i : 4 * i + 4])
        total = total + dot(rows(audio + i * vision, vision), part)
    keep_rows(total.astype(bf16), 4 * audio, vision)

    out_ref[:, :384] = dot(first, enc_ref[:count, :384]).astype(bf16)
    out_ref[:, 384:768] = dot(second, enc_ref[count:, :384]).astype(bf16)
    low = dot(first, enc_ref[:count, 384:])
    high = dot(second, enc_ref[count:, 384:])
    lane = lax.broadcasted_iota(jnp.int32, low.shape, 1)
    out_ref[:, 768:] = jnp.where(lane < 64, low, pltpu.roll(high, 64, 1)).astype(bf16)


def encode(a_at, b_at, shards_a, shards_b, own, other, cells, n_cells):
    bf16 = jnp.bfloat16
    n_enc, rows, width = own.shape
    smem = pl.BlockSpec(memory_space=pltpu.SMEM)
    vmem = pl.BlockSpec(memory_space=pltpu.VMEM)
    anywhere = pl.BlockSpec(memory_space=pl.ANY)
    k = width // 16
    return pl.pallas_call(
        encode_kernel,
        out_shape=jax.ShapeDtypeStruct((n_cells, 896), bf16),
        in_specs=[smem, smem] + [vmem] * 10 + [anywhere] + [vmem] * 2,
        out_specs=vmem,
        scratch_shapes=[
            pltpu.VMEM((16, k, 384), bf16),
            pltpu.VMEM((16, 4 * k, 384), bf16),
            pltpu.VMEM((16, k, 128), bf16),
            pltpu.VMEM((16, 4 * k, 128), bf16),
            pltpu.VMEM((n_enc, rows, width), bf16),
            pltpu.VMEM((2 * cells.shape[1], 512), bf16),
            pltpu.SemaphoreType.DMA((1,)),
        ],
        compiler_params=pltpu.CompilerParams(vmem_limit_bytes=BIG),
        cost_estimate=pl.CostEstimate(
            flops=3_000_000_000, bytes_accessed=11_000_000, transcendentals=0
        ),
    )(a_at, b_at, *shards_a, *shards_b, in_hbm(own), other, cells)


def place_kernel(e_row_ref, arrived_ref, text_hbm, filled_ref, out_ref, text_ref, sem):
    bf16, f32 = jnp.bfloat16, jnp.float32
    load = pltpu.make_async_copy(text_hbm, text_ref, sem)
    load.start()
    rows = out_ref.shape[0]
    each = arrived_ref.shape[0] // 4
    line = lax.broadcasted_iota(jnp.int32, (rows, each), 0)
    first = jnp.where(line == e_row_ref[0:1, :], 1.0, 0.0).astype(bf16)
    second = jnp.where(line == e_row_ref[1:2, :], 1.0, 0.0).astype(bf16)
    both = jnp.concatenate([first, second], axis=1)
    taken = filled_ref[...] > 0.5
    lane = lax.broadcasted_iota(jnp.int32, (rows, 128), 1)
    low = []
    high = []
    load.wait()
    for e in range(4):
        at = slice(e * each, (e + 1) * each)
        main = jnp.concatenate([arrived_ref[at, :384], arrived_ref[at, 384:768]], axis=0)
        cols = slice(e * 384, (e + 1) * 384)
        text = text_ref[:, cols].astype(f32)
        out_ref[:, cols] = jnp.where(taken, dot(both, main), text).astype(bf16)
        last = arrived_ref[at, 768:]
        low.append(dot(first, last))
        high.append(dot(second, last))
    for q in range(2):
        left = low[2 * q] + pltpu.roll(high[2 * q], 64, 1)
        right = pltpu.roll(low[2 * q + 1], 64, 1) + high[2 * q + 1]
        cols = slice(1536 + q * 128, 1536 + (q + 1) * 128)
        text = text_ref[:, cols].astype(f32)
        out_ref[:, cols] = jnp.where(taken, jnp.where(lane < 64, left, right), text).astype(bf16)


def place(spots, arrived, text, filled):
    vmem = pl.BlockSpec(memory_space=pltpu.VMEM)
    return pl.pallas_call(
        place_kernel,
        out_shape=jax.ShapeDtypeStruct(text.shape, text.dtype),
        in_specs=[vmem, vmem, pl.BlockSpec(memory_space=pl.ANY), vmem],
        out_specs=vmem,
        scratch_shapes=[pltpu.VMEM(text.shape, text.dtype), pltpu.SemaphoreType.DMA],
        compiler_params=pltpu.CompilerParams(vmem_limit_bytes=12 * 1024 * 1024),
        cost_estimate=pl.CostEstimate(flops=300_000_000, bytes_accessed=3_000_000, transcendentals=0),
    )(spots, arrived, text, filled)


def finish_kernel(
    half_ref,
    rows_ref,
    keep_ref,
    taken_ref,
    inv_ref,
    stat_ref,
    gain_ref,
    spot_ref,
    out_ref,
    grad_ref,
):
    bf16, f32 = jnp.bfloat16, jnp.float32
    rows, slab = rows_ref.shape
    cells = out_ref.shape[0]
    half = slab // 2
    inv = inv_ref[...]
    gain = gain_ref[pl.ds(half_ref[0], 1), :]
    line = lax.broadcasted_iota(jnp.int32, (cells, rows), 1)
    first = jnp.where(line == spot_ref[:, 0:1], 1.0, 0.0).astype(bf16)
    second = jnp.where(line == spot_ref[:, 1:2], 1.0, 0.0).astype(bf16)
    both = jnp.concatenate([first, second], axis=1)
    sent = taken_ref[:, slab:].astype(f32)
    stat = stat_ref[...] + sent[:, 0:1] + sent[:, 1:2]
    factor = inv * inv * inv / (2 * slab) * stat
    for c in range(0, slab, 128):
        cols = slice(c, c + 128)
        total = keep_ref[:, cols].astype(f32) + taken_ref[:, cols].astype(f32)
        value = (gain[:, cols] * total - rows_ref[:, cols].astype(f32) * factor).astype(bf16)
        at = c // half
        grad_ref[at * rows : (at + 1) * rows, c - at * half : c - at * half + 128] = value
    out_ref[...] = dot(both, grad_ref[...]).astype(bf16)


def finish(half, rows, keep, taken, inv, stat, gain, spots):
    bf16 = jnp.bfloat16
    vmem = pl.BlockSpec(memory_space=pltpu.VMEM)
    cells = spots.shape[0]
    count, slab = rows.shape
    return pl.pallas_call(
        finish_kernel,
        out_shape=jax.ShapeDtypeStruct((cells, slab // 2), bf16),
        in_specs=[pl.BlockSpec(memory_space=pltpu.SMEM)] + [vmem] * 7,
        out_specs=vmem,
        scratch_shapes=[pltpu.VMEM((2 * count, slab // 2), bf16)],
        compiler_params=pltpu.CompilerParams(vmem_limit_bytes=16 * 1024 * 1024),
        cost_estimate=pl.CostEstimate(flops=500_000_000, bytes_accessed=4_000_000, transcendentals=0),
    )(half.reshape(1), rows, keep, taken, inv, stat, gain, spots)


def collect_kernel(cell_ref, returned_ref, audio_ref, vision_ref):
    bf16 = jnp.bfloat16
    count = cell_ref.shape[0]
    cells, half = returned_ref.shape
    audio = audio_ref.shape[0]
    line = lax.broadcasted_iota(jnp.int32, (count, cells), 1)
    for h in range(2):
        hot = jnp.where(line == cell_ref[...] + 4 * h, 1.0, 0.0).astype(bf16)
        value = dot(hot, returned_ref[...]).astype(bf16)
        cols = slice(h * half, (h + 1) * half)
        audio_ref[:, cols] = value[:audio]
        vision_ref[:, cols] = value[audio:]


def collect(cell, returned, audio):
    vmem = pl.BlockSpec(memory_space=pltpu.VMEM)
    count = cell.shape[0]
    width = 2 * returned.shape[1]
    return pl.pallas_call(
        collect_kernel,
        out_shape=(
            jax.ShapeDtypeStruct((audio, width), jnp.bfloat16),
            jax.ShapeDtypeStruct((count - audio, width), jnp.bfloat16),
        ),
        in_specs=[vmem] * 2,
        out_specs=(vmem,) * 2,
        compiler_params=pltpu.CompilerParams(vmem_limit_bytes=12 * 1024 * 1024),
        cost_estimate=pl.CostEstimate(flops=400_000_000, bytes_accessed=2_000_000, transcendentals=0),
    )(cell, returned)


def swap(x):
    return lax.ppermute(x, "tp", [(0, 1), (1, 0)])


def shift(x, axis, k):
    return lax.ppermute(x, axis, [(i, (i + k) % 4) for i in range(4)])


def ranks(dest):
    count = dest.shape[1]
    same = dest[:, :, None] == dest[:, None, :]
    earlier = jnp.arange(count)[None, :] < jnp.arange(count)[:, None]
    return jnp.sum((same & earlier[None]).astype(jnp.int32), axis=2)


def local(
    audio_rows,
    vision_rows,
    audio_weight,
    vision_weight,
    text_rows,
    row_target,
    segment_ids,
    norm_gain,
    qkv_weight,
    attn_grad,
):
    bf16, f32 = jnp.bfloat16, jnp.float32
    t = lax.axis_index("tp")
    e = lax.axis_index("enc")
    j = lax.axis_index(("z", "y"))
    n_enc = 4
    n_seq = 16
    self_index = e * n_seq + j
    senders, enc_rows = row_target.shape
    length, slab = text_rows.shape
    audio_count, audio_width = audio_rows.shape
    vision_count = vision_rows.shape[0]
    merge = vision_weight.shape[1]
    cap = 4
    wide = slab // 128 // n_enc * 128

    piece_a, piece_b, packed = pack(
        jnp.stack([e, t]),
        audio_weight,
        vision_weight,
        audio_rows,
        vision_rows,
    )
    z, y = lax.axis_index("z"), lax.axis_index("y")
    hops = (1, 3, 2)
    back = jnp.array((0,) + hops, jnp.int32)
    a_at = (((z - back) % 4)[:, None] * 4 + ((y - back) % 4)[None, :]).reshape(-1)
    b_at = (((y - back) % 4)[:, None] + ((z - back) % 4)[None, :] * 4).reshape(-1)
    ah, vh = audio_count // 2, vision_count // 2

    line = row_target.reshape(n_enc, n_seq, enc_rows)[:, j]
    line_dest = line // length
    line_slot = line_dest * (n_enc * cap) + jnp.arange(n_enc)[:, None] * cap + ranks(line_dest)
    a_slot = line_slot[:, :audio_count].reshape(2, 2, 2, ah)
    v_slot = line_slot[:, audio_count:].reshape(2, 2, 2, vh)
    halves = jnp.stack([t, 1 - t])
    a_slot = jnp.moveaxis(a_slot, 2, 1)[:, halves].reshape(2, -1)
    v_slot = jnp.moveaxis(v_slot, 2, 1)[:, halves].reshape(2, -1)
    row_slot = jnp.concatenate([a_slot, v_slot], axis=1)
    cells = row_slot // 16 * 8 + row_slot % 8

    dest = row_target // length
    mine = (dest == self_index).astype(jnp.int32)
    rank_all = jnp.cumsum(mine, axis=1) - 1
    hot = (rank_all[:, :, None] == jnp.arange(cap)[None, None, :]) & (mine[:, :, None] == 1)
    incoming = jnp.sum(jnp.where(hot, (row_target % length)[:, :, None] + 1, 0), axis=1) - 1
    by_line = incoming.reshape(2, 2, n_seq, cap).transpose(0, 2, 1, 3).reshape(2, -1)
    filled = jnp.max(
        (jnp.arange(length)[:, None] == incoming.reshape(1, -1)).astype(jnp.float32), axis=1, keepdims=True
    )
    half = slab // 2
    nowhere = jnp.full_like(incoming, -1)
    spots = jnp.stack(
        [
            jnp.stack([incoming, nowhere], axis=1).reshape(-1),
            jnp.stack([nowhere, incoming], axis=1).reshape(-1),
        ],
        axis=1,
    )
    own_target = lax.dynamic_index_in_dim(row_target, self_index, 0, keepdims=True)
    own_dest = own_target // length
    own_cell = (own_dest * (2 * cap) + ranks(own_dest)).reshape(-1, 1)
    gain = norm_gain.reshape(2, slab)
    seg_row = segment_ids
    seg_col = segment_ids.reshape(length, 1)
    along_y = [piece_a] + [shift(piece_a, "y", k) for k in hops]
    along_z = [piece_b] + [shift(piece_b, "z", k) for k in hops]
    along_y, along_z, cells, by_line, filled, spots, own_cell, gain, seg_col, a_at, b_at = (
        lax.optimization_barrier(
            (along_y, along_z, cells, by_line, filled, spots, own_cell, gain, seg_col, a_at, b_at)
        )
    )
    stack_a, stack_b = lax.optimization_barrier((jnp.stack(along_y), jnp.stack(along_z)))
    near_a = [shift(stack_a, "z", 1), shift(stack_a, "z", 3)]
    near_b = [shift(stack_b, "y", 1), shift(stack_b, "y", 3)]
    own = lax.all_gather(packed, "enc", axis=0, tiled=False)
    near_a, near_b, own = lax.optimization_barrier((near_a, near_b, own))
    far_a = [shift(near_a[0][:2], "z", 1), shift(near_a[1][2:], "z", 3)]
    far_b = [shift(near_b[0][:2], "y", 1), shift(near_b[1][2:], "y", 3)]
    shards_a = [stack_a] + near_a + far_a
    shards_b = [stack_b] + near_b + far_b
    other = swap(own)
    outgoing = encode(a_at, b_at, shards_a, shards_b, own, other, cells, senders * 8)
    arrived = lax.all_to_all(
        outgoing.reshape(senders, 8, slab // 2), SPREAD, split_axis=0, concat_axis=0, tiled=True
    )
    row_slab = place(by_line, arrived.reshape(senders * 8, slab // 2), text_rows, filled)

    other_slab = swap(row_slab)
    give, keep, inv_rms, row_part = attend(
        t, row_slab, other_slab, gain, qkv_weight, attn_grad, seg_row, seg_col
    )
    taken = swap(give)

    out8 = finish(t, row_slab, keep, taken, inv_rms, row_part, gain, spots)
    returned = lax.all_to_all(
        out8.reshape(senders, 2 * cap, half), SPREAD, split_axis=0, concat_axis=0, tiled=True
    )
    return collect(own_cell, returned.reshape(senders * 2 * cap, half), audio_count)


SPREAD = ("enc", "z", "y")


def solution(mesh):
    torus = Mesh(mesh.devices.reshape(4, 4, 4, 2), ("enc", "z", "y", "tp"))
    in_specs = (
        P(SPREAD, None),
        P(SPREAD, None),
        P(("z", "y"), "tp"),
        P(("z", "y"), None, "tp"),
        P(SPREAD, "tp"),
        P(),
        P(SPREAD, None),
        P(),
        P(None, "tp"),
        P(SPREAD, "tp"),
    )
    out_specs = (P(SPREAD, "tp"), P(SPREAD, "tp"))
    return jax.shard_map(local, mesh=torus, in_specs=in_specs, out_specs=out_specs, check_vma=False)
```

```python
import jax
import jax.numpy as jnp
from jax import lax
from jax.experimental import pallas as pl
from jax.experimental.pallas import tpu as pltpu
from jax.sharding import Mesh
from jax.sharding import PartitionSpec as P

HEAD_DIM = 128

epsilon = 1e-06


NT = (((1,), (1,)), ((), ()))
NN = (((1,), (0,)), ((), ()))
TAIL = 128
BIG = 26 * 1024 * 1024


def in_hbm(x):
    return pltpu.with_memory_space_constraint(x, pltpu.HBM)


def dot(x, y, dims=NN):
    return lax.dot_general(x, y, dims, preferred_element_type=jnp.float32)


EARLY = 640


def fetch_kernel(weight_hbm, upstream_hbm, weight_ref, upstream_ref, sems):
    copies = [
        pltpu.make_async_copy(weight_hbm.at[:, :EARLY], weight_ref, sems.at[0]),
        pltpu.make_async_copy(upstream_hbm, upstream_ref, sems.at[1]),
    ]
    for copy in copies:
        copy.start()
    for copy in copies:
        copy.wait()


def fetch(weight, upstream):
    return pl.pallas_call(
        fetch_kernel,
        out_shape=(
            pltpu.VMEM((weight.shape[0], EARLY), weight.dtype),
            pltpu.VMEM(upstream.shape, upstream.dtype),
        ),
        in_specs=[pl.BlockSpec(memory_space=pl.ANY)] * 2,
        out_specs=(pl.BlockSpec(memory_space=pltpu.VMEM),) * 2,
        scratch_shapes=[pltpu.SemaphoreType.DMA((2,))],
        compiler_params=pltpu.CompilerParams(vmem_limit_bytes=1024 * 1024),
        cost_estimate=pl.CostEstimate(flops=0, bytes_accessed=10_000_000, transcendentals=0),
    )(in_hbm(weight), in_hbm(upstream))


def attend_kernel(
    half_ref,
    own_ref,
    other_ref,
    gain_ref,
    early_ref,
    weight_hbm,
    upstream_ref,
    seg_row_ref,
    seg_col_ref,
    give_ref,
    keep_ref,
    inv_ref,
    stat_ref,
    normed_ref,
    unscaled_ref,
    scaled_ref,
    sgrad_ref,
    bias_ref,
    late_ref,
    sem,
):
    bf16, f32 = jnp.bfloat16, jnp.float32
    rows, slab = own_ref.shape
    group = weight_hbm.shape[1]
    heads = group // HEAD_DIM - 2
    split = early_ref.shape[1]
    load = pltpu.make_async_copy(weight_hbm.at[:, split:], late_ref, sem)
    load.start()
    place_u = lax.broadcasted_iota(jnp.int32, (rows, rows), 0)
    place_t = lax.broadcasted_iota(jnp.int32, (rows, rows), 1)
    allowed = (seg_col_ref[...] == seg_row_ref[...]) & (place_u <= place_t)
    bias_ref[...] = jnp.where(allowed, 0.0, -1e30)

    t = half_ref[0]
    own_at = pl.multiple_of(t * slab, HEAD_DIM)
    other_at = pl.multiple_of((1 - t) * slab, HEAD_DIM)
    score_scale = HEAD_DIM ** (-0.5)

    squares = jnp.zeros((rows, HEAD_DIM), f32)
    for part, ref in ((t, own_ref), (1 - t, other_ref)):
        gain = gain_ref[pl.ds(part, 1), :]
        for c in range(0, slab, HEAD_DIM):
            x = ref[:, c : c + HEAD_DIM].astype(f32)
            squares = squares + x * x
            at = pl.multiple_of(part * slab + c, HEAD_DIM)
            normed_ref[:, pl.ds(at, HEAD_DIM)] = (x * gain[:, c : c + HEAD_DIM]).astype(bf16)
    inv = lax.rsqrt(jnp.sum(squares, axis=1, keepdims=True) / (2 * slab) + epsilon)
    inv_ref[...] = inv

    for ref, at, end in ((early_ref, 0, split), (late_ref, split, group)):
        if at:
            load.wait()
        value = dot(normed_ref[...], ref[...])
        unscaled_ref[:, at:end] = value
        scaled_ref[:, at:end] = (value * inv).astype(bf16)

    key = scaled_ref[:, heads * HEAD_DIM : (heads + 1) * HEAD_DIM]
    val = scaled_ref[:, (heads + 1) * HEAD_DIM :]
    grad_key = jnp.zeros((rows, HEAD_DIM), f32)
    grad_val = jnp.zeros((rows, HEAD_DIM), f32)
    stat = jnp.zeros((rows, HEAD_DIM), f32)
    for h in range(heads):
        cols = slice(h * HEAD_DIM, (h + 1) * HEAD_DIM)
        query = scaled_ref[:, cols]
        up = upstream_ref[:, cols]
        scores = dot(key, query, NT) * score_scale + bias_ref[...]
        scores = jnp.exp(scores - jnp.max(scores, axis=0, keepdims=True))
        probs = scores * (1.0 / jnp.sum(scores, axis=0, keepdims=True))
        dprobs = dot(val, up, NT)
        delta = jnp.sum(probs * dprobs, axis=0, keepdims=True)
        sgrad = (probs * (dprobs - delta) * score_scale).astype(bf16)
        grad_val = grad_val + dot(probs.astype(bf16), up)
        grad_key = grad_key + dot(sgrad, query)
        grad_query = dot(sgrad.T, key)
        stat = stat + grad_query * unscaled_ref[:, cols]
        sgrad_ref[:, cols] = (grad_query * inv).astype(bf16)
    cols = slice(heads * HEAD_DIM, (heads + 1) * HEAD_DIM)
    stat = stat + grad_key * unscaled_ref[:, cols]
    sgrad_ref[:, cols] = (grad_key * inv).astype(bf16)
    cols = slice((heads + 1) * HEAD_DIM, (heads + 2) * HEAD_DIM)
    stat = stat + grad_val * unscaled_ref[:, cols]
    sgrad_ref[:, cols] = (grad_val * inv).astype(bf16)
    total = jnp.sum(stat, axis=1, keepdims=True)
    stat_ref[...] = total
    lane = lax.broadcasted_iota(jnp.int32, (rows, TAIL), 1)
    high = total.astype(bf16)
    low = (total - high.astype(f32)).astype(bf16)
    give_ref[:, slab:] = jnp.where(lane == 0, high.astype(f32), low.astype(f32)).astype(bf16)


    def back(at):
        rows_at = pl.ds(at, slab)
        return (
            dot(sgrad_ref[:, :split], early_ref[rows_at, :], NT)
            + dot(sgrad_ref[:, split:], late_ref[rows_at, :], NT)
        ).astype(bf16)

    keep_ref[...] = back(own_at)
    give_ref[:, :slab] = back(other_at)


def attend(half, own, other, gain, early, qkv_weight, upstream, seg_row, seg_col):
    rows, slab = own.shape
    group = qkv_weight.shape[1]
    f32, bf16 = jnp.float32, jnp.bfloat16
    vmem = pl.BlockSpec(memory_space=pltpu.VMEM)
    anywhere = pl.BlockSpec(memory_space=pl.ANY)
    return pl.pallas_call(
        attend_kernel,
        out_shape=(
            jax.ShapeDtypeStruct((rows, slab + TAIL), bf16),
            jax.ShapeDtypeStruct((rows, slab), bf16),
            jax.ShapeDtypeStruct((rows, 1), f32),
            jax.ShapeDtypeStruct((rows, 1), f32),
        ),
        in_specs=[pl.BlockSpec(memory_space=pltpu.SMEM), vmem, vmem, vmem]
        + [vmem, anywhere, vmem, vmem, vmem],
        out_specs=(vmem,) * 4,
        scratch_shapes=[
            pltpu.VMEM((rows, 2 * slab), bf16),
            pltpu.VMEM((rows, group), f32),
            pltpu.VMEM((rows, group), bf16),
            pltpu.VMEM((rows, group), bf16),
            pltpu.VMEM((rows, rows), f32),
            pltpu.VMEM((2 * slab, group - early.shape[1]), bf16),
            pltpu.SemaphoreType.DMA,
        ],
        compiler_params=pltpu.CompilerParams(vmem_limit_bytes=BIG),
        cost_estimate=pl.CostEstimate(flops=5_000_000_000, bytes_accessed=14_000_000, transcendentals=500_000),
    )(
        half.reshape(1),
        own,
        other,
        gain,
        early,
        in_hbm(qkv_weight),
        upstream,
        seg_row,
        seg_col,
    )


def roll_half(x):
    return pltpu.roll(x.astype(jnp.float32), 64, 1).astype(x.dtype)


A_ROWS, A_TAIL = 192, 32
B_ROWS, B_TAIL = 208, 48
A_PIECE = A_ROWS + A_TAIL
B_PIECE = B_ROWS + B_TAIL


def pack_kernel(
    place_ref,
    audio_w_ref,
    vision_w_ref,
    audio_ref,
    vision_ref,
    a_ref,
    b_ref,
    rows_ref,
    am_ref,
    at_ref,
    vm_ref,
    vt_ref,
    sems,
    row_sems,
):
    e = place_ref[0]
    t = place_ref[1]
    main_at = pl.multiple_of(e * 384, 128)
    tail_at = pl.multiple_of(1536 + e // 2 * 128, 128)
    loads = [
        pltpu.make_async_copy(vision_w_ref.at[:, :, pl.ds(main_at, 384)], vm_ref, sems.at[0]),
        pltpu.make_async_copy(vision_w_ref.at[:, :, pl.ds(tail_at, 128)], vt_ref, sems.at[1]),
        pltpu.make_async_copy(audio_w_ref.at[:, pl.ds(main_at, 384)], am_ref, sems.at[2]),
        pltpu.make_async_copy(audio_w_ref.at[:, pl.ds(tail_at, 128)], at_ref, sems.at[3]),
    ]
    for copy in loads:
        copy.start()
    width = rows_ref.shape[1]
    ah, vh = audio_ref.shape[0] // 2, vision_ref.shape[0] // 2
    copies = [
        pltpu.make_async_copy(
            audio_ref.at[pl.ds(pl.multiple_of(t * ah, 16), ah), :], rows_ref.at[:ah], row_sems.at[0]
        )
    ] + [
        pltpu.make_async_copy(
            vision_ref.at[pl.ds(pl.multiple_of(t * vh, 16), vh), i * width : (i + 1) * width],
            rows_ref.at[ah + i * vh : ah + (i + 1) * vh],
            row_sems.at[1 + i],
        )
        for i in range(4)
    ]
    for copy in copies:
        copy.start()
    for copy in loads:
        copy.wait()
    k = am_ref.shape[0]
    cut = A_ROWS - k
    vision_main = vm_ref[...].reshape(4 * k, 384)
    a_ref[:k, :] = am_ref[...]
    a_ref[k:A_ROWS, :] = vision_main[:cut]
    b_ref[:B_ROWS, :] = vision_main[cut:]
    odd = e % 2 == 1
    vision_tail = vt_ref[...].reshape(4 * k, 128)
    tail = jnp.concatenate([at_ref[...], vision_tail], axis=0).astype(jnp.float32)
    moved = pltpu.roll(tail, 64, 1)
    first = jnp.where(odd, moved, tail)
    second = jnp.where(odd, tail, moved)
    lane = lax.broadcasted_iota(jnp.int32, (B_TAIL, 128), 1)
    for q in range(3):
        cols = slice(q * 128, (q + 1) * 128)
        low = first[q * A_TAIL : (q + 1) * A_TAIL]
        high = second[96 + q * A_TAIL : 96 + (q + 1) * A_TAIL]
        a_ref[A_ROWS:, cols] = jnp.where(lane[:A_TAIL] < 64, low, high).astype(a_ref.dtype)
    base = A_ROWS
    for q in range(2):
        cols = slice(q * 128, (q + 1) * 128)
        low = first[base + q * B_TAIL : base + (q + 1) * B_TAIL]
        high = second[base + 112 + q * B_TAIL : base + 112 + (q + 1) * B_TAIL]
        b_ref[B_ROWS:, cols] = jnp.where(lane < 64, low, high).astype(b_ref.dtype)
    b_ref[B_ROWS : B_ROWS + 16, 256:] = first[base + 96 : base + 112].astype(b_ref.dtype)
    b_ref[B_ROWS + 16 :, 256:] = jnp.zeros((B_TAIL - 16, 128), b_ref.dtype)
    for copy in copies:
        copy.wait()


def pack(where, audio_weight, vision_weight, audio_rows, vision_rows):
    bf16 = jnp.bfloat16
    vmem = pl.BlockSpec(memory_space=pltpu.VMEM)
    anywhere = pl.BlockSpec(memory_space=pl.ANY)
    k = audio_weight.shape[0]
    return pl.pallas_call(
        pack_kernel,
        out_shape=(
            jax.ShapeDtypeStruct((A_PIECE, 384), bf16),
            jax.ShapeDtypeStruct((B_PIECE, 384), bf16),
            jax.ShapeDtypeStruct(
                (audio_rows.shape[0] // 2 + 2 * vision_rows.shape[0], audio_rows.shape[1]), bf16
            ),
        ),
        in_specs=[pl.BlockSpec(memory_space=pltpu.SMEM)] + [anywhere] * 4,
        out_specs=(vmem, vmem, vmem),
        scratch_shapes=[
            pltpu.VMEM((k, 384), bf16),
            pltpu.VMEM((k, 128), bf16),
            pltpu.VMEM((k, 4, 384), bf16),
            pltpu.VMEM((k, 4, 128), bf16),
            pltpu.SemaphoreType.DMA((4,)),
            pltpu.SemaphoreType.DMA((5,)),
        ],
        compiler_params=pltpu.CompilerParams(vmem_limit_bytes=BIG),
        cost_estimate=pl.CostEstimate(flops=0, bytes_accessed=1_800_000, transcendentals=0),
    )(where, in_hbm(audio_weight), in_hbm(vision_weight), in_hbm(audio_rows), in_hbm(vision_rows))


def encode_kernel(
    a_at_ref,
    b_at_ref,
    ga0,
    ga1,
    ga2,
    ga3,
    ga4,
    gb0,
    gb1,
    gb2,
    gb3,
    gb4,
    own_ref,
    other_ref,
    cell_ref,
    out_ref,
    wa_ref,
    wv_ref,
    ta_ref,
    tv_ref,
    x_ref,
    enc_ref,
    sems,
):
    bf16, f32 = jnp.bfloat16, jnp.float32
    audio_width = x_ref.shape[2]
    audio_k = wa_ref.shape[1]
    cut = A_ROWS - audio_k
    sources = ((ga0, gb0, 0, 4), (ga1, gb1, 4, 4), (ga2, gb2, 8, 4), (ga3, gb3, 12, 2), (ga4, gb4, 14, 2))
    own_copy = pltpu.make_async_copy(own_ref, x_ref, sems.at[0])
    own_copy.start()

    for ga, gb, start, size in sources:

        @pl.loop(0, size)
        def _(n):
            at = a_at_ref[start + n]
            wa_ref[at] = ga[n, :audio_k, :]
            wv_ref[at, :cut, :] = ga[n, audio_k:A_ROWS, :]
            ta = jnp.concatenate([ga[n, A_ROWS:, q * 128 : (q + 1) * 128] for q in range(3)], axis=0)
            ta_ref[at] = ta[:audio_k]
            tv_ref[at, : 96 - audio_k, :] = ta[audio_k:]
            tv_ref[at, 96 - audio_k : cut, :] = roll_half(ta)
            at = b_at_ref[start + n]
            wv_ref[at, cut:, :] = gb[n, :B_ROWS, :]
            tb = jnp.concatenate([gb[n, B_ROWS:, q * 128 : (q + 1) * 128] for q in range(2)], axis=0)
            tv_ref[at, cut : cut + 96, :] = tb
            tv_ref[at, cut + 96 : cut + 112, :] = gb[n, B_ROWS : B_ROWS + 16, 256:]
            tv_ref[at, cut + 112 :, :] = roll_half(tb)

    count = cell_ref.shape[1]
    cells = out_ref.shape[0]
    line = lax.broadcasted_iota(jnp.int32, (cells, count), 0)
    first = jnp.where(line == cell_ref[0:1, :], 1.0, 0.0).astype(bf16)
    second = jnp.where(line == cell_ref[1:2, :], 1.0, 0.0).astype(bf16)

    halves, n_enc = 2, x_ref.shape[0]
    audio = 64
    vision = 32
    n_vision = halves * n_enc * vision

    def weights(main, last):
        size = main.shape[0] * main.shape[1]
        return jnp.concatenate([main.reshape(size, 384), last.reshape(size, 128)], axis=1)

    def keep_rows(value, base, each):
        run = 2 * each
        for h in range(2):
            for g in range(2):
                at = g * count + base + h * run
                enc_ref[at : at + run, :] = value[(2 * h + g) * run : (2 * h + g + 1) * run]

    def rows(at, each):
        parts = [ref[:, at : at + each, :].reshape(n_enc * each, audio_width) for ref in (x_ref, other_ref)]
        return jnp.concatenate(parts, axis=0)

    own_copy.wait()
    keep_rows(dot(rows(0, audio), weights(wa_ref[...], ta_ref[...])).astype(bf16), 0, audio)
    total = jnp.zeros((n_vision, 512), f32)
    for i in range(4):
        part = weights(wv_ref[4 * i : 4 * i + 4], tv_ref[4 * i : 4 * i + 4])
        total = total + dot(rows(audio + i * vision, vision), part)
    keep_rows(total.astype(bf16), 4 * audio, vision)

    out_ref[:, :384] = dot(first, enc_ref[:count, :384]).astype(bf16)
    out_ref[:, 384:768] = dot(second, enc_ref[count:, :384]).astype(bf16)
    low = dot(first, enc_ref[:count, 384:])
    high = dot(second, enc_ref[count:, 384:])
    lane = lax.broadcasted_iota(jnp.int32, low.shape, 1)
    out_ref[:, 768:] = jnp.where(lane < 64, low, pltpu.roll(high, 64, 1)).astype(bf16)


def encode(a_at, b_at, shards_a, shards_b, own, other, cells, n_cells):
    bf16 = jnp.bfloat16
    n_enc, rows, width = own.shape
    smem = pl.BlockSpec(memory_space=pltpu.SMEM)
    vmem = pl.BlockSpec(memory_space=pltpu.VMEM)
    anywhere = pl.BlockSpec(memory_space=pl.ANY)
    k = width // 16
    return pl.pallas_call(
        encode_kernel,
        out_shape=jax.ShapeDtypeStruct((n_cells, 896), bf16),
        in_specs=[smem, smem] + [vmem] * 10 + [anywhere] + [vmem] * 2,
        out_specs=vmem,
        scratch_shapes=[
            pltpu.VMEM((16, k, 384), bf16),
            pltpu.VMEM((16, 4 * k, 384), bf16),
            pltpu.VMEM((16, k, 128), bf16),
            pltpu.VMEM((16, 4 * k, 128), bf16),
            pltpu.VMEM((n_enc, rows, width), bf16),
            pltpu.VMEM((2 * cells.shape[1], 512), bf16),
            pltpu.SemaphoreType.DMA((1,)),
        ],
        compiler_params=pltpu.CompilerParams(vmem_limit_bytes=BIG),
        cost_estimate=pl.CostEstimate(
            flops=3_000_000_000, bytes_accessed=11_000_000, transcendentals=0
        ),
    )(a_at, b_at, *shards_a, *shards_b, in_hbm(own), other, cells)


def place_kernel(e_row_ref, arrived_ref, text_hbm, filled_ref, out_ref, text_ref, sem):
    bf16, f32 = jnp.bfloat16, jnp.float32
    load = pltpu.make_async_copy(text_hbm, text_ref, sem)
    load.start()
    rows = out_ref.shape[0]
    each = arrived_ref.shape[0] // 4
    line = lax.broadcasted_iota(jnp.int32, (rows, each), 0)
    first = jnp.where(line == e_row_ref[0:1, :], 1.0, 0.0).astype(bf16)
    second = jnp.where(line == e_row_ref[1:2, :], 1.0, 0.0).astype(bf16)
    both = jnp.concatenate([first, second], axis=1)
    taken = filled_ref[...] > 0.5
    lane = lax.broadcasted_iota(jnp.int32, (rows, 128), 1)
    low = []
    high = []
    load.wait()
    for e in range(4):
        at = slice(e * each, (e + 1) * each)
        main = jnp.concatenate([arrived_ref[at, :384], arrived_ref[at, 384:768]], axis=0)
        cols = slice(e * 384, (e + 1) * 384)
        text = text_ref[:, cols].astype(f32)
        out_ref[:, cols] = jnp.where(taken, dot(both, main), text).astype(bf16)
        last = arrived_ref[at, 768:]
        low.append(dot(first, last))
        high.append(dot(second, last))
    for q in range(2):
        left = low[2 * q] + pltpu.roll(high[2 * q], 64, 1)
        right = pltpu.roll(low[2 * q + 1], 64, 1) + high[2 * q + 1]
        cols = slice(1536 + q * 128, 1536 + (q + 1) * 128)
        text = text_ref[:, cols].astype(f32)
        out_ref[:, cols] = jnp.where(taken, jnp.where(lane < 64, left, right), text).astype(bf16)


def place(spots, arrived, text, filled):
    vmem = pl.BlockSpec(memory_space=pltpu.VMEM)
    return pl.pallas_call(
        place_kernel,
        out_shape=jax.ShapeDtypeStruct(text.shape, text.dtype),
        in_specs=[vmem, vmem, pl.BlockSpec(memory_space=pl.ANY), vmem],
        out_specs=vmem,
        scratch_shapes=[pltpu.VMEM(text.shape, text.dtype), pltpu.SemaphoreType.DMA],
        compiler_params=pltpu.CompilerParams(vmem_limit_bytes=12 * 1024 * 1024),
        cost_estimate=pl.CostEstimate(flops=300_000_000, bytes_accessed=3_000_000, transcendentals=0),
    )(spots, arrived, text, filled)


def finish_kernel(
    half_ref,
    rows_ref,
    keep_ref,
    taken_ref,
    inv_ref,
    stat_ref,
    gain_ref,
    spot_ref,
    out_ref,
    grad_ref,
):
    bf16, f32 = jnp.bfloat16, jnp.float32
    rows, slab = rows_ref.shape
    cells = out_ref.shape[0]
    half = slab // 2
    inv = inv_ref[...]
    gain = gain_ref[pl.ds(half_ref[0], 1), :]
    line = lax.broadcasted_iota(jnp.int32, (cells, rows), 1)
    first = jnp.where(line == spot_ref[:, 0:1], 1.0, 0.0).astype(bf16)
    second = jnp.where(line == spot_ref[:, 1:2], 1.0, 0.0).astype(bf16)
    both = jnp.concatenate([first, second], axis=1)
    sent = taken_ref[:, slab:].astype(f32)
    stat = stat_ref[...] + sent[:, 0:1] + sent[:, 1:2]
    factor = inv * inv * inv / (2 * slab) * stat
    for c in range(0, slab, 128):
        cols = slice(c, c + 128)
        total = keep_ref[:, cols].astype(f32) + taken_ref[:, cols].astype(f32)
        value = (gain[:, cols] * total - rows_ref[:, cols].astype(f32) * factor).astype(bf16)
        at = c // half
        grad_ref[at * rows : (at + 1) * rows, c - at * half : c - at * half + 128] = value
    out_ref[...] = dot(both, grad_ref[...]).astype(bf16)


def finish(half, rows, keep, taken, inv, stat, gain, spots):
    bf16 = jnp.bfloat16
    vmem = pl.BlockSpec(memory_space=pltpu.VMEM)
    cells = spots.shape[0]
    count, slab = rows.shape
    return pl.pallas_call(
        finish_kernel,
        out_shape=jax.ShapeDtypeStruct((cells, slab // 2), bf16),
        in_specs=[pl.BlockSpec(memory_space=pltpu.SMEM)] + [vmem] * 7,
        out_specs=vmem,
        scratch_shapes=[pltpu.VMEM((2 * count, slab // 2), bf16)],
        compiler_params=pltpu.CompilerParams(vmem_limit_bytes=16 * 1024 * 1024),
        cost_estimate=pl.CostEstimate(flops=500_000_000, bytes_accessed=4_000_000, transcendentals=0),
    )(half.reshape(1), rows, keep, taken, inv, stat, gain, spots)


def collect_kernel(cell_ref, returned_ref, audio_ref, vision_ref):
    bf16 = jnp.bfloat16
    count = cell_ref.shape[0]
    cells, half = returned_ref.shape
    audio = audio_ref.shape[0]
    line = lax.broadcasted_iota(jnp.int32, (count, cells), 1)
    for h in range(2):
        hot = jnp.where(line == cell_ref[...] + 4 * h, 1.0, 0.0).astype(bf16)
        value = dot(hot, returned_ref[...]).astype(bf16)
        cols = slice(h * half, (h + 1) * half)
        audio_ref[:, cols] = value[:audio]
        vision_ref[:, cols] = value[audio:]


def collect(cell, returned, audio):
    vmem = pl.BlockSpec(memory_space=pltpu.VMEM)
    count = cell.shape[0]
    width = 2 * returned.shape[1]
    return pl.pallas_call(
        collect_kernel,
        out_shape=(
            jax.ShapeDtypeStruct((audio, width), jnp.bfloat16),
            jax.ShapeDtypeStruct((count - audio, width), jnp.bfloat16),
        ),
        in_specs=[vmem] * 2,
        out_specs=(vmem,) * 2,
        compiler_params=pltpu.CompilerParams(vmem_limit_bytes=12 * 1024 * 1024),
        cost_estimate=pl.CostEstimate(flops=400_000_000, bytes_accessed=2_000_000, transcendentals=0),
    )(cell, returned)


def swap(x):
    return lax.ppermute(x, "tp", [(0, 1), (1, 0)])


def shift(x, axis, k):
    return lax.ppermute(x, axis, [(i, (i + k) % 4) for i in range(4)])


def ranks(dest):
    count = dest.shape[1]
    same = dest[:, :, None] == dest[:, None, :]
    earlier = jnp.arange(count)[None, :] < jnp.arange(count)[:, None]
    return jnp.sum((same & earlier[None]).astype(jnp.int32), axis=2)


def local(
    audio_rows,
    vision_rows,
    audio_weight,
    vision_weight,
    text_rows,
    row_target,
    segment_ids,
    norm_gain,
    qkv_weight,
    attn_grad,
):
    bf16, f32 = jnp.bfloat16, jnp.float32
    t = lax.axis_index("tp")
    e = lax.axis_index("enc")
    j = lax.axis_index(("z", "y"))
    n_enc = 4
    n_seq = 16
    self_index = e * n_seq + j
    senders, enc_rows = row_target.shape
    length, slab = text_rows.shape
    audio_count, audio_width = audio_rows.shape
    vision_count = vision_rows.shape[0]
    merge = vision_weight.shape[1]
    cap = 4
    wide = slab // 128 // n_enc * 128

    piece_a, piece_b, packed = pack(
        jnp.stack([e, t]),
        audio_weight,
        vision_weight,
        audio_rows,
        vision_rows,
    )
    hops = (1, 3, 2)
    along_y = [piece_a] + [shift(piece_a, "y", k) for k in hops]
    along_z = [piece_b] + [shift(piece_b, "z", k) for k in hops]
    along_y, along_z = lax.optimization_barrier((along_y, along_z))
    stack_a, stack_b, row_target = lax.optimization_barrier(
        (jnp.stack(along_y), jnp.stack(along_z), row_target)
    )
    near_a = [shift(stack_a, "z", 1), shift(stack_a, "z", 3)]
    near_b = [shift(stack_b, "y", 1), shift(stack_b, "y", 3)]
    z, y = lax.axis_index("z"), lax.axis_index("y")
    back = jnp.array((0,) + hops, jnp.int32)
    a_at = (((z - back) % 4)[:, None] * 4 + ((y - back) % 4)[None, :]).reshape(-1)
    b_at = (((y - back) % 4)[:, None] + ((z - back) % 4)[None, :] * 4).reshape(-1)
    ah, vh = audio_count // 2, vision_count // 2

    line = row_target.reshape(n_enc, n_seq, enc_rows)[:, j]
    line_dest = line // length
    line_slot = line_dest * (n_enc * cap) + jnp.arange(n_enc)[:, None] * cap + ranks(line_dest)
    a_slot = line_slot[:, :audio_count].reshape(2, 2, 2, ah)
    v_slot = line_slot[:, audio_count:].reshape(2, 2, 2, vh)
    halves = jnp.stack([t, 1 - t])
    a_slot = jnp.moveaxis(a_slot, 2, 1)[:, halves].reshape(2, -1)
    v_slot = jnp.moveaxis(v_slot, 2, 1)[:, halves].reshape(2, -1)
    row_slot = jnp.concatenate([a_slot, v_slot], axis=1)
    cells = row_slot // 16 * 8 + row_slot % 8

    dest = row_target // length
    mine = (dest == self_index).astype(jnp.int32)
    rank_all = jnp.cumsum(mine, axis=1) - 1
    hot = (rank_all[:, :, None] == jnp.arange(cap)[None, None, :]) & (mine[:, :, None] == 1)
    incoming = jnp.sum(jnp.where(hot, (row_target % length)[:, :, None] + 1, 0), axis=1) - 1
    by_line = incoming.reshape(2, 2, n_seq, cap).transpose(0, 2, 1, 3).reshape(2, -1)
    filled = jnp.max(
        (jnp.arange(length)[:, None] == incoming.reshape(1, -1)).astype(jnp.float32), axis=1, keepdims=True
    )
    half = slab // 2
    nowhere = jnp.full_like(incoming, -1)
    spots = jnp.stack(
        [
            jnp.stack([incoming, nowhere], axis=1).reshape(-1),
            jnp.stack([nowhere, incoming], axis=1).reshape(-1),
        ],
        axis=1,
    )
    own_target = lax.dynamic_index_in_dim(row_target, self_index, 0, keepdims=True)
    own_dest = own_target // length
    own_cell = (own_dest * (2 * cap) + ranks(own_dest)).reshape(-1, 1)
    gain = norm_gain.reshape(2, slab)
    seg_row = segment_ids
    seg_col = segment_ids.reshape(length, 1)
    own = lax.all_gather(packed, "enc", axis=0, tiled=False)
    pass_a = [near_a[0][:2], near_a[1][2:]]
    pass_b = [near_b[0][:2], near_b[1][2:]]
    (
        near_a, near_b, pass_a, pass_b, own, cells, by_line, filled, spots, own_cell, gain, seg_col, a_at, b_at
    ) = lax.optimization_barrier(
        (near_a, near_b, pass_a, pass_b, own, cells, by_line, filled, spots, own_cell, gain, seg_col, a_at, b_at)
    )
    far_a = [shift(pass_a[0], "z", 1), shift(pass_a[1], "z", 3)]
    far_b = [shift(pass_b[0], "y", 1), shift(pass_b[1], "y", 3)]
    shards_a = [stack_a] + near_a + far_a
    shards_b = [stack_b] + near_b + far_b
    other = swap(own)
    outgoing = encode(a_at, b_at, shards_a, shards_b, own, other, cells, senders * 8)
    arrived = lax.all_to_all(
        outgoing.reshape(senders, 8, slab // 2), SPREAD, split_axis=0, concat_axis=0, tiled=True
    )
    row_slab = place(by_line, arrived.reshape(senders * 8, slab // 2), text_rows, filled)

    row_slab, qkv_weight, attn_grad = lax.optimization_barrier((row_slab, qkv_weight, attn_grad))
    other_slab = swap(row_slab)
    early, upstream = fetch(qkv_weight, attn_grad)
    give, keep, inv_rms, row_part = attend(
        t, row_slab, other_slab, gain, early, qkv_weight, upstream, seg_row, seg_col
    )
    taken = swap(give)

    out8 = finish(t, row_slab, keep, taken, inv_rms, row_part, gain, spots)
    returned = lax.all_to_all(
        out8.reshape(senders, 2 * cap, half), SPREAD, split_axis=0, concat_axis=0, tiled=True
    )
    return collect(own_cell, returned.reshape(senders * 2 * cap, half), audio_count)


SPREAD = ("enc", "z", "y")


def solution(mesh):
    torus = Mesh(mesh.devices.reshape(4, 4, 4, 2), ("enc", "z", "y", "tp"))
    in_specs = (
        P(SPREAD, None),
        P(SPREAD, None),
        P(("z", "y"), "tp"),
        P(("z", "y"), None, "tp"),
        P(SPREAD, "tp"),
        P(),
        P(SPREAD, None),
        P(),
        P(None, "tp"),
        P(SPREAD, "tp"),
    )
    out_specs = (P(SPREAD, "tp"), P(SPREAD, "tp"))
    return jax.shard_map(local, mesh=torus, in_specs=in_specs, out_specs=out_specs, check_vma=False)
```

```python
import jax
import jax.numpy as jnp
from jax import lax
from jax.experimental import pallas as pl
from jax.experimental.pallas import tpu as pltpu
from jax.sharding import Mesh
from jax.sharding import PartitionSpec as P

HEAD_DIM = 128

epsilon = 1e-06


NT = (((1,), (1,)), ((), ()))
NN = (((1,), (0,)), ((), ()))
TAIL = 128
BIG = 26 * 1024 * 1024


def in_hbm(x):
    return pltpu.with_memory_space_constraint(x, pltpu.HBM)


def dot(x, y, dims=NN):
    return lax.dot_general(x, y, dims, preferred_element_type=jnp.float32)


EARLY = 640


def fetch_kernel(weight_hbm, upstream_hbm, weight_ref, upstream_ref, sems):
    copies = [
        pltpu.make_async_copy(weight_hbm.at[:, :EARLY], weight_ref, sems.at[0]),
        pltpu.make_async_copy(upstream_hbm, upstream_ref, sems.at[1]),
    ]
    for copy in copies:
        copy.start()
    for copy in copies:
        copy.wait()


def fetch(weight, upstream):
    return pl.pallas_call(
        fetch_kernel,
        out_shape=(
            pltpu.VMEM((weight.shape[0], EARLY), weight.dtype),
            pltpu.VMEM(upstream.shape, upstream.dtype),
        ),
        in_specs=[pl.BlockSpec(memory_space=pl.ANY)] * 2,
        out_specs=(pl.BlockSpec(memory_space=pltpu.VMEM),) * 2,
        scratch_shapes=[pltpu.SemaphoreType.DMA((2,))],
        compiler_params=pltpu.CompilerParams(vmem_limit_bytes=1024 * 1024),
        cost_estimate=pl.CostEstimate(flops=0, bytes_accessed=10_000_000, transcendentals=0),
    )(in_hbm(weight), in_hbm(upstream))


def attend_kernel(
    half_ref,
    own_ref,
    other_ref,
    gain_ref,
    early_ref,
    weight_hbm,
    upstream_ref,
    seg_row_ref,
    seg_col_ref,
    give_ref,
    keep_ref,
    inv_ref,
    stat_ref,
    normed_ref,
    unscaled_ref,
    scaled_ref,
    sgrad_ref,
    bias_ref,
    late_ref,
    sem,
):
    bf16, f32 = jnp.bfloat16, jnp.float32
    rows, slab = own_ref.shape
    group = weight_hbm.shape[1]
    heads = group // HEAD_DIM - 2
    split = early_ref.shape[1]
    load = pltpu.make_async_copy(weight_hbm.at[:, split:], late_ref, sem)
    load.start()
    place_u = lax.broadcasted_iota(jnp.int32, (rows, rows), 0)
    place_t = lax.broadcasted_iota(jnp.int32, (rows, rows), 1)
    allowed = (seg_col_ref[...] == seg_row_ref[...]) & (place_u <= place_t)
    bias_ref[...] = jnp.where(allowed, 0.0, -1e30)

    t = half_ref[0]
    own_at = pl.multiple_of(t * slab, HEAD_DIM)
    other_at = pl.multiple_of((1 - t) * slab, HEAD_DIM)
    score_scale = HEAD_DIM ** (-0.5)

    squares = jnp.zeros((rows, HEAD_DIM), f32)
    for part, ref in ((t, own_ref), (1 - t, other_ref)):
        gain = gain_ref[pl.ds(part, 1), :]
        for c in range(0, slab, HEAD_DIM):
            x = ref[:, c : c + HEAD_DIM].astype(f32)
            squares = squares + x * x
            at = pl.multiple_of(part * slab + c, HEAD_DIM)
            normed_ref[:, pl.ds(at, HEAD_DIM)] = (x * gain[:, c : c + HEAD_DIM]).astype(bf16)
    inv = lax.rsqrt(jnp.sum(squares, axis=1, keepdims=True) / (2 * slab) + epsilon)
    inv_ref[...] = inv

    for ref, at, end in ((early_ref, 0, split), (late_ref, split, group)):
        if at:
            load.wait()
        value = dot(normed_ref[...], ref[...])
        unscaled_ref[:, at:end] = value
        scaled_ref[:, at:end] = (value * inv).astype(bf16)

    key = scaled_ref[:, heads * HEAD_DIM : (heads + 1) * HEAD_DIM]
    val = scaled_ref[:, (heads + 1) * HEAD_DIM :]
    grad_key = jnp.zeros((rows, HEAD_DIM), f32)
    grad_val = jnp.zeros((rows, HEAD_DIM), f32)
    stat = jnp.zeros((rows, HEAD_DIM), f32)
    for h in range(heads):
        cols = slice(h * HEAD_DIM, (h + 1) * HEAD_DIM)
        query = scaled_ref[:, cols]
        up = upstream_ref[:, cols]
        scores = dot(key, query, NT) * score_scale + bias_ref[...]
        scores = jnp.exp(scores - jnp.max(scores, axis=0, keepdims=True))
        probs = scores * (1.0 / jnp.sum(scores, axis=0, keepdims=True))
        dprobs = dot(val, up, NT)
        delta = jnp.sum(probs * dprobs, axis=0, keepdims=True)
        sgrad = (probs * (dprobs - delta) * score_scale).astype(bf16)
        grad_val = grad_val + dot(probs.astype(bf16), up)
        grad_key = grad_key + dot(sgrad, query)
        grad_query = dot(sgrad.T, key)
        stat = stat + grad_query * unscaled_ref[:, cols]
        sgrad_ref[:, cols] = (grad_query * inv).astype(bf16)
    cols = slice(heads * HEAD_DIM, (heads + 1) * HEAD_DIM)
    stat = stat + grad_key * unscaled_ref[:, cols]
    sgrad_ref[:, cols] = (grad_key * inv).astype(bf16)
    cols = slice((heads + 1) * HEAD_DIM, (heads + 2) * HEAD_DIM)
    stat = stat + grad_val * unscaled_ref[:, cols]
    sgrad_ref[:, cols] = (grad_val * inv).astype(bf16)
    total = jnp.sum(stat, axis=1, keepdims=True)
    stat_ref[...] = total
    lane = lax.broadcasted_iota(jnp.int32, (rows, TAIL), 1)
    high = total.astype(bf16)
    low = (total - high.astype(f32)).astype(bf16)
    give_ref[:, slab:] = jnp.where(lane == 0, high.astype(f32), low.astype(f32)).astype(bf16)


    def back(at):
        rows_at = pl.ds(at, slab)
        return (
            dot(sgrad_ref[:, :split], early_ref[rows_at, :], NT)
            + dot(sgrad_ref[:, split:], late_ref[rows_at, :], NT)
        ).astype(bf16)

    keep_ref[...] = back(own_at)
    give_ref[:, :slab] = back(other_at)


def attend(half, own, other, gain, early, qkv_weight, upstream, seg_row, seg_col):
    rows, slab = own.shape
    group = qkv_weight.shape[1]
    f32, bf16 = jnp.float32, jnp.bfloat16
    vmem = pl.BlockSpec(memory_space=pltpu.VMEM)
    anywhere = pl.BlockSpec(memory_space=pl.ANY)
    return pl.pallas_call(
        attend_kernel,
        out_shape=(
            jax.ShapeDtypeStruct((rows, slab + TAIL), bf16),
            jax.ShapeDtypeStruct((rows, slab), bf16),
            jax.ShapeDtypeStruct((rows, 1), f32),
            jax.ShapeDtypeStruct((rows, 1), f32),
        ),
        in_specs=[pl.BlockSpec(memory_space=pltpu.SMEM), vmem, vmem, vmem]
        + [vmem, anywhere, vmem, vmem, vmem],
        out_specs=(vmem,) * 4,
        scratch_shapes=[
            pltpu.VMEM((rows, 2 * slab), bf16),
            pltpu.VMEM((rows, group), f32),
            pltpu.VMEM((rows, group), bf16),
            pltpu.VMEM((rows, group), bf16),
            pltpu.VMEM((rows, rows), f32),
            pltpu.VMEM((2 * slab, group - early.shape[1]), bf16),
            pltpu.SemaphoreType.DMA,
        ],
        compiler_params=pltpu.CompilerParams(vmem_limit_bytes=BIG),
        cost_estimate=pl.CostEstimate(flops=5_000_000_000, bytes_accessed=14_000_000, transcendentals=500_000),
    )(
        half.reshape(1),
        own,
        other,
        gain,
        early,
        in_hbm(qkv_weight),
        upstream,
        seg_row,
        seg_col,
    )


def roll_half(x):
    return pltpu.roll(x.astype(jnp.float32), 64, 1).astype(x.dtype)


A_ROWS, A_TAIL = 192, 32
B_ROWS, B_TAIL = 208, 48
A_PIECE = A_ROWS + A_TAIL
B_PIECE = B_ROWS + B_TAIL


def pack_kernel(
    place_ref,
    audio_w_ref,
    vision_w_ref,
    audio_ref,
    vision_ref,
    a_ref,
    b_ref,
    rows_ref,
    am_ref,
    at_ref,
    vm_ref,
    vt_ref,
    sems,
    row_sems,
):
    e = place_ref[0]
    t = place_ref[1]
    main_at = pl.multiple_of(e * 384, 128)
    tail_at = pl.multiple_of(1536 + e // 2 * 128, 128)
    loads = [
        pltpu.make_async_copy(vision_w_ref.at[:, :, pl.ds(main_at, 384)], vm_ref, sems.at[0]),
        pltpu.make_async_copy(vision_w_ref.at[:, :, pl.ds(tail_at, 128)], vt_ref, sems.at[1]),
        pltpu.make_async_copy(audio_w_ref.at[:, pl.ds(main_at, 384)], am_ref, sems.at[2]),
        pltpu.make_async_copy(audio_w_ref.at[:, pl.ds(tail_at, 128)], at_ref, sems.at[3]),
    ]
    for copy in loads:
        copy.start()
    width = rows_ref.shape[1]
    ah, vh = audio_ref.shape[0] // 2, vision_ref.shape[0] // 2
    copies = [
        pltpu.make_async_copy(
            audio_ref.at[pl.ds(pl.multiple_of(t * ah, 16), ah), :], rows_ref.at[:ah], row_sems.at[0]
        )
    ] + [
        pltpu.make_async_copy(
            vision_ref.at[pl.ds(pl.multiple_of(t * vh, 16), vh), i * width : (i + 1) * width],
            rows_ref.at[ah + i * vh : ah + (i + 1) * vh],
            row_sems.at[1 + i],
        )
        for i in range(4)
    ]
    for copy in copies:
        copy.start()
    for copy in loads:
        copy.wait()
    k = am_ref.shape[0]
    cut = A_ROWS - k
    vision_main = vm_ref[...].reshape(4 * k, 384)
    a_ref[:k, :] = am_ref[...]
    a_ref[k:A_ROWS, :] = vision_main[:cut]
    b_ref[:B_ROWS, :] = vision_main[cut:]
    odd = e % 2 == 1
    vision_tail = vt_ref[...].reshape(4 * k, 128)
    tail = jnp.concatenate([at_ref[...], vision_tail], axis=0).astype(jnp.float32)
    moved = pltpu.roll(tail, 64, 1)
    first = jnp.where(odd, moved, tail)
    second = jnp.where(odd, tail, moved)
    lane = lax.broadcasted_iota(jnp.int32, (B_TAIL, 128), 1)
    for q in range(3):
        cols = slice(q * 128, (q + 1) * 128)
        low = first[q * A_TAIL : (q + 1) * A_TAIL]
        high = second[96 + q * A_TAIL : 96 + (q + 1) * A_TAIL]
        a_ref[A_ROWS:, cols] = jnp.where(lane[:A_TAIL] < 64, low, high).astype(a_ref.dtype)
    base = A_ROWS
    for q in range(2):
        cols = slice(q * 128, (q + 1) * 128)
        low = first[base + q * B_TAIL : base + (q + 1) * B_TAIL]
        high = second[base + 112 + q * B_TAIL : base + 112 + (q + 1) * B_TAIL]
        b_ref[B_ROWS:, cols] = jnp.where(lane < 64, low, high).astype(b_ref.dtype)
    b_ref[B_ROWS : B_ROWS + 16, 256:] = first[base + 96 : base + 112].astype(b_ref.dtype)
    b_ref[B_ROWS + 16 :, 256:] = jnp.zeros((B_TAIL - 16, 128), b_ref.dtype)
    for copy in copies:
        copy.wait()


def pack(where, audio_weight, vision_weight, audio_rows, vision_rows):
    bf16 = jnp.bfloat16
    vmem = pl.BlockSpec(memory_space=pltpu.VMEM)
    anywhere = pl.BlockSpec(memory_space=pl.ANY)
    k = audio_weight.shape[0]
    return pl.pallas_call(
        pack_kernel,
        out_shape=(
            jax.ShapeDtypeStruct((A_PIECE, 384), bf16),
            jax.ShapeDtypeStruct((B_PIECE, 384), bf16),
            jax.ShapeDtypeStruct(
                (audio_rows.shape[0] // 2 + 2 * vision_rows.shape[0], audio_rows.shape[1]), bf16
            ),
        ),
        in_specs=[pl.BlockSpec(memory_space=pltpu.SMEM)] + [anywhere] * 4,
        out_specs=(vmem, vmem, vmem),
        scratch_shapes=[
            pltpu.VMEM((k, 384), bf16),
            pltpu.VMEM((k, 128), bf16),
            pltpu.VMEM((k, 4, 384), bf16),
            pltpu.VMEM((k, 4, 128), bf16),
            pltpu.SemaphoreType.DMA((4,)),
            pltpu.SemaphoreType.DMA((5,)),
        ],
        compiler_params=pltpu.CompilerParams(vmem_limit_bytes=BIG),
        cost_estimate=pl.CostEstimate(flops=0, bytes_accessed=1_800_000, transcendentals=0),
    )(where, in_hbm(audio_weight), in_hbm(vision_weight), in_hbm(audio_rows), in_hbm(vision_rows))


def encode_kernel(
    a_at_ref,
    b_at_ref,
    ga0,
    ga1,
    ga2,
    ga3,
    ga4,
    gb0,
    gb1,
    gb2,
    gb3,
    gb4,
    own_ref,
    other_ref,
    cell_ref,
    out_ref,
    wa_ref,
    wv_ref,
    ta_ref,
    tv_ref,
    x_ref,
    enc_ref,
    sems,
):
    bf16, f32 = jnp.bfloat16, jnp.float32
    audio_width = x_ref.shape[2]
    audio_k = wa_ref.shape[1]
    cut = A_ROWS - audio_k
    sources = ((ga0, gb0, 0, 4), (ga1, gb1, 4, 4), (ga2, gb2, 8, 4), (ga3, gb3, 12, 2), (ga4, gb4, 14, 2))
    own_copy = pltpu.make_async_copy(own_ref, x_ref, sems.at[0])
    own_copy.start()

    for ga, gb, start, size in sources:

        @pl.loop(0, size)
        def _(n):
            at = a_at_ref[start + n]
            wa_ref[at] = ga[n, :audio_k, :]
            wv_ref[at, :cut, :] = ga[n, audio_k:A_ROWS, :]
            ta = jnp.concatenate([ga[n, A_ROWS:, q * 128 : (q + 1) * 128] for q in range(3)], axis=0)
            ta_ref[at] = ta[:audio_k]
            tv_ref[at, : 96 - audio_k, :] = ta[audio_k:]
            tv_ref[at, 96 - audio_k : cut, :] = roll_half(ta)
            at = b_at_ref[start + n]
            wv_ref[at, cut:, :] = gb[n, :B_ROWS, :]
            tb = jnp.concatenate([gb[n, B_ROWS:, q * 128 : (q + 1) * 128] for q in range(2)], axis=0)
            tv_ref[at, cut : cut + 96, :] = tb
            tv_ref[at, cut + 96 : cut + 112, :] = gb[n, B_ROWS : B_ROWS + 16, 256:]
            tv_ref[at, cut + 112 :, :] = roll_half(tb)

    count = cell_ref.shape[1]
    cells = out_ref.shape[0]
    line = lax.broadcasted_iota(jnp.int32, (cells, count), 0)
    first = jnp.where(line == cell_ref[0:1, :], 1.0, 0.0).astype(bf16)
    second = jnp.where(line == cell_ref[1:2, :], 1.0, 0.0).astype(bf16)

    halves, n_enc = 2, x_ref.shape[0]
    audio = 64
    vision = 32
    n_vision = halves * n_enc * vision

    def weights(main, last):
        size = main.shape[0] * main.shape[1]
        return jnp.concatenate([main.reshape(size, 384), last.reshape(size, 128)], axis=1)

    def keep_rows(value, base, each):
        run = 2 * each
        for h in range(2):
            for g in range(2):
                at = g * count + base + h * run
                enc_ref[at : at + run, :] = value[(2 * h + g) * run : (2 * h + g + 1) * run]

    def rows(at, each):
        parts = [ref[:, at : at + each, :].reshape(n_enc * each, audio_width) for ref in (x_ref, other_ref)]
        return jnp.concatenate(parts, axis=0)

    own_copy.wait()
    keep_rows(dot(rows(0, audio), weights(wa_ref[...], ta_ref[...])).astype(bf16), 0, audio)
    total = jnp.zeros((n_vision, 512), f32)
    for i in range(4):
        part = weights(wv_ref[4 * i : 4 * i + 4], tv_ref[4 * i : 4 * i + 4])
        total = total + dot(rows(audio + i * vision, vision), part)
    keep_rows(total.astype(bf16), 4 * audio, vision)

    out_ref[:, :384] = dot(first, enc_ref[:count, :384]).astype(bf16)
    out_ref[:, 384:768] = dot(second, enc_ref[count:, :384]).astype(bf16)
    low = dot(first, enc_ref[:count, 384:])
    high = dot(second, enc_ref[count:, 384:])
    lane = lax.broadcasted_iota(jnp.int32, low.shape, 1)
    out_ref[:, 768:] = jnp.where(lane < 64, low, pltpu.roll(high, 64, 1)).astype(bf16)


def encode(a_at, b_at, shards_a, shards_b, own, other, cells, n_cells):
    bf16 = jnp.bfloat16
    n_enc, rows, width = own.shape
    smem = pl.BlockSpec(memory_space=pltpu.SMEM)
    vmem = pl.BlockSpec(memory_space=pltpu.VMEM)
    anywhere = pl.BlockSpec(memory_space=pl.ANY)
    k = width // 16
    return pl.pallas_call(
        encode_kernel,
        out_shape=jax.ShapeDtypeStruct((n_cells, 896), bf16),
        in_specs=[smem, smem] + [vmem] * 10 + [anywhere] + [vmem] * 2,
        out_specs=vmem,
        scratch_shapes=[
            pltpu.VMEM((16, k, 384), bf16),
            pltpu.VMEM((16, 4 * k, 384), bf16),
            pltpu.VMEM((16, k, 128), bf16),
            pltpu.VMEM((16, 4 * k, 128), bf16),
            pltpu.VMEM((n_enc, rows, width), bf16),
            pltpu.VMEM((2 * cells.shape[1], 512), bf16),
            pltpu.SemaphoreType.DMA((1,)),
        ],
        compiler_params=pltpu.CompilerParams(vmem_limit_bytes=BIG),
        cost_estimate=pl.CostEstimate(
            flops=3_000_000_000, bytes_accessed=11_000_000, transcendentals=0
        ),
    )(a_at, b_at, *shards_a, *shards_b, in_hbm(own), other, cells)


def cut_kernel(a0, a1, b0, b1, low_a, high_a, low_b, high_b):
    low_a[...] = a0[:2]
    high_a[...] = a1[2:]
    low_b[...] = b0[:2]
    high_b[...] = b1[2:]


def cut(near_a, near_b):
    vmem = pl.BlockSpec(memory_space=pltpu.VMEM)
    shapes = [(2,) + x.shape[1:] for x in near_a + near_b]
    halves = pl.pallas_call(
        cut_kernel,
        out_shape=[jax.ShapeDtypeStruct(shape, jnp.bfloat16) for shape in shapes],
        in_specs=[vmem] * 4,
        out_specs=[vmem] * 4,
        compiler_params=pltpu.CompilerParams(vmem_limit_bytes=8 * 1024 * 1024),
        cost_estimate=pl.CostEstimate(flops=0, bytes_accessed=3_000_000, transcendentals=0),
    )(*near_a, *near_b)
    return halves[:2], halves[2:]


def place_kernel(e_row_ref, arrived_ref, text_hbm, filled_ref, out_ref, text_ref, sem):
    bf16, f32 = jnp.bfloat16, jnp.float32
    load = pltpu.make_async_copy(text_hbm, text_ref, sem)
    load.start()
    rows = out_ref.shape[0]
    each = arrived_ref.shape[0] // 4
    line = lax.broadcasted_iota(jnp.int32, (rows, each), 0)
    first = jnp.where(line == e_row_ref[0:1, :], 1.0, 0.0).astype(bf16)
    second = jnp.where(line == e_row_ref[1:2, :], 1.0, 0.0).astype(bf16)
    both = jnp.concatenate([first, second], axis=1)
    taken = filled_ref[...] > 0.5
    lane = lax.broadcasted_iota(jnp.int32, (rows, 128), 1)
    low = []
    high = []
    load.wait()
    for e in range(4):
        at = slice(e * each, (e + 1) * each)
        main = jnp.concatenate([arrived_ref[at, :384], arrived_ref[at, 384:768]], axis=0)
        cols = slice(e * 384, (e + 1) * 384)
        text = text_ref[:, cols].astype(f32)
        out_ref[:, cols] = jnp.where(taken, dot(both, main), text).astype(bf16)
        last = arrived_ref[at, 768:]
        low.append(dot(first, last))
        high.append(dot(second, last))
    for q in range(2):
        left = low[2 * q] + pltpu.roll(high[2 * q], 64, 1)
        right = pltpu.roll(low[2 * q + 1], 64, 1) + high[2 * q + 1]
        cols = slice(1536 + q * 128, 1536 + (q + 1) * 128)
        text = text_ref[:, cols].astype(f32)
        out_ref[:, cols] = jnp.where(taken, jnp.where(lane < 64, left, right), text).astype(bf16)


def place(spots, arrived, text, filled):
    vmem = pl.BlockSpec(memory_space=pltpu.VMEM)
    return pl.pallas_call(
        place_kernel,
        out_shape=jax.ShapeDtypeStruct(text.shape, text.dtype),
        in_specs=[vmem, vmem, pl.BlockSpec(memory_space=pl.ANY), vmem],
        out_specs=vmem,
        scratch_shapes=[pltpu.VMEM(text.shape, text.dtype), pltpu.SemaphoreType.DMA],
        compiler_params=pltpu.CompilerParams(vmem_limit_bytes=12 * 1024 * 1024),
        cost_estimate=pl.CostEstimate(flops=300_000_000, bytes_accessed=3_000_000, transcendentals=0),
    )(spots, arrived, text, filled)


def finish_kernel(
    half_ref,
    rows_ref,
    keep_ref,
    taken_ref,
    inv_ref,
    stat_ref,
    gain_ref,
    spot_ref,
    out_ref,
    grad_ref,
):
    bf16, f32 = jnp.bfloat16, jnp.float32
    rows, slab = rows_ref.shape
    cells = out_ref.shape[0]
    half = slab // 2
    inv = inv_ref[...]
    gain = gain_ref[pl.ds(half_ref[0], 1), :]
    line = lax.broadcasted_iota(jnp.int32, (cells, rows), 1)
    first = jnp.where(line == spot_ref[:, 0:1], 1.0, 0.0).astype(bf16)
    second = jnp.where(line == spot_ref[:, 1:2], 1.0, 0.0).astype(bf16)
    both = jnp.concatenate([first, second], axis=1)
    sent = taken_ref[:, slab:].astype(f32)
    stat = stat_ref[...] + sent[:, 0:1] + sent[:, 1:2]
    factor = inv * inv * inv / (2 * slab) * stat
    for c in range(0, slab, 128):
        cols = slice(c, c + 128)
        total = keep_ref[:, cols].astype(f32) + taken_ref[:, cols].astype(f32)
        value = (gain[:, cols] * total - rows_ref[:, cols].astype(f32) * factor).astype(bf16)
        at = c // half
        grad_ref[at * rows : (at + 1) * rows, c - at * half : c - at * half + 128] = value
    out_ref[...] = dot(both, grad_ref[...]).astype(bf16)


def finish(half, rows, keep, taken, inv, stat, gain, spots):
    bf16 = jnp.bfloat16
    vmem = pl.BlockSpec(memory_space=pltpu.VMEM)
    cells = spots.shape[0]
    count, slab = rows.shape
    return pl.pallas_call(
        finish_kernel,
        out_shape=jax.ShapeDtypeStruct((cells, slab // 2), bf16),
        in_specs=[pl.BlockSpec(memory_space=pltpu.SMEM)] + [vmem] * 7,
        out_specs=vmem,
        scratch_shapes=[pltpu.VMEM((2 * count, slab // 2), bf16)],
        compiler_params=pltpu.CompilerParams(vmem_limit_bytes=16 * 1024 * 1024),
        cost_estimate=pl.CostEstimate(flops=500_000_000, bytes_accessed=4_000_000, transcendentals=0),
    )(half.reshape(1), rows, keep, taken, inv, stat, gain, spots)


def collect_kernel(cell_ref, returned_ref, audio_ref, vision_ref):
    bf16 = jnp.bfloat16
    count = cell_ref.shape[0]
    cells, half = returned_ref.shape
    audio = audio_ref.shape[0]
    line = lax.broadcasted_iota(jnp.int32, (count, cells), 1)
    for h in range(2):
        hot = jnp.where(line == cell_ref[...] + 4 * h, 1.0, 0.0).astype(bf16)
        value = dot(hot, returned_ref[...]).astype(bf16)
        cols = slice(h * half, (h + 1) * half)
        audio_ref[:, cols] = value[:audio]
        vision_ref[:, cols] = value[audio:]


def collect(cell, returned, audio):
    vmem = pl.BlockSpec(memory_space=pltpu.VMEM)
    count = cell.shape[0]
    width = 2 * returned.shape[1]
    return pl.pallas_call(
        collect_kernel,
        out_shape=(
            jax.ShapeDtypeStruct((audio, width), jnp.bfloat16),
            jax.ShapeDtypeStruct((count - audio, width), jnp.bfloat16),
        ),
        in_specs=[vmem] * 2,
        out_specs=(vmem,) * 2,
        compiler_params=pltpu.CompilerParams(vmem_limit_bytes=12 * 1024 * 1024),
        cost_estimate=pl.CostEstimate(flops=400_000_000, bytes_accessed=2_000_000, transcendentals=0),
    )(cell, returned)


def swap(x):
    return lax.ppermute(x, "tp", [(0, 1), (1, 0)])


def shift(x, axis, k):
    return lax.ppermute(x, axis, [(i, (i + k) % 4) for i in range(4)])


def ranks(dest):
    count = dest.shape[1]
    same = dest[:, :, None] == dest[:, None, :]
    earlier = jnp.arange(count)[None, :] < jnp.arange(count)[:, None]
    return jnp.sum((same & earlier[None]).astype(jnp.int32), axis=2)


def local(
    audio_rows,
    vision_rows,
    audio_weight,
    vision_weight,
    text_rows,
    row_target,
    segment_ids,
    norm_gain,
    qkv_weight,
    attn_grad,
):
    bf16, f32 = jnp.bfloat16, jnp.float32
    t = lax.axis_index("tp")
    e = lax.axis_index("enc")
    j = lax.axis_index(("z", "y"))
    n_enc = 4
    n_seq = 16
    self_index = e * n_seq + j
    senders, enc_rows = row_target.shape
    length, slab = text_rows.shape
    audio_count, audio_width = audio_rows.shape
    vision_count = vision_rows.shape[0]
    merge = vision_weight.shape[1]
    cap = 4
    wide = slab // 128 // n_enc * 128

    piece_a, piece_b, packed = pack(
        jnp.stack([e, t]),
        audio_weight,
        vision_weight,
        audio_rows,
        vision_rows,
    )
    hops = (1, 3, 2)
    across_y, across_z = shift(piece_a, "y", 2), shift(piece_b, "z", 2)
    along_y = [piece_a, shift(piece_a, "y", 1), shift(piece_a, "y", 3), across_y]
    along_z = [piece_b, shift(piece_b, "z", 1), shift(piece_b, "z", 3), across_z]
    along_y, along_z = lax.optimization_barrier((along_y, along_z))
    stack_a, stack_b, row_target = lax.optimization_barrier(
        (jnp.stack(along_y), jnp.stack(along_z), row_target)
    )
    near_a = [shift(stack_a, "z", 1), shift(stack_a, "z", 3)]
    near_b = [shift(stack_b, "y", 1), shift(stack_b, "y", 3)]
    z, y = lax.axis_index("z"), lax.axis_index("y")
    back = jnp.array((0,) + hops, jnp.int32)
    a_at = (((z - back) % 4)[:, None] * 4 + ((y - back) % 4)[None, :]).reshape(-1)
    b_at = (((y - back) % 4)[:, None] + ((z - back) % 4)[None, :] * 4).reshape(-1)
    ah, vh = audio_count // 2, vision_count // 2

    line = row_target.reshape(n_enc, n_seq, enc_rows)[:, j]
    line_dest = line // length
    line_slot = line_dest * (n_enc * cap) + jnp.arange(n_enc)[:, None] * cap + ranks(line_dest)
    a_slot = line_slot[:, :audio_count].reshape(2, 2, 2, ah)
    v_slot = line_slot[:, audio_count:].reshape(2, 2, 2, vh)
    halves = jnp.stack([t, 1 - t])
    a_slot = jnp.moveaxis(a_slot, 2, 1)[:, halves].reshape(2, -1)
    v_slot = jnp.moveaxis(v_slot, 2, 1)[:, halves].reshape(2, -1)
    row_slot = jnp.concatenate([a_slot, v_slot], axis=1)
    cells = row_slot // 16 * 8 + row_slot % 8

    dest = row_target // length
    mine = (dest == self_index).astype(jnp.int32)
    rank_all = jnp.cumsum(mine, axis=1) - 1
    hot = (rank_all[:, :, None] == jnp.arange(cap)[None, None, :]) & (mine[:, :, None] == 1)
    incoming = jnp.sum(jnp.where(hot, (row_target % length)[:, :, None] + 1, 0), axis=1) - 1
    by_line = incoming.reshape(2, 2, n_seq, cap).transpose(0, 2, 1, 3).reshape(2, -1)
    filled = jnp.max(
        (jnp.arange(length)[:, None] == incoming.reshape(1, -1)).astype(jnp.float32), axis=1, keepdims=True
    )
    half = slab // 2
    nowhere = jnp.full_like(incoming, -1)
    spots = jnp.stack(
        [
            jnp.stack([incoming, nowhere], axis=1).reshape(-1),
            jnp.stack([nowhere, incoming], axis=1).reshape(-1),
        ],
        axis=1,
    )
    own_target = lax.dynamic_index_in_dim(row_target, self_index, 0, keepdims=True)
    own_dest = own_target // length
    own_cell = (own_dest * (2 * cap) + ranks(own_dest)).reshape(-1, 1)
    gain = norm_gain.reshape(2, slab)
    seg_row = segment_ids
    seg_col = segment_ids.reshape(length, 1)
    own = lax.all_gather(packed, "enc", axis=0, tiled=False)
    pass_a, pass_b = cut(near_a, near_b)
    (
        near_a, near_b, pass_a, pass_b, own, cells, by_line, filled, spots, own_cell, gain, seg_col, a_at, b_at
    ) = lax.optimization_barrier(
        (near_a, near_b, pass_a, pass_b, own, cells, by_line, filled, spots, own_cell, gain, seg_col, a_at, b_at)
    )
    far_a = [shift(pass_a[0], "z", 1), shift(pass_a[1], "z", 3)]
    far_b = [shift(pass_b[0], "y", 1), shift(pass_b[1], "y", 3)]
    shards_a = [stack_a] + near_a + far_a
    shards_b = [stack_b] + near_b + far_b
    other = swap(own)
    outgoing = encode(a_at, b_at, shards_a, shards_b, own, other, cells, senders * 8)
    arrived = lax.all_to_all(
        outgoing.reshape(senders, 8, slab // 2), SPREAD, split_axis=0, concat_axis=0, tiled=True
    )
    row_slab = place(by_line, arrived.reshape(senders * 8, slab // 2), text_rows, filled)

    row_slab, qkv_weight, attn_grad = lax.optimization_barrier((row_slab, qkv_weight, attn_grad))
    other_slab = swap(row_slab)
    early, upstream = fetch(qkv_weight, attn_grad)
    give, keep, inv_rms, row_part = attend(
        t, row_slab, other_slab, gain, early, qkv_weight, upstream, seg_row, seg_col
    )
    taken = swap(give)

    out8 = finish(t, row_slab, keep, taken, inv_rms, row_part, gain, spots)
    returned = lax.all_to_all(
        out8.reshape(senders, 2 * cap, half), SPREAD, split_axis=0, concat_axis=0, tiled=True
    )
    return collect(own_cell, returned.reshape(senders * 2 * cap, half), audio_count)


SPREAD = ("enc", "z", "y")


def solution(mesh):
    torus = Mesh(mesh.devices.reshape(4, 4, 4, 2), ("enc", "z", "y", "tp"))
    in_specs = (
        P(SPREAD, None),
        P(SPREAD, None),
        P(("z", "y"), "tp"),
        P(("z", "y"), None, "tp"),
        P(SPREAD, "tp"),
        P(),
        P(SPREAD, None),
        P(),
        P(None, "tp"),
        P(SPREAD, "tp"),
    )
    out_specs = (P(SPREAD, "tp"), P(SPREAD, "tp"))
    return jax.shard_map(local, mesh=torus, in_specs=in_specs, out_specs=out_specs, check_vma=False)
```

```python
import jax
import jax.numpy as jnp
from jax import lax
from jax.experimental import pallas as pl
from jax.experimental.pallas import tpu as pltpu
from jax.sharding import Mesh
from jax.sharding import PartitionSpec as P

HEAD_DIM = 128

epsilon = 1e-06


NT = (((1,), (1,)), ((), ()))
NN = (((1,), (0,)), ((), ()))
TAIL = 128
BIG = 26 * 1024 * 1024


def in_hbm(x):
    return pltpu.with_memory_space_constraint(x, pltpu.HBM)


def dot(x, y, dims=NN):
    return lax.dot_general(x, y, dims, preferred_element_type=jnp.float32)


EARLY = 640


def fetch_kernel(weight_hbm, upstream_hbm, weight_ref, upstream_ref, sems):
    copies = [
        pltpu.make_async_copy(weight_hbm.at[:, :EARLY], weight_ref, sems.at[0]),
        pltpu.make_async_copy(upstream_hbm, upstream_ref, sems.at[1]),
    ]
    for copy in copies:
        copy.start()
    for copy in copies:
        copy.wait()


def fetch(weight, upstream):
    return pl.pallas_call(
        fetch_kernel,
        out_shape=(
            pltpu.VMEM((weight.shape[0], EARLY), weight.dtype),
            pltpu.VMEM(upstream.shape, upstream.dtype),
        ),
        in_specs=[pl.BlockSpec(memory_space=pl.ANY)] * 2,
        out_specs=(pl.BlockSpec(memory_space=pltpu.VMEM),) * 2,
        scratch_shapes=[pltpu.SemaphoreType.DMA((2,))],
        compiler_params=pltpu.CompilerParams(vmem_limit_bytes=1024 * 1024),
        cost_estimate=pl.CostEstimate(flops=0, bytes_accessed=10_000_000, transcendentals=0),
    )(in_hbm(weight), in_hbm(upstream))


def attend_kernel(
    half_ref,
    own_ref,
    other_ref,
    gain_ref,
    early_ref,
    weight_hbm,
    upstream_ref,
    seg_row_ref,
    seg_col_ref,
    give_ref,
    keep_ref,
    inv_ref,
    stat_ref,
    normed_ref,
    unscaled_ref,
    scaled_ref,
    sgrad_ref,
    bias_ref,
    late_ref,
    sem,
):
    bf16, f32 = jnp.bfloat16, jnp.float32
    rows, slab = own_ref.shape
    group = weight_hbm.shape[1]
    heads = group // HEAD_DIM - 2
    split = early_ref.shape[1]
    load = pltpu.make_async_copy(weight_hbm.at[:, split:], late_ref, sem)
    load.start()
    place_u = lax.broadcasted_iota(jnp.int32, (rows, rows), 0)
    place_t = lax.broadcasted_iota(jnp.int32, (rows, rows), 1)
    allowed = (seg_col_ref[...] == seg_row_ref[...]) & (place_u <= place_t)
    bias_ref[...] = jnp.where(allowed, 0.0, -1e30)

    t = half_ref[0]
    own_at = pl.multiple_of(t * slab, HEAD_DIM)
    other_at = pl.multiple_of((1 - t) * slab, HEAD_DIM)
    score_scale = HEAD_DIM ** (-0.5)

    squares = jnp.zeros((rows, HEAD_DIM), f32)
    for part, ref in ((t, own_ref), (1 - t, other_ref)):
        gain = gain_ref[pl.ds(part, 1), :]
        for c in range(0, slab, HEAD_DIM):
            x = ref[:, c : c + HEAD_DIM].astype(f32)
            squares = squares + x * x
            at = pl.multiple_of(part * slab + c, HEAD_DIM)
            normed_ref[:, pl.ds(at, HEAD_DIM)] = (x * gain[:, c : c + HEAD_DIM]).astype(bf16)
    inv = lax.rsqrt(jnp.sum(squares, axis=1, keepdims=True) / (2 * slab) + epsilon)
    inv_ref[...] = inv

    for ref, at, end in ((early_ref, 0, split), (late_ref, split, group)):
        if at:
            load.wait()
        value = dot(normed_ref[...], ref[...])
        unscaled_ref[:, at:end] = value
        scaled_ref[:, at:end] = (value * inv).astype(bf16)

    key = scaled_ref[:, heads * HEAD_DIM : (heads + 1) * HEAD_DIM]
    val = scaled_ref[:, (heads + 1) * HEAD_DIM :]
    grad_key = jnp.zeros((rows, HEAD_DIM), f32)
    grad_val = jnp.zeros((rows, HEAD_DIM), f32)
    stat = jnp.zeros((rows, HEAD_DIM), f32)
    for h in range(heads):
        cols = slice(h * HEAD_DIM, (h + 1) * HEAD_DIM)
        query = scaled_ref[:, cols]
        up = upstream_ref[:, cols]
        scores = dot(key, query, NT) * score_scale + bias_ref[...]
        scores = jnp.exp(scores - jnp.max(scores, axis=0, keepdims=True))
        probs = scores * (1.0 / jnp.sum(scores, axis=0, keepdims=True))
        dprobs = dot(val, up, NT)
        delta = jnp.sum(probs * dprobs, axis=0, keepdims=True)
        sgrad = (probs * (dprobs - delta) * score_scale).astype(bf16)
        grad_val = grad_val + dot(probs.astype(bf16), up)
        grad_key = grad_key + dot(sgrad, query)
        grad_query = dot(sgrad.T, key)
        stat = stat + grad_query * unscaled_ref[:, cols]
        sgrad_ref[:, cols] = (grad_query * inv).astype(bf16)
    cols = slice(heads * HEAD_DIM, (heads + 1) * HEAD_DIM)
    stat = stat + grad_key * unscaled_ref[:, cols]
    sgrad_ref[:, cols] = (grad_key * inv).astype(bf16)
    cols = slice((heads + 1) * HEAD_DIM, (heads + 2) * HEAD_DIM)
    stat = stat + grad_val * unscaled_ref[:, cols]
    sgrad_ref[:, cols] = (grad_val * inv).astype(bf16)
    total = jnp.sum(stat, axis=1, keepdims=True)
    stat_ref[...] = total
    lane = lax.broadcasted_iota(jnp.int32, (rows, TAIL), 1)
    high = total.astype(bf16)
    low = (total - high.astype(f32)).astype(bf16)
    give_ref[:, slab:] = jnp.where(lane == 0, high.astype(f32), low.astype(f32)).astype(bf16)


    def back(at):
        rows_at = pl.ds(at, slab)
        return (
            dot(sgrad_ref[:, :split], early_ref[rows_at, :], NT)
            + dot(sgrad_ref[:, split:], late_ref[rows_at, :], NT)
        ).astype(bf16)

    keep_ref[...] = back(own_at)
    give_ref[:, :slab] = back(other_at)


def attend(half, own, other, gain, early, qkv_weight, upstream, seg_row, seg_col):
    rows, slab = own.shape
    group = qkv_weight.shape[1]
    f32, bf16 = jnp.float32, jnp.bfloat16
    vmem = pl.BlockSpec(memory_space=pltpu.VMEM)
    anywhere = pl.BlockSpec(memory_space=pl.ANY)
    return pl.pallas_call(
        attend_kernel,
        out_shape=(
            jax.ShapeDtypeStruct((rows, slab + TAIL), bf16),
            jax.ShapeDtypeStruct((rows, slab), bf16),
            jax.ShapeDtypeStruct((rows, 1), f32),
            jax.ShapeDtypeStruct((rows, 1), f32),
        ),
        in_specs=[pl.BlockSpec(memory_space=pltpu.SMEM), vmem, vmem, vmem]
        + [vmem, anywhere, vmem, vmem, vmem],
        out_specs=(vmem,) * 4,
        scratch_shapes=[
            pltpu.VMEM((rows, 2 * slab), bf16),
            pltpu.VMEM((rows, group), f32),
            pltpu.VMEM((rows, group), bf16),
            pltpu.VMEM((rows, group), bf16),
            pltpu.VMEM((rows, rows), f32),
            pltpu.VMEM((2 * slab, group - early.shape[1]), bf16),
            pltpu.SemaphoreType.DMA,
        ],
        compiler_params=pltpu.CompilerParams(vmem_limit_bytes=BIG),
        cost_estimate=pl.CostEstimate(flops=5_000_000_000, bytes_accessed=14_000_000, transcendentals=500_000),
    )(
        half.reshape(1),
        own,
        other,
        gain,
        early,
        in_hbm(qkv_weight),
        upstream,
        seg_row,
        seg_col,
    )


def roll_half(x):
    return pltpu.roll(x.astype(jnp.float32), 64, 1).astype(x.dtype)


A_ROWS, A_TAIL = 192, 32
B_ROWS, B_TAIL = 208, 48
A_PIECE = A_ROWS + A_TAIL
B_PIECE = B_ROWS + B_TAIL


def pack_kernel(
    place_ref,
    audio_w_ref,
    vision_w_ref,
    audio_ref,
    vision_ref,
    a_ref,
    b_ref,
    rows_ref,
    am_ref,
    at_ref,
    vm_ref,
    vt_ref,
    sems,
    row_sems,
):
    e = place_ref[0]
    t = place_ref[1]
    main_at = pl.multiple_of(e * 384, 128)
    tail_at = pl.multiple_of(1536 + e // 2 * 128, 128)
    loads = [
        pltpu.make_async_copy(vision_w_ref.at[:, :, pl.ds(main_at, 384)], vm_ref, sems.at[0]),
        pltpu.make_async_copy(vision_w_ref.at[:, :, pl.ds(tail_at, 128)], vt_ref, sems.at[1]),
        pltpu.make_async_copy(audio_w_ref.at[:, pl.ds(main_at, 384)], am_ref, sems.at[2]),
        pltpu.make_async_copy(audio_w_ref.at[:, pl.ds(tail_at, 128)], at_ref, sems.at[3]),
    ]
    for copy in loads:
        copy.start()
    width = rows_ref.shape[1]
    ah, vh = audio_ref.shape[0] // 2, vision_ref.shape[0] // 2
    copies = [
        pltpu.make_async_copy(
            audio_ref.at[pl.ds(pl.multiple_of(t * ah, 16), ah), :], rows_ref.at[:ah], row_sems.at[0]
        )
    ] + [
        pltpu.make_async_copy(
            vision_ref.at[pl.ds(pl.multiple_of(t * vh, 16), vh), i * width : (i + 1) * width],
            rows_ref.at[ah + i * vh : ah + (i + 1) * vh],
            row_sems.at[1 + i],
        )
        for i in range(4)
    ]
    for copy in copies:
        copy.start()
    for copy in loads:
        copy.wait()
    k = am_ref.shape[0]
    cut = A_ROWS - k
    vision_main = vm_ref[...].reshape(4 * k, 384)
    a_ref[:k, :] = am_ref[...]
    a_ref[k:A_ROWS, :] = vision_main[:cut]
    b_ref[:B_ROWS, :] = vision_main[cut:]
    odd = e % 2 == 1
    vision_tail = vt_ref[...].reshape(4 * k, 128)
    tail = jnp.concatenate([at_ref[...], vision_tail], axis=0).astype(jnp.float32)
    moved = pltpu.roll(tail, 64, 1)
    first = jnp.where(odd, moved, tail)
    second = jnp.where(odd, tail, moved)
    lane = lax.broadcasted_iota(jnp.int32, (B_TAIL, 128), 1)
    for q in range(3):
        cols = slice(q * 128, (q + 1) * 128)
        low = first[q * A_TAIL : (q + 1) * A_TAIL]
        high = second[96 + q * A_TAIL : 96 + (q + 1) * A_TAIL]
        a_ref[A_ROWS:, cols] = jnp.where(lane[:A_TAIL] < 64, low, high).astype(a_ref.dtype)
    base = A_ROWS
    for q in range(2):
        cols = slice(q * 128, (q + 1) * 128)
        low = first[base + q * B_TAIL : base + (q + 1) * B_TAIL]
        high = second[base + 112 + q * B_TAIL : base + 112 + (q + 1) * B_TAIL]
        b_ref[B_ROWS:, cols] = jnp.where(lane < 64, low, high).astype(b_ref.dtype)
    b_ref[B_ROWS : B_ROWS + 16, 256:] = first[base + 96 : base + 112].astype(b_ref.dtype)
    b_ref[B_ROWS + 16 :, 256:] = jnp.zeros((B_TAIL - 16, 128), b_ref.dtype)
    for copy in copies:
        copy.wait()


def pack(where, audio_weight, vision_weight, audio_rows, vision_rows):
    bf16 = jnp.bfloat16
    vmem = pl.BlockSpec(memory_space=pltpu.VMEM)
    anywhere = pl.BlockSpec(memory_space=pl.ANY)
    k = audio_weight.shape[0]
    return pl.pallas_call(
        pack_kernel,
        out_shape=(
            jax.ShapeDtypeStruct((A_PIECE, 384), bf16),
            jax.ShapeDtypeStruct((B_PIECE, 384), bf16),
            jax.ShapeDtypeStruct(
                (audio_rows.shape[0] // 2 + 2 * vision_rows.shape[0], audio_rows.shape[1]), bf16
            ),
        ),
        in_specs=[pl.BlockSpec(memory_space=pltpu.SMEM)] + [anywhere] * 4,
        out_specs=(vmem, vmem, vmem),
        scratch_shapes=[
            pltpu.VMEM((k, 384), bf16),
            pltpu.VMEM((k, 128), bf16),
            pltpu.VMEM((k, 4, 384), bf16),
            pltpu.VMEM((k, 4, 128), bf16),
            pltpu.SemaphoreType.DMA((4,)),
            pltpu.SemaphoreType.DMA((5,)),
        ],
        compiler_params=pltpu.CompilerParams(vmem_limit_bytes=BIG),
        cost_estimate=pl.CostEstimate(flops=0, bytes_accessed=1_800_000, transcendentals=0),
    )(where, in_hbm(audio_weight), in_hbm(vision_weight), in_hbm(audio_rows), in_hbm(vision_rows))


def encode_kernel(
    a_at_ref,
    b_at_ref,
    ga0,
    ga1,
    ga2,
    ga3,
    ga4,
    gb0,
    gb1,
    gb2,
    gb3,
    gb4,
    own_ref,
    other_ref,
    cell_ref,
    out_ref,
    wa_ref,
    wv_ref,
    ta_ref,
    tv_ref,
    x_ref,
    enc_ref,
    sems,
):
    bf16, f32 = jnp.bfloat16, jnp.float32
    audio_width = x_ref.shape[2]
    audio_k = wa_ref.shape[1]
    cut = A_ROWS - audio_k
    sources = ((ga0, gb0, 0, 4), (ga1, gb1, 4, 4), (ga2, gb2, 8, 4), (ga3, gb3, 12, 2), (ga4, gb4, 14, 2))
    own_copy = pltpu.make_async_copy(own_ref, x_ref, sems.at[0])
    own_copy.start()

    for ga, gb, start, size in sources:

        @pl.loop(0, size)
        def _(n):
            at = a_at_ref[start + n]
            wa_ref[at] = ga[n, :audio_k, :]
            wv_ref[at, :cut, :] = ga[n, audio_k:A_ROWS, :]
            ta = jnp.concatenate([ga[n, A_ROWS:, q * 128 : (q + 1) * 128] for q in range(3)], axis=0)
            ta_ref[at] = ta[:audio_k]
            tv_ref[at, : 96 - audio_k, :] = ta[audio_k:]
            tv_ref[at, 96 - audio_k : cut, :] = roll_half(ta)
            at = b_at_ref[start + n]
            wv_ref[at, cut:, :] = gb[n, :B_ROWS, :]
            tb = jnp.concatenate([gb[n, B_ROWS:, q * 128 : (q + 1) * 128] for q in range(2)], axis=0)
            tv_ref[at, cut : cut + 96, :] = tb
            tv_ref[at, cut + 96 : cut + 112, :] = gb[n, B_ROWS : B_ROWS + 16, 256:]
            tv_ref[at, cut + 112 :, :] = roll_half(tb)

    count = cell_ref.shape[1]
    cells = out_ref.shape[0]
    line = lax.broadcasted_iota(jnp.int32, (cells, count), 0)
    first = jnp.where(line == cell_ref[0:1, :], 1.0, 0.0).astype(bf16)
    second = jnp.where(line == cell_ref[1:2, :], 1.0, 0.0).astype(bf16)

    halves, n_enc = 2, x_ref.shape[0]
    audio = 64
    vision = 32
    n_vision = halves * n_enc * vision

    def weights(main, last):
        size = main.shape[0] * main.shape[1]
        return jnp.concatenate([main.reshape(size, 384), last.reshape(size, 128)], axis=1)

    def keep_rows(value, base, each):
        run = 2 * each
        for h in range(2):
            for g in range(2):
                at = g * count + base + h * run
                enc_ref[at : at + run, :] = value[(2 * h + g) * run : (2 * h + g + 1) * run]

    def rows(at, each):
        parts = [ref[:, at : at + each, :].reshape(n_enc * each, audio_width) for ref in (x_ref, other_ref)]
        return jnp.concatenate(parts, axis=0)

    own_copy.wait()
    keep_rows(dot(rows(0, audio), weights(wa_ref[...], ta_ref[...])).astype(bf16), 0, audio)
    total = jnp.zeros((n_vision, 512), f32)
    for i in range(4):
        part = weights(wv_ref[4 * i : 4 * i + 4], tv_ref[4 * i : 4 * i + 4])
        total = total + dot(rows(audio + i * vision, vision), part)
    keep_rows(total.astype(bf16), 4 * audio, vision)

    out_ref[:, :384] = dot(first, enc_ref[:count, :384]).astype(bf16)
    out_ref[:, 384:768] = dot(second, enc_ref[count:, :384]).astype(bf16)
    low = dot(first, enc_ref[:count, 384:])
    high = dot(second, enc_ref[count:, 384:])
    lane = lax.broadcasted_iota(jnp.int32, low.shape, 1)
    out_ref[:, 768:] = jnp.where(lane < 64, low, pltpu.roll(high, 64, 1)).astype(bf16)


def encode(a_at, b_at, shards_a, shards_b, own, other, cells, n_cells):
    bf16 = jnp.bfloat16
    n_enc, rows, width = own.shape
    smem = pl.BlockSpec(memory_space=pltpu.SMEM)
    vmem = pl.BlockSpec(memory_space=pltpu.VMEM)
    anywhere = pl.BlockSpec(memory_space=pl.ANY)
    k = width // 16
    return pl.pallas_call(
        encode_kernel,
        out_shape=jax.ShapeDtypeStruct((n_cells, 896), bf16),
        in_specs=[smem, smem] + [vmem] * 10 + [anywhere] + [vmem] * 2,
        out_specs=vmem,
        scratch_shapes=[
            pltpu.VMEM((16, k, 384), bf16),
            pltpu.VMEM((16, 4 * k, 384), bf16),
            pltpu.VMEM((16, k, 128), bf16),
            pltpu.VMEM((16, 4 * k, 128), bf16),
            pltpu.VMEM((n_enc, rows, width), bf16),
            pltpu.VMEM((2 * cells.shape[1], 512), bf16),
            pltpu.SemaphoreType.DMA((1,)),
        ],
        compiler_params=pltpu.CompilerParams(vmem_limit_bytes=BIG),
        cost_estimate=pl.CostEstimate(
            flops=3_000_000_000, bytes_accessed=11_000_000, transcendentals=0
        ),
    )(a_at, b_at, *shards_a, *shards_b, in_hbm(own), other, cells)


def place_kernel(e_row_ref, arrived_ref, text_hbm, filled_ref, out_ref, text_ref, sem):
    bf16, f32 = jnp.bfloat16, jnp.float32
    load = pltpu.make_async_copy(text_hbm, text_ref, sem)
    load.start()
    rows = out_ref.shape[0]
    each = arrived_ref.shape[0] // 4
    line = lax.broadcasted_iota(jnp.int32, (rows, each), 0)
    first = jnp.where(line == e_row_ref[0:1, :], 1.0, 0.0).astype(bf16)
    second = jnp.where(line == e_row_ref[1:2, :], 1.0, 0.0).astype(bf16)
    both = jnp.concatenate([first, second], axis=1)
    taken = filled_ref[...] > 0.5
    lane = lax.broadcasted_iota(jnp.int32, (rows, 128), 1)
    low = []
    high = []
    load.wait()
    for e in range(4):
        at = slice(e * each, (e + 1) * each)
        main = jnp.concatenate([arrived_ref[at, :384], arrived_ref[at, 384:768]], axis=0)
        cols = slice(e * 384, (e + 1) * 384)
        text = text_ref[:, cols].astype(f32)
        out_ref[:, cols] = jnp.where(taken, dot(both, main), text).astype(bf16)
        last = arrived_ref[at, 768:]
        low.append(dot(first, last))
        high.append(dot(second, last))
    for q in range(2):
        left = low[2 * q] + pltpu.roll(high[2 * q], 64, 1)
        right = pltpu.roll(low[2 * q + 1], 64, 1) + high[2 * q + 1]
        cols = slice(1536 + q * 128, 1536 + (q + 1) * 128)
        text = text_ref[:, cols].astype(f32)
        out_ref[:, cols] = jnp.where(taken, jnp.where(lane < 64, left, right), text).astype(bf16)


def place(spots, arrived, text, filled):
    vmem = pl.BlockSpec(memory_space=pltpu.VMEM)
    return pl.pallas_call(
        place_kernel,
        out_shape=jax.ShapeDtypeStruct(text.shape, text.dtype),
        in_specs=[vmem, vmem, pl.BlockSpec(memory_space=pl.ANY), vmem],
        out_specs=vmem,
        scratch_shapes=[pltpu.VMEM(text.shape, text.dtype), pltpu.SemaphoreType.DMA],
        compiler_params=pltpu.CompilerParams(vmem_limit_bytes=12 * 1024 * 1024),
        cost_estimate=pl.CostEstimate(flops=300_000_000, bytes_accessed=3_000_000, transcendentals=0),
    )(spots, arrived, text, filled)


def finish_kernel(
    half_ref,
    rows_ref,
    keep_ref,
    taken_ref,
    inv_ref,
    stat_ref,
    gain_ref,
    spot_ref,
    out_ref,
    grad_ref,
):
    bf16, f32 = jnp.bfloat16, jnp.float32
    rows, slab = rows_ref.shape
    cells = out_ref.shape[0]
    half = slab // 2
    inv = inv_ref[...]
    gain = gain_ref[pl.ds(half_ref[0], 1), :]
    line = lax.broadcasted_iota(jnp.int32, (cells, rows), 1)
    first = jnp.where(line == spot_ref[:, 0:1], 1.0, 0.0).astype(bf16)
    second = jnp.where(line == spot_ref[:, 1:2], 1.0, 0.0).astype(bf16)
    both = jnp.concatenate([first, second], axis=1)
    sent = taken_ref[:, slab:].astype(f32)
    stat = stat_ref[...] + sent[:, 0:1] + sent[:, 1:2]
    factor = inv * inv * inv / (2 * slab) * stat
    for c in range(0, slab, 128):
        cols = slice(c, c + 128)
        total = keep_ref[:, cols].astype(f32) + taken_ref[:, cols].astype(f32)
        value = (gain[:, cols] * total - rows_ref[:, cols].astype(f32) * factor).astype(bf16)
        at = c // half
        grad_ref[at * rows : (at + 1) * rows, c - at * half : c - at * half + 128] = value
    out_ref[...] = dot(both, grad_ref[...]).astype(bf16)


def finish(half, rows, keep, taken, inv, stat, gain, spots):
    bf16 = jnp.bfloat16
    vmem = pl.BlockSpec(memory_space=pltpu.VMEM)
    cells = spots.shape[0]
    count, slab = rows.shape
    return pl.pallas_call(
        finish_kernel,
        out_shape=jax.ShapeDtypeStruct((cells, slab // 2), bf16),
        in_specs=[pl.BlockSpec(memory_space=pltpu.SMEM)] + [vmem] * 7,
        out_specs=vmem,
        scratch_shapes=[pltpu.VMEM((2 * count, slab // 2), bf16)],
        compiler_params=pltpu.CompilerParams(vmem_limit_bytes=16 * 1024 * 1024),
        cost_estimate=pl.CostEstimate(flops=500_000_000, bytes_accessed=4_000_000, transcendentals=0),
    )(half.reshape(1), rows, keep, taken, inv, stat, gain, spots)


def collect_kernel(cell_ref, returned_ref, audio_ref, vision_ref):
    bf16 = jnp.bfloat16
    count = cell_ref.shape[0]
    cells, half = returned_ref.shape
    audio = audio_ref.shape[0]
    line = lax.broadcasted_iota(jnp.int32, (count, cells), 1)
    for h in range(2):
        hot = jnp.where(line == cell_ref[...] + 4 * h, 1.0, 0.0).astype(bf16)
        value = dot(hot, returned_ref[...]).astype(bf16)
        cols = slice(h * half, (h + 1) * half)
        audio_ref[:, cols] = value[:audio]
        vision_ref[:, cols] = value[audio:]


def collect(cell, returned, audio):
    vmem = pl.BlockSpec(memory_space=pltpu.VMEM)
    count = cell.shape[0]
    width = 2 * returned.shape[1]
    return pl.pallas_call(
        collect_kernel,
        out_shape=(
            jax.ShapeDtypeStruct((audio, width), jnp.bfloat16),
            jax.ShapeDtypeStruct((count - audio, width), jnp.bfloat16),
        ),
        in_specs=[vmem] * 2,
        out_specs=(vmem,) * 2,
        compiler_params=pltpu.CompilerParams(vmem_limit_bytes=12 * 1024 * 1024),
        cost_estimate=pl.CostEstimate(flops=400_000_000, bytes_accessed=2_000_000, transcendentals=0),
    )(cell, returned)


def swap(x):
    return lax.ppermute(x, "tp", [(0, 1), (1, 0)])


def shift(x, axis, k):
    return lax.ppermute(x, axis, [(i, (i + k) % 4) for i in range(4)])


def ranks(dest):
    count = dest.shape[1]
    same = dest[:, :, None] == dest[:, None, :]
    earlier = jnp.arange(count)[None, :] < jnp.arange(count)[:, None]
    return jnp.sum((same & earlier[None]).astype(jnp.int32), axis=2)


def local(
    audio_rows,
    vision_rows,
    audio_weight,
    vision_weight,
    text_rows,
    row_target,
    segment_ids,
    norm_gain,
    qkv_weight,
    attn_grad,
):
    bf16, f32 = jnp.bfloat16, jnp.float32
    t = lax.axis_index("tp")
    e = lax.axis_index("enc")
    j = lax.axis_index(("z", "y"))
    n_enc = 4
    n_seq = 16
    self_index = e * n_seq + j
    senders, enc_rows = row_target.shape
    length, slab = text_rows.shape
    audio_count, audio_width = audio_rows.shape
    vision_count = vision_rows.shape[0]
    merge = vision_weight.shape[1]
    cap = 4
    wide = slab // 128 // n_enc * 128

    piece_a, piece_b, packed = pack(
        jnp.stack([e, t]),
        audio_weight,
        vision_weight,
        audio_rows,
        vision_rows,
    )
    hops = (1, 3, 2)
    along_y = [piece_a] + [shift(piece_a, "y", k) for k in hops]
    along_z = [piece_b] + [shift(piece_b, "z", k) for k in hops]
    along_y, along_z = lax.optimization_barrier((along_y, along_z))
    stack_a, stack_b, row_target = lax.optimization_barrier(
        (jnp.stack(along_y), jnp.stack(along_z), row_target)
    )
    near_a = [shift(stack_a, "z", 1), shift(stack_a, "z", 3)]
    near_b = [shift(stack_b, "y", 1), shift(stack_b, "y", 3)]
    z, y = lax.axis_index("z"), lax.axis_index("y")
    back = jnp.array((0,) + hops, jnp.int32)
    a_at = (((z - back) % 4)[:, None] * 4 + ((y - back) % 4)[None, :]).reshape(-1)
    b_at = (((y - back) % 4)[:, None] + ((z - back) % 4)[None, :] * 4).reshape(-1)
    ah, vh = audio_count // 2, vision_count // 2

    line = row_target.reshape(n_enc, n_seq, enc_rows)[:, j]
    line_dest = line // length
    line_slot = line_dest * (n_enc * cap) + jnp.arange(n_enc)[:, None] * cap + ranks(line_dest)
    a_slot = line_slot[:, :audio_count].reshape(2, 2, 2, ah)
    v_slot = line_slot[:, audio_count:].reshape(2, 2, 2, vh)
    halves = jnp.stack([t, 1 - t])
    a_slot = jnp.moveaxis(a_slot, 2, 1)[:, halves].reshape(2, -1)
    v_slot = jnp.moveaxis(v_slot, 2, 1)[:, halves].reshape(2, -1)
    row_slot = jnp.concatenate([a_slot, v_slot], axis=1)
    cells = row_slot // 16 * 8 + row_slot % 8

    dest = row_target // length
    mine = (dest == self_index).astype(jnp.int32)
    rank_all = jnp.cumsum(mine, axis=1) - 1
    hot = (rank_all[:, :, None] == jnp.arange(cap)[None, None, :]) & (mine[:, :, None] == 1)
    incoming = jnp.sum(jnp.where(hot, (row_target % length)[:, :, None] + 1, 0), axis=1) - 1
    by_line = incoming.reshape(2, 2, n_seq, cap).transpose(0, 2, 1, 3).reshape(2, -1)
    filled = jnp.max(
        (jnp.arange(length)[:, None] == incoming.reshape(1, -1)).astype(jnp.float32), axis=1, keepdims=True
    )
    half = slab // 2
    nowhere = jnp.full_like(incoming, -1)
    spots = jnp.stack(
        [
            jnp.stack([incoming, nowhere], axis=1).reshape(-1),
            jnp.stack([nowhere, incoming], axis=1).reshape(-1),
        ],
        axis=1,
    )
    own_target = lax.dynamic_index_in_dim(row_target, self_index, 0, keepdims=True)
    own_dest = own_target // length
    own_cell = (own_dest * (2 * cap) + ranks(own_dest)).reshape(-1, 1)
    gain = norm_gain.reshape(2, slab)
    seg_row = segment_ids
    seg_col = segment_ids.reshape(length, 1)
    own = lax.all_gather(packed, "enc", axis=0, tiled=False)
    (
        near_a, near_b, own, cells, by_line, filled, spots, own_cell, gain, seg_col, a_at, b_at
    ) = lax.optimization_barrier(
        (near_a, near_b, own, cells, by_line, filled, spots, own_cell, gain, seg_col, a_at, b_at)
    )
    pass_a = [near_a[0][:2], near_a[1][2:]]
    pass_b = [near_b[0][:2], near_b[1][2:]]
    far_a = [shift(pass_a[0], "z", 1), shift(pass_a[1], "z", 3)]
    far_b = [shift(pass_b[0], "y", 1), shift(pass_b[1], "y", 3)]
    shards_a = [stack_a] + near_a + far_a
    shards_b = [stack_b] + near_b + far_b
    other = swap(own)
    outgoing = encode(a_at, b_at, shards_a, shards_b, own, other, cells, senders * 8)
    arrived = lax.all_to_all(
        outgoing.reshape(senders, 8, slab // 2), SPREAD, split_axis=0, concat_axis=0, tiled=True
    )
    row_slab = place(by_line, arrived.reshape(senders * 8, slab // 2), text_rows, filled)

    row_slab, qkv_weight, attn_grad = lax.optimization_barrier((row_slab, qkv_weight, attn_grad))
    other_slab = swap(row_slab)
    early, upstream = fetch(qkv_weight, attn_grad)
    give, keep, inv_rms, row_part = attend(
        t, row_slab, other_slab, gain, early, qkv_weight, upstream, seg_row, seg_col
    )
    taken = swap(give)

    out8 = finish(t, row_slab, keep, taken, inv_rms, row_part, gain, spots)
    returned = lax.all_to_all(
        out8.reshape(senders, 2 * cap, half), SPREAD, split_axis=0, concat_axis=0, tiled=True
    )
    return collect(own_cell, returned.reshape(senders * 2 * cap, half), audio_count)


SPREAD = ("enc", "z", "y")


def solution(mesh):
    torus = Mesh(mesh.devices.reshape(4, 4, 4, 2), ("enc", "z", "y", "tp"))
    in_specs = (
        P(SPREAD, None),
        P(SPREAD, None),
        P(("z", "y"), "tp"),
        P(("z", "y"), None, "tp"),
        P(SPREAD, "tp"),
        P(),
        P(SPREAD, None),
        P(),
        P(None, "tp"),
        P(SPREAD, "tp"),
    )
    out_specs = (P(SPREAD, "tp"), P(SPREAD, "tp"))
    return jax.shard_map(local, mesh=torus, in_specs=in_specs, out_specs=out_specs, check_vma=False)
```
